32 devices in a mesh: expert: 16 (over z, x, core), tensor: 2 (over y).
Axes of the slice: x: 2, y: 2, z: 4, core: 2. Of those that a mesh axis runs over, the one named last changes fastest.
Arguments:
- tokens_in: bfloat16 [4096, 2048], P('expert'), may hold values from -6 to 6
- cotangent: bfloat16 [4096, 2048], P('expert'), may hold values from -6 to 6
- norm_gains: bfloat16 [2, 2048], P(None, 'expert'), may hold values from 0.5 to 1.5
- qkv_weight: bfloat16 [2048, 3, 2048], P('expert', None, 'tensor'), may hold values from -0.125 to 0.125
- qkv_bias: bfloat16 [3, 16, 128], P(None, 'tensor', 'expert'), may hold values from -4 to 4
- out_weight: bfloat16 [2048, 2048], P('tensor', 'expert'), may hold values from -1.5 to 1.5
- router_weight: bfloat16 [2048, 16], P('expert'), may hold values from -0.0625 to 0.0625
- shared_gate: bfloat16 [2048], P('expert'), may hold values from -0.125 to 0.125
- shared_in: bfloat16 [2048, 2, 5632], P('expert', None, 'tensor'), may hold values from -0.125 to 0.125
- shared_out: bfloat16 [5632, 2048], P('tensor', 'expert'), may hold values from -0.078125 to 0.078125
- expert_in: bfloat16 [16, 2048, 2, 1408], P('expert', None, None, 'tensor'), may hold values from -0.375 to 0.375
- expert_out: bfloat16 [16, 1408, 2048], P('expert', 'tensor'), may hold values from -0.0546875 to 0.0546875
- expert_ids: int32 [4096, 4], P('expert'), may hold values from 0 to 15, all different within a row; in each aligned block of 256 rows (0 to 255, 256 to 511, ...) at most 96 rows name the same one
- prefix_len: int32 [16], P('expert'), may hold values from 25 to 128
Outputs:
- output: bfloat16 [4096, 2048], P('expert')
- input_grad: bfloat16 [4096, 2048], P('expert')
- gains_grad: float32 [2, 2048], P(None, 'expert')
- qkv_weight_grad: float32 [2048, 3, 2048], P('expert', None, 'tensor')
- qkv_bias_grad: float32 [3, 16, 128], P(None, 'tensor', 'expert')
- out_weight_grad: float32 [2048, 2048], P('tensor', 'expert')
- router_grad: float32 [2048, 16], P('expert')
- shared_gate_grad: float32 [2048], P('expert')
- shared_in_grad: float32 [2048, 2, 5632], P('expert', None, 'tensor')
- shared_out_grad: float32 [5632, 2048], P('tensor', 'expert')
- expert_in_grad: float32 [16, 2048, 2, 1408], P('expert', None, None, 'tensor')
- expert_out_grad: float32 [16, 1408, 2048], P('expert', 'tensor')
The draws below stay inside these ranges and needn't reach their ends.
Inputs may be any that keep to these rules, and one draw needn't show every extreme that they name: `expert_ids`: each token names 4 different experts; among the tokens of one sequence no expert is named more than 96 times, a bound that some block reaches.
All inputs are finite; a program needn't handle non-finite values.
Results may differ from the reference program's by a relative error of at most 0.02.
Values may be sent and summed in bfloat16 or wider, within the bound.
No kernel may reach another device: no remote copies, remote signals or barrier semaphores. Data moves between devices by JAX's collectives and lax.ppermute only.
A program may use at most 384 MiB of HBM per device.

```python
import math
import jax
import jax.numpy as jnp
import numpy as np
from jax import lax

D = 2048
HEADS = 16
HD = 128
EFF = 1408
SFF = 5632
TOPK = 4
TOK_DEV = 256
EXPERTS = 16
SEQS = 16
TOKENS = 4096
CAP = 96
N_EXPERT = 16
N_TENSOR = 2


def touch_ends(values, key, low, top_value):
    longest = values.shape.index(max(values.shape))
    spots = []
    for shift in (0, 1):
        where = [jax.random.randint(jax.random.fold_in(key, axis), (), 0, length) for axis, length in enumerate(values.shape)]
        where[longest] = (where[longest] + shift) % values.shape[longest]
        spots.append(tuple(where))
    return values.at[spots[0]].set(low).at[spots[1]].set(top_value)


def block_levels(rng, shape, split, least, top_value):
    loudness, own = 1.0, jax.random.fold_in(rng, 6)
    for position, blocks in split:
        steps = jnp.exp(jax.random.uniform(jax.random.fold_in(own, position), (blocks,), jnp.float32, least / len(split), top_value / len(split)))
        loudness = loudness * jnp.repeat(steps, shape[position] // blocks).reshape([-1 if axis == position else 1 for axis in range(len(shape))])
    return loudness


def assign_block(stream_key, own, number, rows, count, top, reach, lean):
    sequence = jax.random.permutation(stream_key, count)
    crowded, ordinary = shares(count, rows * top, reach, lean, True), shares(count, rows * top, reach, lean, False)
    places = jnp.arange(count)

    def named(tallies, turn):
        used = int((tallies > 0).sum())
        fixed = max(1, used // 4)
        passed = fixed + (places - fixed + turn * (used - fixed)) % max(1, count - fixed)
        return jnp.zeros((count,), jnp.int32).at[sequence[jnp.where(places < fixed, places, passed)]].set(jnp.asarray(tallies, jnp.int32))

    tallies = jnp.where(number % 4 == 0, named(crowded, number // 4), named(ordinary, number - number // 4 - 1))
    mixed = jax.random.permutation(jax.random.fold_in(own, 3), count)
    giver, sink = mixed[0:count // 2 * 2:2], mixed[1:count // 2 * 2:2]
    room = jnp.minimum(tallies[giver] - 1, reach - tallies[sink]) // 2
    room = jnp.where((giver == sequence[0]) | (sink == sequence[0]) | (tallies[sink] == 0), 0, jnp.maximum(room, 0))
    passed = jax.random.randint(jax.random.fold_in(own, 4), (count // 2,), 0, 1 << 20) % (room + 1)
    tallies = tallies.at[giver].add(-passed).at[sink].add(passed)
    labels = jnp.searchsorted(jnp.cumsum(tallies), jnp.arange(rows * top), side="right").astype(jnp.int32)
    listing = labels.reshape(top, rows).T
    listing = listing[jax.random.permutation(jax.random.fold_in(own, 1), rows)]
    turn = jax.random.randint(jax.random.fold_in(own, 2), (rows, 1), 0, top)
    return jnp.take_along_axis(listing, (jnp.arange(top)[None, :] + turn) % top, axis=1)


def shares(count, total, reach, slope, full):
    portions = [(1 << 20) // math.isqrt(standing ** slope) + 1 for standing in range(1, count + 1)]
    largest = reach if full else min(reach, max(-(-total // count), total * portions[0] // sum(portions)))
    least = 1 if total - largest >= count - 1 else 0
    given, spare = [largest] + [least] * (count - 1), total - largest - least * (count - 1)
    while spare > 0:
        movable = [i for i in range(1, count) if given[i] < largest] or [i for i in range(1, count) if given[i] < reach]
        whole, remaining = sum([portions[i] for i in movable]), spare
        for i in movable:
            more = min(reach - given[i], max(1, remaining * portions[i] // whole), spare)
            given[i] = given[i] + more
            spare = spare - more
    return np.array(given)


def centred(own_key, extent, spread, limit, split=(), kind=jnp.bfloat16):
    factor_of = block_levels(own_key, extent, split, -0.22, 0.18) if split else 1.0
    values = jax.random.normal(own_key, extent, jnp.float32) * spread * factor_of
    return jnp.minimum(jnp.maximum(values, -limit), limit).astype(kind)


def setup_inputs(seed: int = 0) -> dict:
    keys = jax.random.split(jax.random.key(seed), 15)
    tokens_in = centred(keys[0], (TOKENS, D), 1.0, 6.0, ((0, 16),))
    cotangent = centred(keys[1], (TOKENS, D), 1.0, 6.0, ((0, 16),))
    norm_gains = jnp.clip(1.0 + 0.1 * jax.random.normal(keys[2], (2, D), jnp.float32), 0.5, 1.5).astype(jnp.bfloat16)
    qkv_weight = centred(keys[3], (D, 3, HEADS * HD), D ** -0.5, 0.125, ((0, 16), (2, 2)))
    qkv_bias = centred(keys[4], (3, HEADS, HD), 0.3, 4.0, ((1, 2), (2, 16)))
    out_weight = centred(keys[5], (HEADS * HD, D), (HEADS * HD // 128) ** -0.5, 1.5, ((0, 2), (1, 16)))
    router_weight = centred(keys[6], (D, EXPERTS), (4 * D) ** -0.5, 0.0625, ((0, 16),))
    shared_gate = centred(keys[7], (D,), D ** -0.5, 0.125, ((0, 16),))
    shared_in = centred(keys[8], (D, 2, SFF), D ** -0.5, 0.125, ((0, 16), (2, 2)))
    shared_out = centred(keys[9], (SFF, D), SFF ** -0.5, 0.078125, ((0, 2), (1, 16)))
    expert_in = centred(keys[10], (EXPERTS, D, 2, EFF), (D // 9) ** -0.5, 0.375, ((0, 16), (3, 2)))
    expert_out = centred(keys[11], (EXPERTS, EFF, D), (9 * EFF) ** -0.5, 0.0546875, ((0, 16), (1, 2)))
    expert_ids_keys = jax.random.split(jax.random.fold_in(keys[12], 1), TOKENS // TOK_DEV)
    expert_ids_turns = jax.random.permutation(jax.random.fold_in(keys[12], 3), TOKENS // TOK_DEV)
    expert_ids = jax.vmap(lambda own, number: assign_block(jax.random.fold_in(keys[12], 2), own, number, TOK_DEV, EXPERTS, TOPK, CAP, 1))(expert_ids_keys, expert_ids_turns).reshape((TOKENS, TOPK))
    prefix_len = touch_ends(jax.random.randint(keys[13], (SEQS,), TOK_DEV // 10, TOK_DEV // 2 + 1), jax.random.fold_in(keys[13], 1), TOK_DEV // 10, (TOK_DEV // 2 + 1) - 1).astype(jnp.int32)
    return dict(tokens_in=tokens_in, cotangent=cotangent, norm_gains=norm_gains, qkv_weight=qkv_weight, qkv_bias=qkv_bias, out_weight=out_weight, router_weight=router_weight, shared_gate=shared_gate, shared_in=shared_in, shared_out=shared_out, expert_in=expert_in, expert_out=expert_out, expert_ids=expert_ids, prefix_len=prefix_len)


@jax.custom_vjp
def low(v):
    return lax.optimization_barrier(v.astype(jnp.bfloat16)).astype(jnp.float32)

@jax.custom_vjp
def low_back(v):
    return v

def low_keep(v):
    return (low(v), None)

def low_pass(kept, grad):
    return (grad,)

def back_keep(v):
    return (v, None)

def back_low(kept, grad):
    return (low(grad),)
low.defvjp(low_keep, low_pass)
low_back.defvjp(back_keep, back_low)
eps = 1e-06
theta_base = 1000000.0
neg_large = -1e+30
highest = lax.Precision.HIGHEST

def rms_norm(values, gain_row):
    factor = lax.rsqrt(lax.optimization_barrier(jnp.mean(values * values, axis=-1, keepdims=True)) + eps)
    return values * factor * gain_row

def rotary(values):
    length, head_count, head_size = values.shape
    half_size = head_size // 2
    frequency = theta_base ** (-(jnp.arange(half_size, dtype=jnp.float32) * 2.0) / head_size)
    angles = jnp.arange(length, dtype=jnp.float32)[:, None] * frequency[None, :]
    cosine = jnp.concatenate([jnp.cos(angles), jnp.cos(angles)], axis=-1)[:, None, :]
    sine_table = jnp.concatenate([jnp.sin(angles), jnp.sin(angles)], axis=-1)[:, None, :]
    turned = jnp.concatenate([-values[..., half_size:], values[..., :half_size]], axis=-1)
    return values * cosine + turned * sine_table

def slot_tables(expert_ids):
    grouped = expert_ids.reshape(N_EXPERT, TOK_DEV * TOPK)
    onehot = (grouped[:, :, None] == jnp.arange(EXPERTS, dtype=jnp.int32)[None, None, :]).astype(jnp.int32)
    slot_rank = lax.optimization_barrier(jnp.sum(jnp.cumsum(onehot, axis=1) * onehot, axis=-1)) - 1
    source = jnp.arange(N_EXPERT, dtype=jnp.int32)[:, None]
    places = (grouped * (N_EXPERT * CAP) + source * CAP + slot_rank).astype(jnp.int32)
    filler = jnp.full((EXPERTS * N_EXPERT * CAP,), TOKENS * TOPK, jnp.int32)
    entry_table = filler.at[places.reshape(-1)].set(jnp.arange(TOKENS * TOPK, dtype=jnp.int32))
    return entry_table.reshape(EXPERTS, N_EXPERT * CAP)

def reference(tokens_in, cotangent, norm_gains, qkv_weight, qkv_bias, out_weight, router_weight, shared_gate, shared_in, shared_out, expert_in, expert_out, expert_ids, prefix_len):
    entry_table = slot_tables(expert_ids)
    score_scale = HD ** (-0.5)
    part_size = EFF // N_TENSOR

    def forward(inputs, gains, qkv_w, qkv_b, out_w, router_w, gate_vec, sh_in, sh_out, ex_in, ex_out):
        first_normed = low(rms_norm(inputs, gains[0]))
        bias_flat = qkv_b.reshape(3, HEADS * HD)

        def attend_one(pieces):
            normed_rows, prefix_cut = pieces
            projected = jnp.einsum('ld,dcf->lcf', normed_rows, qkv_w, precision=highest) + bias_flat[None]
            projected = low_back(projected).reshape(TOK_DEV, 3, HEADS, HD)
            query_heads = low(rotary(projected[:, 0]))
            key_heads = low(rotary(projected[:, 1]))
            value_heads = low(projected[:, 2])
            scores = jnp.einsum('qhd,khd->hqk', query_heads, key_heads, precision=highest) * score_scale
            scores = low_back(scores)
            row_index = jnp.arange(TOK_DEV, dtype=jnp.int32)[:, None]
            col_index = jnp.arange(TOK_DEV, dtype=jnp.int32)[None, :]
            allowed = (col_index <= row_index) | (col_index < prefix_cut)
            scores = jnp.where(allowed[None], scores, neg_large)
            probs = jax.nn.softmax(scores, axis=-1)
            mixed_heads = jnp.einsum('hqk,khd->qhd', low(probs), value_heads, precision=highest)
            return low(low_back(mixed_heads.reshape(TOK_DEV, HEADS * HD)))
        mixed_all = lax.map(jax.checkpoint(attend_one), (first_normed.reshape(SEQS, TOK_DEV, D), prefix_len))
        attn_out = low_back(jnp.dot(mixed_all.reshape(TOKENS, HEADS * HD), out_w, precision=highest))
        residual = inputs + attn_out
        second_normed = low(rms_norm(residual, gains[1]))
        logits = low_back(jnp.dot(second_normed, router_w, precision=highest))
        chosen = jnp.take_along_axis(logits, expert_ids, axis=1)
        gate_weights = jax.nn.softmax(chosen, axis=-1)
        shared_sigma = jax.nn.sigmoid(jnp.dot(second_normed, gate_vec, precision=highest))
        shared_gu = low_back(jnp.einsum('td,dcf->tcf', second_normed, sh_in, precision=highest))
        shared_hidden = low(jax.nn.silu(shared_gu[:, 0]) * shared_gu[:, 1])
        shared_y = low_back(jnp.dot(shared_hidden, sh_out, precision=highest))
        padded_rows = jnp.concatenate([second_normed, jnp.zeros((1, D), jnp.float32)], axis=0)
        padded_gates = jnp.concatenate([gate_weights.reshape(-1), jnp.zeros((1,), jnp.float32)], axis=0)

        def one_expert(pieces):
            entries, weight_in, weight_out = pieces
            token_index = (entries // TOPK).astype(jnp.int32)
            slot_rows = padded_rows[token_index]
            slot_gate = padded_gates[entries]
            expert_sum = jnp.zeros((N_EXPERT * CAP, D), jnp.float32)
            for part_index in range(N_TENSOR):
                lower = part_index * part_size
                part_rows = low_back(slot_rows)
                gate_up = jnp.einsum('rd,dcf->rcf', part_rows, weight_in[:, :, lower:lower + part_size], precision=highest)
                gate_up = low_back(gate_up)
                hidden = low(jax.nn.silu(gate_up[:, 0]) * gate_up[:, 1])
                piece_out = jnp.dot(hidden, weight_out[lower:lower + part_size], precision=highest)
                expert_sum = expert_sum + low(low_back(piece_out))
            return slot_gate[:, None] * expert_sum
        weighted = lax.map(jax.checkpoint(one_expert), (entry_table, ex_in, ex_out))
        target = (entry_table // TOPK).astype(jnp.int32).reshape(-1)
        routed = jnp.zeros((TOKENS + 1, D), jnp.float32).at[target].add(weighted.reshape(-1, D))[:TOKENS]
        return residual + routed + shared_sigma[:, None] * shared_y
    floats = (tokens_in, norm_gains, qkv_weight, qkv_bias, out_weight, router_weight, shared_gate, shared_in, shared_out, expert_in, expert_out)
    floats = tuple((item.astype(jnp.float32) for item in floats))
    primal, pullback = jax.vjp(forward, *floats)
    grads = pullback(cotangent.astype(jnp.float32))
    return (primal.astype(jnp.bfloat16), grads[0].astype(jnp.bfloat16), grads[1], grads[2], grads[3], grads[4], grads[5], grads[6], grads[7], grads[8], grads[9], grads[10])
```

```python
import jax
import jax.numpy as jnp
import numpy as np
from jax import lax
from jax.sharding import PartitionSpec as P

eps = 1e-06
theta_base = 1000000.0
neg_large = -1e30
bf16 = jnp.bfloat16
f32 = jnp.float32


def rms_norm(values, gain_row):
    factor = lax.rsqrt(jnp.mean(values * values, axis=-1, keepdims=True) + eps)
    return values * factor * gain_row


def rotary_tables(length, head_size):
    half_size = head_size // 2
    frequency = np.float32(theta_base) ** (
        -(np.arange(half_size, dtype=np.float32) * np.float32(2.0)) / np.float32(head_size)
    )
    angles = np.arange(length, dtype=np.float32)[:, None] * frequency[None, :].astype(np.float32)
    cosine = np.concatenate([np.cos(angles), np.cos(angles)], axis=-1)[None, :, None, :]
    sine = np.concatenate([np.sin(angles), np.sin(angles)], axis=-1)[None, :, None, :]
    return jnp.asarray(cosine, f32), jnp.asarray(sine, f32)


def rotary(values, cosine, sine):
    half_size = values.shape[-1] // 2
    turned = jnp.concatenate([-values[..., half_size:], values[..., :half_size]], axis=-1)
    return values * cosine + turned * sine


def rotary_back(grads, cosine, sine):
    half_size = grads.shape[-1] // 2
    scaled = grads * sine
    turned = jnp.concatenate([scaled[..., half_size:], -scaled[..., :half_size]], axis=-1)
    return grads * cosine + turned


def silu_product(gate_part, up_part):
    return jax.nn.silu(gate_part) * up_part


def silu_back(gate_part, up_part, grad):
    return jax.vjp(silu_product, gate_part, up_part)[1](grad)


def chip_ring(chips):
    columns = chips // 4
    if chips % 4 or columns < 2 or columns % 2:
        return list(range(chips))
    walk = [(0, 0)]
    for column in range(columns):
        rows = range(1, 4) if column % 2 == 0 else range(3, 0, -1)
        walk += [(row, column) for row in rows]
    walk += [(0, column) for column in range(columns - 1, 0, -1)]
    return [row * columns + column for row, column in walk]


def mm(left, right, contract_left=1, contract_right=0):
    return lax.dot_general(
        left,
        right,
        (((contract_left,), (contract_right,)), ((), ())),
        preferred_element_type=f32,
    )


class Ring:
    def __init__(self, devices):
        self.devices = devices
        self.chips = devices // 2
        order = chip_ring(self.chips)
        n = self.chips
        self.next = [
            (order[i] * 2 + c, order[(i + 1) % n] * 2 + c) for i in range(n) for c in range(2)
        ]
        self.prev = [(b, a) for a, b in self.next]
        self.core = [(e, e ^ 1) for e in range(devices)]
        half = n // 2
        offsets = [0]
        for k in range(1, half):
            offsets += [-k, k]
        self.offsets = offsets + [half]
        place = {chip: i for i, chip in enumerate(order)}
        self.chip_table = np.array(
            [
                [order[(place[e // 2] + o) % n] for o in self.offsets]
                for e in range(devices)
            ],
            np.int32,
        )
        self.seq_table = np.stack(
            [
                2 * self.chip_table + (np.arange(devices) % 2)[:, None],
                2 * self.chip_table + 1 - (np.arange(devices) % 2)[:, None],
            ],
            axis=-1,
        ).reshape(devices, devices)
        self.seq_inverse = np.argsort(self.seq_table, axis=1).astype(np.int32)

    def gather(self, block):
        half = self.chips // 2
        found = {0: block}
        ahead = back = block
        for k in range(1, half):
            ahead = lax.ppermute(ahead, "expert", self.next)
            back = lax.ppermute(back, "expert", self.prev)
            found[-k], found[k] = ahead, back
        cut = block.shape[0] // 2
        first = lax.ppermute(ahead[:cut], "expert", self.next)
        second = lax.ppermute(back[cut:], "expert", self.prev)
        found[half] = jnp.concatenate([first, second], axis=0)
        return found

    def reduce(self, terms):
        half = self.chips // 2

        def total(offset, more=()):
            out = None
            for term in list(terms[offset]) + list(more):
                out = term.astype(f32) if out is None else out + term.astype(f32)
            return out

        far = total(half).astype(bf16)
        cut = far.shape[0] // 2
        ahead = lax.ppermute(far[:cut], "expert", self.next)
        back = lax.ppermute(far[cut:], "expert", self.prev)
        for k in range(half - 1, 0, -1):
            mine, yours = total(k), total(-k)
            if k == half - 1:
                mine = jnp.concatenate([mine[:cut] + ahead.astype(f32), mine[cut:]], axis=0)
                yours = jnp.concatenate([yours[:cut], yours[cut:] + back.astype(f32)], axis=0)
            else:
                mine = mine + ahead.astype(f32)
                yours = yours + back.astype(f32)
            ahead = lax.ppermute(mine.astype(bf16), "expert", self.next)
            back = lax.ppermute(yours.astype(bf16), "expert", self.prev)
        return total(0, (ahead, back))

    def swap_core(self, block):
        return lax.ppermute(block, "expert", self.core)

    def gather_small(self, row, me):
        held = row[None]
        step = 1
        while step < self.devices:
            pairs = [(e, e ^ step) for e in range(self.devices)]
            other = lax.ppermute(held, "expert", pairs)
            upper = (me // step) % 2 == 1
            held = jnp.where(
                upper, jnp.concatenate([other, held]), jnp.concatenate([held, other])
            )
            step *= 2
        return held


def after(value, *others):
    return lax.optimization_barrier((value,) + others)[0]


def swap_tensor(block):
    return lax.ppermute(block, "tensor", [(0, 1), (1, 0)])


def sum_tensor(part):
    own = part.astype(bf16)
    return own.astype(f32) + swap_tensor(own).astype(f32)


def make_local(ring):
    devices, chips = ring.devices, ring.chips

    def local(
        tokens_in,
        cotangent,
        norm_gains,
        qkv_weight,
        qkv_bias,
        out_weight,
        router_weight,
        shared_gate,
        shared_in,
        shared_out,
        expert_in,
        expert_out,
        expert_ids,
        prefix_len,
    ):
        me = lax.axis_index("expert")
        core = me % 2
        length, width = tokens_in.shape
        top_count = expert_ids.shape[1]
        experts = router_weight.shape[1]
        capacity = length * top_count * 3 // (2 * experts)
        rows_dev = qkv_weight.shape[0]
        heads_t = qkv_bias.shape[1]
        heads = heads_t // 2
        hd_dev = qkv_bias.shape[2]
        head_size = hd_dev * devices
        half_cols = heads * head_size
        score_scale = head_size ** (-0.5)
        chip_of = jnp.asarray(ring.chip_table)[me]
        seq_of = jnp.asarray(ring.seq_table)[me]
        seq_inv = jnp.asarray(ring.seq_inverse)[me]

        def own_first(own, other):
            return jnp.where(
                core == 0,
                jnp.concatenate([own, other], axis=0),
                jnp.concatenate([other, own], axis=0),
            )

        pieces = [
            norm_gains.reshape(-1),
            qkv_bias.reshape(-1),
            router_weight.reshape(-1),
            shared_gate.reshape(-1),
            expert_ids.astype(bf16).reshape(-1),
            prefix_len.astype(bf16).reshape(-1),
        ]
        sizes = [p.shape[0] for p in pieces]
        total = sum(sizes)
        padded = -(-total // 1024) * 1024
        small = jnp.concatenate(pieces + [jnp.zeros((padded - total,), bf16)])
        small_all = ring.gather_small(small, me)
        cuts = np.cumsum([0] + sizes)
        found = [small_all[:, cuts[i] : cuts[i + 1]] for i in range(len(sizes))]
        gains_f = (
            found[0].reshape(devices, 2, rows_dev).transpose(1, 0, 2).reshape(2, width).astype(f32)
        )
        bias_all = (
            found[1].reshape(devices, 3, heads_t, hd_dev).transpose(1, 2, 0, 3)
            .reshape(3, 2, half_cols)
        )
        bias = lax.dynamic_index_in_dim(bias_all, core, 1, keepdims=False).astype(f32)
        router_w = found[2].reshape(width, experts)
        gate_vec = found[3].reshape(width)
        ids_all = found[4].reshape(devices, length, top_count).astype(jnp.int32)
        prefix_all = found[5].reshape(devices).astype(jnp.int32)
        prefix_pair = jnp.stack([prefix_all[me], prefix_all[me ^ 1]])

        def halve(weight, parts):
            halves = weight.reshape(rows_dev, parts, 2, half_cols)
            own = lax.dynamic_index_in_dim(halves, core, 2, keepdims=False)
            other = lax.dynamic_index_in_dim(halves, 1 - core, 2, keepdims=False)
            got = ring.swap_core(other.reshape(rows_dev, -1))
            return own_first(own.reshape(rows_dev, -1), got)

        def assemble(blocks):
            depth = 2 * rows_dev
            whole = jnp.zeros((width, blocks[0].shape[1]), bf16)
            for i, offset in enumerate(ring.offsets):
                whole = lax.dynamic_update_slice(whole, blocks[offset], (chip_of[i] * depth, 0))
            return whole

        qkv_blocks = ring.gather(halve(qkv_weight, 3))
        qkv_w = assemble(qkv_blocks)
        out_block = after(halve(out_weight.T, 1), qkv_blocks[chips // 2 - 1])
        out_w = assemble(ring.gather(out_block))

        units = shared_out.shape[0]
        unit_chip = units // chips
        sh_rows = jnp.concatenate(
            [
                shared_in.reshape(rows_dev, 2, chips, unit_chip),
                shared_out.T.reshape(rows_dev, 1, chips, unit_chip),
            ],
            axis=1,
        )
        sh_send = sh_rows.transpose(2, 0, 1, 3).reshape(chips, rows_dev, 3 * unit_chip)
        sh_send = after(sh_send, qkv_blocks[chips // 2])
        same_core = [[2 * i + c for i in range(chips)] for c in range(2)]
        sh_mine = lax.all_to_all(
            sh_send, "expert", split_axis=0, concat_axis=0, tiled=True, axis_index_groups=same_core
        )
        sh_other = ring.swap_core(sh_mine)
        sh_w = jnp.where(
            core == 0,
            jnp.stack([sh_mine, sh_other], axis=1),
            jnp.stack([sh_other, sh_mine], axis=1),
        ).reshape(width, 3 * unit_chip)
        sh_in = sh_w[:, : 2 * unit_chip]
        sh_out_t = sh_w[:, 2 * unit_chip :]

        up_own = ring.gather(after(cotangent, qkv_blocks[chips // 2]))
        up_other = {o: ring.swap_core(b) for o, b in up_own.items()}

        inputs = tokens_in.astype(f32)
        first_b = rms_norm(inputs, gains_f[0]).astype(bf16)
        first_pair = jnp.concatenate([first_b, ring.swap_core(first_b)], axis=0)
        cosine, sine = rotary_tables(length, head_size)
        projected = mm(first_pair, qkv_w) + bias.reshape(-1)[None]
        projected = projected.reshape(2, length, 3, heads, head_size)
        query_heads = rotary(projected[:, :, 0], cosine, sine).astype(bf16)
        key_heads = rotary(projected[:, :, 1], cosine, sine).astype(bf16)
        value_heads = projected[:, :, 2].astype(bf16)
        scores = (
            jnp.einsum("bqhd,bkhd->bhqk", query_heads, key_heads, preferred_element_type=f32)
            * score_scale
        )
        row_index = jnp.arange(length, dtype=jnp.int32)[None, :, None]
        col_index = jnp.arange(length, dtype=jnp.int32)[None, None, :]
        allowed = (col_index <= row_index) | (col_index < prefix_pair[:, None, None])
        scores = jnp.where(allowed[:, None], scores, neg_large)
        row_max = jnp.max(scores, axis=-1, keepdims=True)
        weights = jnp.exp(scores - row_max)
        probs = weights / jnp.sum(weights, axis=-1, keepdims=True)
        probs_low = probs.astype(bf16)
        mixed = jnp.einsum("bhqk,bkhd->bqhd", probs_low, value_heads, preferred_element_type=f32)
        mixed = mixed.reshape(2 * length, half_cols).astype(bf16)
        attn_part = mm(mixed, out_w, 1, 1)
        attn_got = ring.swap_core(attn_part[length:].astype(bf16))
        attn_out = sum_tensor(attn_part[:length] + attn_got.astype(f32))
        residual = inputs + attn_out
        second_b = rms_norm(residual, gains_f[1]).astype(bf16)

        rows_own = ring.gather(second_b)
        rows_other = {o: ring.swap_core(b) for o, b in rows_own.items()}

        logits = mm(second_b, router_w)
        expert_range = jnp.arange(experts, dtype=jnp.int32)
        route_match = expert_ids[:, :, None] == expert_range[None, None, :]
        chosen = jnp.sum(jnp.where(route_match, logits[:, None, :], 0.0), axis=-1)
        gate_weights = jax.nn.softmax(chosen, axis=-1)
        shared_sigma = jax.nn.sigmoid(
            jnp.sum(second_b.astype(f32) * gate_vec.astype(f32)[None], axis=-1)
        )
        gate_dense = jnp.sum(jnp.where(route_match, gate_weights[:, :, None], 0.0), axis=1)
        gate_send = jnp.stack(
            [gate_dense.T, jnp.broadcast_to(shared_sigma[None], (experts, length))], axis=1
        )
        gate_all = lax.all_to_all(gate_send, "expert", split_axis=0, concat_axis=0, tiled=True)
        gate_all = gate_all[seq_of]
        gate_tok, sigma_tok = gate_all[:, 0], gate_all[:, 1]

        match = jnp.any(ids_all[seq_of] == me, axis=-1)
        triangle = jnp.asarray(np.triu(np.ones((length, length), np.float32)), bf16)
        rank = mm(match.astype(bf16), triangle) - 1.0
        slots = jnp.arange(capacity, dtype=f32)[None, :, None]
        pick = (slots == rank[:, None, :]) & match[:, None, :]
        pick_b = pick.astype(bf16)
        gate_slot = jnp.sum(jnp.where(pick, gate_tok[:, None, :], 0.0), axis=-1)

        ex_in = expert_in[0].reshape(width, -1)
        ex_out = expert_out[0]
        part_units = ex_out.shape[0]
        near = [i for i, o in enumerate(ring.offsets) if 4 * abs(o) <= chips]
        far = [i for i, o in enumerate(ring.offsets) if 4 * abs(o) > chips]

        def forward(group):
            held = {}
            offs = [ring.offsets[i] for i in group]
            held["rows"] = jnp.concatenate(
                [
                    mm(pick_b[2 * i + c], (rows_own, rows_other)[c][ring.offsets[i]]).astype(bf16)
                    for i in group
                    for c in range(2)
                ],
                axis=0,
            )
            gate_up = mm(held["rows"], ex_in)
            held["gate"], held["up"] = gate_up[:, :part_units], gate_up[:, part_units:]
            held["hidden"] = silu_product(held["gate"], held["up"]).astype(bf16)
            held["produced"] = mm(held["hidden"], ex_out).astype(bf16)
            lo, hi = 2 * group[0], 2 * group[-1] + 2
            held["gates"] = gate_slot[lo:hi].reshape(-1, 1)
            weighted = (held["gates"] * held["produced"].astype(f32)).astype(bf16)
            held["tokens"] = jnp.concatenate([rows_own[o] for o in offs], axis=0)
            shared_gu = mm(held["tokens"], sh_in)
            held["sgate"], held["sup"] = shared_gu[:, :unit_chip], shared_gu[:, unit_chip:]
            held["shidden"] = silu_product(held["sgate"], held["sup"]).astype(bf16)
            held["shared"] = mm(held["shidden"], sh_out_t, 1, 1)
            held["sigma"] = sigma_tok.reshape(-1, 2, length)[group[0] : group[-1] + 1, 0].reshape(-1, 1)
            gated = held["sigma"] * held["shared"]
            own, other = {}, {}
            for j, i in enumerate(group):
                block = weighted[2 * j * capacity : (2 * j + 1) * capacity]
                routed = mm(pick_b[2 * i], block, 0, 0)
                own[offs[j]] = (routed + gated[j * length : (j + 1) * length]).astype(bf16)
                block = weighted[(2 * j + 1) * capacity : (2 * j + 2) * capacity]
                other[offs[j]] = mm(pick_b[2 * i + 1], block, 0, 0).astype(bf16)
            return held, own, other

        def backward(group, held):
            offs = [ring.offsets[i] for i in group]
            lo, hi = 2 * group[0], 2 * group[-1] + 2
            up_rows = jnp.concatenate(
                [
                    mm(pick_b[2 * i + c], (up_own, up_other)[c][ring.offsets[i]])
                    for i in group
                    for c in range(2)
                ],
                axis=0,
            )
            dots = jnp.sum(up_rows * held["produced"].astype(f32), axis=-1)
            dots = jnp.sum(
                jnp.where(pick[lo:hi], dots.reshape(-1, capacity)[:, :, None], 0.0), axis=1
            )
            slot_grad = (held["gates"] * up_rows).astype(bf16)
            hidden_grad = mm(slot_grad, ex_out, 1, 1)
            gate_grad, up_grad = silu_back(held["gate"], held["up"], hidden_grad)
            gu_grad = jnp.concatenate([gate_grad.astype(bf16), up_grad.astype(bf16)], axis=1)
            entry_grad = mm(gu_grad, ex_in, 1, 1).astype(bf16)
            upstream = jnp.concatenate([up_own[o] for o in offs], axis=0).astype(f32)
            sigma_dots = jnp.sum(upstream * held["shared"], axis=-1).reshape(-1, length)
            y_grad = (held["sigma"] * upstream).astype(bf16)
            shared_hidden_grad = mm(y_grad, sh_out_t)
            gate_grad, up_grad = silu_back(held["sgate"], held["sup"], shared_hidden_grad)
            shared_gu_grad = jnp.concatenate([gate_grad.astype(bf16), up_grad.astype(bf16)], axis=1)
            shared_back = mm(shared_gu_grad, sh_in, 1, 1)
            own, other = {}, {}
            for j, i in enumerate(group):
                block = entry_grad[2 * j * capacity : (2 * j + 1) * capacity]
                routed = mm(pick_b[2 * i], block, 0, 0)
                own[offs[j]] = (routed + shared_back[j * length : (j + 1) * length]).astype(bf16)
                block = entry_grad[(2 * j + 1) * capacity : (2 * j + 2) * capacity]
                other[offs[j]] = mm(pick_b[2 * i + 1], block, 0, 0).astype(bf16)
            later = (slot_grad, gu_grad, y_grad, shared_gu_grad)
            return own, other, dots, sigma_dots, later

        held_near, moe_near, moe_near_o = forward(near)
        held_far, moe_far, moe_far_o = forward(far)
        moe_own, moe_other = {**moe_near, **moe_far}, {**moe_near_o, **moe_far_o}

        back_far, back_far_o, dots_far, sdots_far, later_far = backward(far, held_far)
        back_near, back_near_o, dots_near, sdots_near, later_near = backward(near, held_near)
        back_own, back_other = {**back_near, **back_far}, {**back_near_o, **back_far_o}
        back_terms = {o: [b, ring.swap_core(back_other[o])] for o, b in back_own.items()}
        second_part = ring.reduce(back_terms)

        moe_terms = {o: [b, ring.swap_core(moe_other[o])] for o, b in moe_own.items()}
        moe_part = ring.reduce(moe_terms)
        output = (residual + sum_tensor(moe_part)).astype(bf16)

        dots = jnp.concatenate([dots_near, dots_far], axis=0)
        sdots = jnp.concatenate([sdots_near, sdots_far], axis=0)
        sdots = jnp.stack([sdots, jnp.zeros_like(sdots)], axis=1).reshape(devices, length)
        dot_send = jnp.stack([dots, sdots], axis=1)[seq_inv]
        dot_got = lax.all_to_all(dot_send, "expert", split_axis=0, concat_axis=0, tiled=True)
        dot_got = jnp.concatenate([dot_got[:, 0], jnp.sum(dot_got[:, 1], axis=0)[None]], axis=0)
        dot_got = dot_got + swap_tensor(dot_got)
        gate_grad_dense, sigma_grad = dot_got[:experts].T, dot_got[experts]
        row_term = jnp.sum(gate_dense * gate_grad_dense, axis=-1, keepdims=True)
        logit_grad = (gate_dense * (gate_grad_dense - row_term)).astype(bf16)
        gate_logit_grad = sigma_grad * shared_sigma * (1.0 - shared_sigma)

        second_grad = sum_tensor(second_part)
        second_grad = second_grad + mm(logit_grad, router_w, 1, 1)
        second_grad = second_grad + gate_logit_grad[:, None] * gate_vec.astype(f32)[None]
        upstream = cotangent.astype(f32)
        residual_norm_grad, gain_two_grad = jax.vjp(rms_norm, residual, gains_f[1])[1](second_grad)
        residual_grad = upstream + residual_norm_grad
        attn_grad = residual_grad.astype(bf16)
        attn_grad_pair = jnp.concatenate([attn_grad, ring.swap_core(attn_grad)], axis=0)

        depth = 2 * rows_dev

        def by_chip(left, right):
            return {
                offset: [
                    mm(lax.dynamic_slice_in_dim(left, chip_of[i] * depth, depth, 1), right, 0, 0)
                ]
                for i, offset in enumerate(ring.offsets)
            }

        out_grad = ring.reduce(by_chip(attn_grad_pair, mixed))
        mixed_grad = mm(attn_grad_pair, out_w).astype(bf16).reshape(2, length, heads, head_size)
        prob_grad = jnp.einsum(
            "bqhd,bkhd->bhqk", mixed_grad, value_heads, preferred_element_type=f32
        )
        row_term = jnp.sum(probs * prob_grad, axis=-1, keepdims=True)
        score_grad = (probs * (prob_grad - row_term)).astype(bf16)
        query_grad = (
            jnp.einsum("bhqk,bkhd->bqhd", score_grad, key_heads, preferred_element_type=f32)
            * score_scale
        )
        key_grad = (
            jnp.einsum("bhqk,bqhd->bkhd", score_grad, query_heads, preferred_element_type=f32)
            * score_scale
        )
        value_grad = jnp.einsum(
            "bhqk,bqhd->bkhd", probs_low, mixed_grad, preferred_element_type=f32
        )
        proj_grad = jnp.stack(
            [
                rotary_back(query_grad, cosine, sine).astype(bf16),
                rotary_back(key_grad, cosine, sine).astype(bf16),
                value_grad.astype(bf16),
            ],
            axis=2,
        ).reshape(2 * length, 3 * half_cols)
        qkv_grad = ring.reduce(by_chip(first_pair, proj_grad))
        bias_grad = jnp.sum(proj_grad.astype(f32), axis=0)
        first_part = mm(proj_grad, qkv_w, 1, 1)
        first_got = ring.swap_core(first_part[length:].astype(bf16))
        first_grad = sum_tensor(first_part[:length] + first_got.astype(f32))
        input_norm_grad, gain_one_grad = jax.vjp(rms_norm, inputs, gains_f[0])[1](first_grad)
        input_grad = (residual_grad + input_norm_grad).astype(bf16)

        def regroup(grad, parts):
            grad = grad.reshape(2, rows_dev, parts * half_cols)
            own = lax.dynamic_index_in_dim(grad, core, 0, keepdims=False)
            other = lax.dynamic_index_in_dim(grad, 1 - core, 0, keepdims=False)
            own = own.astype(bf16).reshape(rows_dev, parts, half_cols)
            got = ring.swap_core(other.astype(bf16)).reshape(rows_dev, parts, half_cols)
            both = jnp.where(
                core == 0, jnp.stack([own, got], axis=2), jnp.stack([got, own], axis=2)
            )
            return both.reshape(rows_dev, parts, 2 * half_cols).astype(f32)

        qkv_weight_grad = regroup(qkv_grad, 3)
        out_weight_grad = regroup(out_grad, 1)[:, 0].T

        def two(left, right):
            return mm(left[0], right[0], 0, 0) + mm(left[1], right[1], 0, 0)

        slot_grads, gu_grads, y_grads, sgu_grads = zip(later_near, later_far, strict=True)
        expert_out_grad = two((held_near["hidden"], held_far["hidden"]), slot_grads)[None]
        expert_in_grad = two((held_near["rows"], held_far["rows"]), gu_grads).reshape(
            1, width, 2, part_units
        )
        tokens = (held_near["tokens"], held_far["tokens"])
        sh_grad = jnp.concatenate(
            [
                two(tokens, sgu_grads).astype(bf16),
                two(y_grads, (held_near["shidden"], held_far["shidden"])).astype(bf16),
            ],
            axis=1,
        ).reshape(chips, 2, rows_dev, 3 * unit_chip)
        sh_own = lax.dynamic_index_in_dim(sh_grad, core, 1, keepdims=False)
        sh_give = lax.dynamic_index_in_dim(sh_grad, 1 - core, 1, keepdims=False)
        sh_sum = (sh_own.astype(f32) + ring.swap_core(sh_give).astype(f32)).astype(bf16)
        sh_back = lax.all_to_all(
            sh_sum, "expert", split_axis=0, concat_axis=0, tiled=True, axis_index_groups=same_core
        )
        sh_back = sh_back.reshape(chips, rows_dev, 3, unit_chip).transpose(1, 2, 0, 3)
        sh_back = sh_back.reshape(rows_dev, 3, units).astype(f32)
        shared_in_grad = sh_back[:, :2]
        shared_out_grad = sh_back[:, 2].T

        second_f = second_b.astype(f32)
        router_part = mm(second_b, logit_grad, 0, 0)
        shared_gate_part = jnp.sum(gate_logit_grad[:, None] * second_f, axis=0)
        early = jnp.concatenate(
            [router_part, shared_gate_part[:, None], gain_two_grad[:, None]], axis=1
        ).reshape(devices, rows_dev * (experts + 2))
        early = lax.all_to_all(early, "expert", split_axis=0, concat_axis=0, tiled=True)
        early = jnp.sum(early, axis=0).reshape(rows_dev, experts + 2)
        router_grad, shared_gate_grad = early[:, :experts], early[:, experts]
        bias_send = bias_grad.reshape(3 * heads, devices, hd_dev).transpose(1, 0, 2)
        late = jnp.concatenate(
            [gain_one_grad.reshape(devices, rows_dev), bias_send.reshape(devices, -1)], axis=1
        )
        late = lax.all_to_all(late, "expert", split_axis=0, concat_axis=0, tiled=True)
        gain_one = jnp.sum(late[:, :rows_dev], axis=0)
        bias_got = jnp.sum(late[:, rows_dev:].reshape(chips, 2, 3, heads, hd_dev), axis=0)
        qkv_bias_grad = bias_got.transpose(1, 0, 2, 3).reshape(3, heads_t, hd_dev)
        gains_grad = jnp.stack([gain_one, early[:, experts + 1]], axis=0)

        return (
            output,
            input_grad,
            gains_grad,
            qkv_weight_grad,
            qkv_bias_grad,
            out_weight_grad,
            router_grad,
            shared_gate_grad,
            shared_in_grad,
            shared_out_grad,
            expert_in_grad,
            expert_out_grad,
        )

    return local


def solution(mesh):
    ring = Ring(mesh.shape["expert"])
    return jax.shard_map(
        make_local(ring),
        mesh=mesh,
        in_specs=(
            P("expert", None),
            P("expert", None),
            P(None, "expert"),
            P("expert", None, "tensor"),
            P(None, "tensor", "expert"),
            P("tensor", "expert"),
            P("expert", None),
            P("expert"),
            P("expert", None, "tensor"),
            P("tensor", "expert"),
            P("expert", None, None, "tensor"),
            P("expert", "tensor", None),
            P("expert", None),
            P("expert"),
        ),
        out_specs=(
            P("expert", None),
            P("expert", None),
            P(None, "expert"),
            P("expert", None, "tensor"),
            P(None, "tensor", "expert"),
            P("tensor", "expert"),
            P("expert", None),
            P("expert"),
            P("expert", None, "tensor"),
            P("tensor", "expert"),
            P("expert", None, None, "tensor"),
            P("expert", "tensor", None),
        ),
        check_vma=False,
    )
```

```python
import functools

import jax
import jax.numpy as jnp
import numpy as np
from jax import lax
from jax.experimental import pallas as pl
from jax.experimental.pallas import tpu as pltpu
from jax.sharding import PartitionSpec as P

eps = 1e-06
theta_base = 1000000.0
neg_large = -1e30
no_slot = -100000.0
bf16 = jnp.bfloat16
f32 = jnp.float32
in_vmem = pl.BlockSpec(memory_space=pltpu.VMEM)
in_smem = pl.BlockSpec(memory_space=pltpu.SMEM)
in_any = pl.BlockSpec(memory_space=pl.ANY)


def rms_norm(values, gain_row):
    factor = lax.rsqrt(jnp.mean(values * values, axis=-1, keepdims=True) + eps)
    return values * factor * gain_row


def rotary_tables(length, head_size):
    half_size = head_size // 2
    frequency = np.float32(theta_base) ** (
        -(np.arange(half_size, dtype=np.float32) * np.float32(2.0)) / np.float32(head_size)
    )
    angles = np.arange(length, dtype=np.float32)[:, None] * frequency[None, :].astype(np.float32)
    cosine = np.concatenate([np.cos(angles), np.cos(angles)], axis=-1)
    sine = np.concatenate([-np.sin(angles), np.sin(angles)], axis=-1)
    return jnp.asarray(cosine, f32), jnp.asarray(sine, f32)


def chip_ring(chips):
    columns = chips // 4
    if chips % 4 or columns < 2 or columns % 2:
        return list(range(chips))
    walk = [(0, 0)]
    for column in range(columns):
        rows = range(1, 4) if column % 2 == 0 else range(3, 0, -1)
        walk += [(row, column) for row in rows]
    walk += [(0, column) for column in range(columns - 1, 0, -1)]
    return [row * columns + column for row, column in walk]


def mm(left, right, contract_left=1, contract_right=0):
    return lax.dot_general(
        left,
        right,
        (((contract_left,), (contract_right,)), ((), ())),
        preferred_element_type=f32,
    )


def nt(left, right):
    return mm(left, right, 1, 1)


def tiles(total, size):
    return [(lo, min(size, total - lo)) for lo in range(0, total, size)]


def params():
    return pltpu.CompilerParams(vmem_limit_bytes=56 * 1024 * 1024)


def half_turn(values):
    return pltpu.roll(values, values.shape[1] // 2, 1)


def masked(scores, prefix_cut):
    length = scores.shape[0]
    row = lax.broadcasted_iota(jnp.int32, (length, length), 0)
    col = lax.broadcasted_iota(jnp.int32, (length, length), 1)
    return jnp.where((col <= row) | (col < prefix_cut), scores, neg_large)


def softmax_rows(scores):
    weights = jnp.exp(scores - jnp.max(scores, axis=-1, keepdims=True))
    return weights / jnp.sum(weights, axis=-1, keepdims=True)


def load_blocks(chip_ref, blocks, scratch, sem, parts):
    depth = blocks[0].shape[0] // parts
    copies = []
    for i, block in enumerate(blocks):
        start = pl.multiple_of(chip_ref[i] * depth, depth)
        for c in range(parts):
            copies.append(
                pltpu.make_async_copy(
                    block.at[pl.ds(c * depth, depth)],
                    scratch.at[c, pl.ds(start, depth)],
                    sem.at[i * parts + c],
                )
            )
    for copy in copies:
        copy.start()
    return copies


def attend_kernel(count, heads, scale, *refs):
    chip_ref, prefix_ref, own, other, bias, cosine, sine = refs[:7]
    blocks = refs[7 : 7 + count]
    query, key, value, mixed, weight, sem = refs[7 + count :]
    copies = load_blocks(chip_ref, blocks, weight, sem, 3)
    length, head_size = cosine.shape
    columns = heads * head_size
    for copy in copies:
        copy.wait()
    for c, out in enumerate((query, key, value)):
        for b, rows in enumerate((own, other)):
            for lo, size in tiles(columns, 2 * head_size):
                part = mm(rows[...], weight[c, :, lo : lo + size])
                part = part + bias[:, c * columns + lo : c * columns + lo + size]
                for at in range(0, size, head_size):
                    one = part[:, at : at + head_size]
                    if c < 2:
                        one = one * cosine[...] + half_turn(one) * sine[...]
                    out[b * length : (b + 1) * length, lo + at : lo + at + head_size] = one.astype(
                        bf16
                    )
    for b in range(2):
        rows = slice(b * length, (b + 1) * length)
        for h in range(heads):
            cols = slice(h * head_size, (h + 1) * head_size)
            scores = masked(nt(query[rows, cols], key[rows, cols]) * scale, prefix_ref[b])
            probs = softmax_rows(scores).astype(bf16)
            mixed[rows, cols] = mm(probs, value[rows, cols]).astype(bf16)


def project_kernel(count, *refs):
    chip_ref, mixed = refs[:2]
    blocks = refs[2 : 2 + count]
    own, other, weight, sem = refs[2 + count :]
    copies = load_blocks(chip_ref, blocks, weight, sem, 1)
    for copy in copies:
        copy.wait()
    length, width = own.shape
    for lo, size in tiles(width, 512):
        part = nt(mixed[...], weight[0, lo : lo + size, :])
        own[:, lo : lo + size] = part[:length].astype(own.dtype)
        other[:, lo : lo + size] = part[length:].astype(other.dtype)


def attend_back_kernel(count, heads, scale, *refs):
    chip_ref, prefix_ref, own, other, query, key, value, cosine, sine = refs[:9]
    blocks = refs[9 : 9 + count]
    grad, bias, weight, sem = refs[9 + count :]
    copies = load_blocks(chip_ref, blocks, weight, sem, 1)
    length, head_size = cosine.shape
    columns = heads * head_size
    for copy in copies:
        copy.wait()
    for b, up in enumerate((own, other)):
        rows = slice(b * length, (b + 1) * length)
        mixed_grad = mm(up[...], weight[0]).astype(bf16)
        for h in range(heads):
            cols = slice(h * head_size, (h + 1) * head_size)
            q, k, v = query[rows, cols], key[rows, cols], value[rows, cols]
            up_head = mixed_grad[:, cols]
            probs = softmax_rows(masked(nt(q, k) * scale, prefix_ref[b]))
            prob_grad = nt(up_head, v)
            row_term = jnp.sum(probs * prob_grad, axis=-1, keepdims=True)
            score_grad = (probs * (prob_grad - row_term)).astype(bf16)
            q_grad = mm(score_grad, k) * scale
            k_grad = mm(score_grad, q, 0, 0) * scale
            v_grad = mm(probs.astype(bf16), up_head, 0, 0)
            for c, one in enumerate((q_grad, k_grad, v_grad)):
                if c < 2:
                    one = one * cosine[...] - half_turn(one) * sine[...]
                one = one.astype(bf16)
                at = slice(c * columns + h * head_size, c * columns + (h + 1) * head_size)
                grad[rows, at] = one
                column_sum = jnp.sum(one.astype(f32), axis=0, keepdims=True)
                bias[:, at] = column_sum if b == 0 else bias[:, at] + column_sum


def project_back_kernel(count, *refs):
    chip_ref, grad = refs[:2]
    blocks = refs[2 : 2 + count]
    own, other, weight, sem = refs[2 + count :]
    copies = load_blocks(chip_ref, blocks, weight, sem, 3)
    for copy in copies:
        copy.wait()
    length, width = own.shape
    columns = grad.shape[1] // 3
    for lo, size in tiles(width, 512):
        part = nt(grad[:, :columns], weight[0, lo : lo + size, :])
        for c in range(1, 3):
            part = part + nt(grad[:, c * columns : (c + 1) * columns], weight[c, lo : lo + size, :])
        own[:, lo : lo + size] = part[:length].astype(own.dtype)
        other[:, lo : lo + size] = part[length:].astype(other.dtype)


def moe_kernel(index, first, plan, sizes, *refs):
    length, width, capacity, units, shared_units = sizes
    count = sum(len(p) for p in plan)
    half_ref, row_ref, col_ref = refs[:3]
    given = refs[3 : 3 + count]
    in_hbm, out_hbm, shared_hbm = refs[3 + count : 6 + count]
    rest = refs[6 + count + (0 if first else 8) :]
    kept = rest[:8]
    moe_own, moe_other, back_own, back_other, dots = rest[8:13]
    (tok, up, w_in, w_out, w_sh, rows, up_rows, slots, hidden, gu, y_grad, s_hidden, s_gu) = rest[
        13:26
    ]
    load_sem, weight_sem, keep_sem = rest[26:]

    loads = []
    for which, pieces in enumerate(plan):
        target = (tok, tok, up, up)[which]
        for start_zero, start_one, size in pieces:
            start = start_zero + half_ref[0] * (start_one - start_zero)
            start = pl.multiple_of(start + (which % 2) * length, 16)
            loads.append(
                pltpu.make_async_copy(
                    given[len(loads)], target.at[pl.ds(start, size)], load_sem.at[len(loads)]
                )
            )
    weights = [
        pltpu.make_async_copy(a, b, weight_sem.at[i])
        for i, (a, b) in enumerate(((in_hbm, w_in), (out_hbm, w_out), (shared_hbm, w_sh)))
    ]
    for copy in loads + weights:
        copy.start()

    def keep(slot, source):
        target = kept[slot]
        target = target.at[:, index] if len(target.shape) == 4 else target.at[index]
        copy = pltpu.make_async_copy(source, target, keep_sem.at[slot])
        copy.start()
        return copy

    rank_own, rank_other = row_ref[index, 0:1, :], row_ref[index, 1:2, :]
    slot = lax.broadcasted_iota(jnp.int32, (capacity, length), 0).astype(f32)
    pick_own, pick_other = slot == rank_own, slot == rank_other
    one_own = jnp.where(pick_own, 1.0, 0.0).astype(bf16)
    one_other = jnp.where(pick_other, 1.0, 0.0).astype(bf16)
    gate_own = jnp.sum(jnp.where(pick_own, row_ref[index, 2:3, :], 0.0), axis=1, keepdims=True)
    gate_other = jnp.sum(jnp.where(pick_other, row_ref[index, 3:4, :], 0.0), axis=1, keepdims=True)
    gates = jnp.concatenate([gate_own, gate_other], axis=0)
    lane = lax.broadcasted_iota(jnp.int32, (length, 2 * capacity), 1).astype(f32)
    place = jnp.concatenate(
        [
            jnp.where(lane == col_ref[index, :, 0:1], 1.0, 0.0).astype(bf16),
            jnp.where(lane == col_ref[index, :, 1:2] + float(capacity), 1.0, 0.0).astype(bf16),
        ],
        axis=0,
    )
    sigma = col_ref[index, :, 2:3]
    for copy in loads:
        copy.wait()
    kept_copies = [keep(4, tok.at[0:length])]

    wide = min(512, width)

    @pl.loop(0, width // wide)
    def _(n):
        cols = pl.ds(pl.multiple_of(n * wide, wide), wide)
        rows[0:capacity, cols] = mm(one_own, tok[0:length, cols]).astype(bf16)
        rows[capacity:, cols] = mm(one_other, tok[length:, cols]).astype(bf16)
        got = mm(one_own, up[0:length, cols])
        up_rows[0:capacity, cols] = got.astype(bf16)
        slots[0:capacity, cols] = (gate_own * got).astype(bf16)
        got = mm(one_other, up[length:, cols])
        up_rows[capacity:, cols] = got.astype(bf16)
        slots[capacity:, cols] = (gate_other * got).astype(bf16)
        y_grad[:, cols] = (sigma * up[0:length, cols].astype(f32)).astype(bf16)

    kept_copies += [keep(0, rows), keep(1, slots), keep(5, y_grad)]

    def gated(gate_part, up_part, grad):
        sig = 1.0 / (1.0 + jnp.exp(-gate_part))
        silu = gate_part * sig
        return (
            (silu * up_part).astype(bf16),
            (grad * up_part * (sig * (1.0 + gate_part * (1.0 - sig)))).astype(bf16),
            (grad * silu).astype(bf16),
        )

    weights[0].wait()
    weights[1].wait()
    for lo, size in tiles(units, 256):
        at = slice(lo, lo + size)
        gate_part = nt(rows[...], w_in[0, at, :])
        up_part = nt(rows[...], w_in[1, at, :])
        grad = nt(slots[...], w_out[at, :])
        hidden[:, at], gu[0, :, at], gu[1, :, at] = gated(gate_part, up_part, grad)
    kept_copies += [keep(2, hidden), keep(3, gu)]
    weights[2].wait()
    for lo, size in tiles(shared_units, 256):
        at = slice(lo, lo + size)
        gate_part = nt(tok[0:length, :], w_sh[0, at, :])
        up_part = nt(tok[0:length, :], w_sh[1, at, :])
        grad = nt(y_grad[...], w_sh[2, at, :])
        s_hidden[:, at], s_gu[0, :, at], s_gu[1, :, at] = gated(gate_part, up_part, grad)
    kept_copies += [keep(6, s_hidden), keep(7, s_gu)]

    def last(n, sums):
        slot_dots, sigma_dots = sums
        cols = pl.ds(pl.multiple_of(n * wide, wide), wide)
        made = mm(hidden[...], w_out[:, cols]).astype(bf16).astype(f32)
        slot_dots = slot_dots + jnp.sum(
            up_rows[:, cols].astype(f32) * made, axis=1, keepdims=True
        )
        routed = mm(place, (gates * made).astype(bf16))
        shared = mm(s_hidden[...], w_sh[2, :, cols])
        sigma_dots = sigma_dots + jnp.sum(
            up[0:length, cols].astype(f32) * shared, axis=1, keepdims=True
        )
        moe_own[:, cols] = (routed[:length] + sigma * shared).astype(bf16)
        moe_other[:, cols] = routed[length:].astype(bf16)
        entry = mm(gu[0], w_in[0, :, cols]) + mm(gu[1], w_in[1, :, cols])
        routed = mm(place, entry.astype(bf16))
        shared = mm(s_gu[0], w_sh[0, :, cols]) + mm(s_gu[1], w_sh[1, :, cols])
        back_own[:, cols] = (routed[:length] + shared).astype(bf16)
        back_other[:, cols] = routed[length:].astype(bf16)
        return slot_dots, sigma_dots

    slot_dots, sigma_dots = lax.fori_loop(
        0,
        width // wide,
        last,
        (jnp.zeros((2 * capacity, 1), f32), jnp.zeros((length, 1), f32)),
    )
    dots[0:1, :] = jnp.sum(jnp.where(pick_own, slot_dots[:capacity], 0.0), axis=0, keepdims=True)
    dots[1:2, :] = jnp.sum(jnp.where(pick_other, slot_dots[capacity:], 0.0), axis=0, keepdims=True)
    row = lax.broadcasted_iota(jnp.int32, (length, length), 0)
    col = lax.broadcasted_iota(jnp.int32, (length, length), 1)
    dots[2:3, :] = jnp.sum(jnp.where(row == col, sigma_dots, 0.0), axis=0, keepdims=True)
    dots[3:, :] = jnp.zeros((dots.shape[0] - 3, length), f32)
    for copy in kept_copies:
        copy.wait()


def moe_call(index, sizes, chips, pieces, half, row_aux, col_aux, weights, kept):
    length, width, capacity, units, shared_units = sizes
    plan = [[(a, b, piece.shape[0]) for piece, a, b in group] for group in pieces]
    arrays = [piece for group in pieces for piece, _, _ in group]
    first = kept is None
    kept_shapes = [
        jax.ShapeDtypeStruct(shape, bf16)
        for shape in (
            (chips, 2 * capacity, width),
            (chips, 2 * capacity, width),
            (chips, 2 * capacity, units),
            (2, chips, 2 * capacity, units),
            (chips, length, width),
            (chips, length, width),
            (chips, length, shared_units),
            (2, chips, length, shared_units),
        )
    ]
    block = jax.ShapeDtypeStruct((length, width), bf16)
    operands = [half, row_aux, col_aux, *arrays, *weights] + ([] if first else list(kept))
    aliases = {} if first else {len(operands) - 8 + i: i for i in range(8)}
    flops = 2 * 2 * capacity * width * units * 6 + 2 * length * width * shared_units * 6
    flops += 2 * 2 * length * 2 * capacity * width * 4
    out = pl.pallas_call(
        functools.partial(moe_kernel, index, first, plan, sizes),
        out_shape=kept_shapes + [block] * 4 + [jax.ShapeDtypeStruct((8, length), f32)],
        in_specs=[in_smem, in_vmem, in_vmem]
        + [in_any] * (len(arrays) + 3 + (0 if first else 8)),
        out_specs=[in_any] * 8 + [in_vmem] * 5,
        scratch_shapes=[
            pltpu.VMEM((2 * length, width), bf16),
            pltpu.VMEM((2 * length, width), bf16),
            pltpu.VMEM((2, units, width), bf16),
            pltpu.VMEM((units, width), bf16),
            pltpu.VMEM((3, shared_units, width), bf16),
            pltpu.VMEM((2 * capacity, width), bf16),
            pltpu.VMEM((2 * capacity, width), bf16),
            pltpu.VMEM((2 * capacity, width), bf16),
            pltpu.VMEM((2 * capacity, units), bf16),
            pltpu.VMEM((2, 2 * capacity, units), bf16),
            pltpu.VMEM((length, width), bf16),
            pltpu.VMEM((length, shared_units), bf16),
            pltpu.VMEM((2, length, shared_units), bf16),
            pltpu.SemaphoreType.DMA((len(arrays),)),
            pltpu.SemaphoreType.DMA((3,)),
            pltpu.SemaphoreType.DMA((8,)),
        ],
        input_output_aliases=aliases,
        compiler_params=params(),
        cost_estimate=pl.CostEstimate(
            flops=flops, bytes_accessed=32 * 1024 * 1024, transcendentals=0
        ),
        name=f"experts_{index}",
    )(*operands)
    return out[:8], out[8:12], out[12]


class Ring:
    def __init__(self, devices):
        self.devices = devices
        self.chips = devices // 2
        order = chip_ring(self.chips)
        n = self.chips
        self.next = [
            (order[i] * 2 + c, order[(i + 1) % n] * 2 + c) for i in range(n) for c in range(2)
        ]
        self.prev = [(b, a) for a, b in self.next]
        self.core = [(e, e ^ 1) for e in range(devices)]
        half = n // 2
        offsets = [0]
        for k in range(1, half):
            offsets += [-k, k]
        self.offsets = offsets + [half]
        place = {chip: i for i, chip in enumerate(order)}
        self.chip_table = np.array(
            [
                [order[(place[e // 2] + o) % n] for o in self.offsets]
                for e in range(devices)
            ],
            np.int32,
        )
        self.seq_table = np.stack(
            [
                2 * self.chip_table + (np.arange(devices) % 2)[:, None],
                2 * self.chip_table + 1 - (np.arange(devices) % 2)[:, None],
            ],
            axis=-1,
        ).reshape(devices, devices)
        self.seq_inverse = np.argsort(self.seq_table, axis=1).astype(np.int32)

    def gather(self, block):
        half = self.chips // 2
        found = {0: block}
        ahead = back = block
        for k in range(1, half):
            ahead = lax.ppermute(ahead, "expert", self.next)
            back = lax.ppermute(back, "expert", self.prev)
            found[-k], found[k] = ahead, back
        cut = block.shape[0] // 2
        first = lax.ppermute(ahead[:cut], "expert", self.next)
        second = lax.ppermute(back[cut:], "expert", self.prev)
        return {o: [b] for o, b in found.items()} | {half: [first, second]}

    def gather_whole(self, block):
        found = self.gather(block)
        return [
            found[o][0] if len(found[o]) == 1 else jnp.concatenate(found[o], axis=0)
            for o in self.offsets
        ]

    def reduce(self, terms):
        half = self.chips // 2

        def total(offset, more=()):
            out = None
            for term in list(terms[offset]) + list(more):
                out = term.astype(f32) if out is None else out + term.astype(f32)
            return out

        far = total(half).astype(bf16)
        cut = far.shape[0] // 2
        ahead = lax.ppermute(far[:cut], "expert", self.next)
        back = lax.ppermute(far[cut:], "expert", self.prev)
        for k in range(half - 1, 0, -1):
            mine, yours = total(k), total(-k)
            if k == half - 1:
                mine = jnp.concatenate([mine[:cut] + ahead.astype(f32), mine[cut:]], axis=0)
                yours = jnp.concatenate([yours[:cut], yours[cut:] + back.astype(f32)], axis=0)
            else:
                mine = mine + ahead.astype(f32)
                yours = yours + back.astype(f32)
            ahead = lax.ppermute(mine.astype(bf16), "expert", self.next)
            back = lax.ppermute(yours.astype(bf16), "expert", self.prev)
        return total(0, (ahead, back))

    def swap_core(self, block):
        return lax.ppermute(block, "expert", self.core)

    def gather_small(self, row, me):
        held = row[None]
        step = 1
        while step < self.devices:
            pairs = [(e, e ^ step) for e in range(self.devices)]
            other = lax.ppermute(held, "expert", pairs)
            upper = (me // step) % 2 == 1
            held = jnp.where(
                upper, jnp.concatenate([other, held]), jnp.concatenate([held, other])
            )
            step *= 2
        return held


def after(value, *others):
    return lax.optimization_barrier((value,) + others)[0]


def swap_tensor(block):
    return lax.ppermute(block, "tensor", [(0, 1), (1, 0)])


def sum_tensor(part):
    own = part.astype(bf16)
    return own.astype(f32) + swap_tensor(own).astype(f32)


def make_local(ring):
    devices, chips = ring.devices, ring.chips

    def local(
        tokens_in,
        cotangent,
        norm_gains,
        qkv_weight,
        qkv_bias,
        out_weight,
        router_weight,
        shared_gate,
        shared_in,
        shared_out,
        expert_in,
        expert_out,
        expert_ids,
        prefix_len,
    ):
        me = lax.axis_index("expert")
        core = me % 2
        half = lax.axis_index("tensor")
        length, width = tokens_in.shape
        top_count = expert_ids.shape[1]
        experts = router_weight.shape[1]
        capacity = length * top_count * 3 // (2 * experts)
        rows_dev = qkv_weight.shape[0]
        heads_t = qkv_bias.shape[1]
        heads = heads_t // 2
        hd_dev = qkv_bias.shape[2]
        head_size = hd_dev * devices
        half_cols = heads * head_size
        score_scale = head_size ** (-0.5)
        chip_of = jnp.asarray(ring.chip_table)[me]
        seq_of = jnp.asarray(ring.seq_table)[me]
        seq_inv = jnp.asarray(ring.seq_inverse)[me]

        pieces = [
            norm_gains.reshape(-1),
            qkv_bias.reshape(-1),
            router_weight.reshape(-1),
            shared_gate.reshape(-1),
            expert_ids.T.astype(bf16).reshape(-1),
            prefix_len.astype(bf16).reshape(-1),
        ]
        sizes = [p.shape[0] for p in pieces]
        total = sum(sizes)
        padded = -(-total // 1024) * 1024
        small = jnp.concatenate(pieces + [jnp.zeros((padded - total,), bf16)])
        small_all = ring.gather_small(small, me)
        cuts = np.cumsum([0] + sizes)
        found = [small_all[:, cuts[i] : cuts[i + 1]] for i in range(len(sizes))]
        gains_f = (
            found[0].reshape(devices, 2, rows_dev).transpose(1, 0, 2).reshape(2, width).astype(f32)
        )
        bias_all = (
            found[1].reshape(devices, 3, heads_t, hd_dev).transpose(1, 2, 0, 3)
            .reshape(3, 2, half_cols)
        )
        bias = lax.dynamic_index_in_dim(bias_all, core, 1, keepdims=False).astype(f32)
        router_w = found[2].reshape(width, experts)
        gate_vec = found[3].reshape(width)
        ids_all = found[4].reshape(devices, top_count, length).astype(jnp.int32)
        prefix_all = found[5].reshape(devices).astype(jnp.int32)
        prefix_pair = jnp.stack([prefix_all[me], prefix_all[me ^ 1]])

        depth = 2 * rows_dev

        def by_core(own, other, axis):
            return jnp.where(
                core == 0,
                jnp.concatenate([own, other], axis=axis),
                jnp.concatenate([other, own], axis=axis),
            )

        def halves(array, axis):
            size = array.shape[axis] // 2
            own = lax.dynamic_slice_in_dim(array, core * size, size, axis)
            return own, lax.dynamic_slice_in_dim(array, (1 - core) * size, size, axis)

        own, other = halves(qkv_weight.transpose(1, 0, 2), 2)
        qkv_blocks = ring.gather_whole(
            by_core(own, ring.swap_core(other), 1).reshape(3 * depth, half_cols)
        )
        own, other = halves(out_weight, 0)
        out_block = by_core(own.T, ring.swap_core(other).T, 0)
        out_blocks = ring.gather_whole(after(out_block, qkv_blocks[-1]))

        units = shared_out.shape[0]
        unit_chip = units // chips
        sh_send = jnp.concatenate(
            [
                shared_in.transpose(1, 2, 0).reshape(2, chips, unit_chip, rows_dev),
                shared_out.reshape(1, chips, unit_chip, rows_dev),
            ],
            axis=0,
        ).transpose(1, 0, 2, 3)
        sh_send = after(sh_send.reshape(chips, 3 * unit_chip, rows_dev), qkv_blocks[-1])
        same_core = [[2 * i + c for i in range(chips)] for c in range(2)]
        sh_mine = lax.all_to_all(
            sh_send, "expert", split_axis=0, concat_axis=0, tiled=True, axis_index_groups=same_core
        )
        sh_w = by_core(sh_mine[:, None], ring.swap_core(sh_mine)[:, None], 1)
        sh_w = sh_w.transpose(2, 0, 1, 3).reshape(3, unit_chip, width)

        half_length = length // 2
        up_half = lax.dynamic_slice_in_dim(cotangent, half * half_length, half_length, 0)
        up_ring = ring.gather(after(up_half, out_blocks[-1]))
        up_own, up_other = {}, {}
        for offset in ring.offsets:
            pieces, at = [], 0
            for piece in up_ring[offset]:
                pieces.append((piece, at, half_length + at))
                pieces.append((swap_tensor(piece), half_length + at, at))
                at += piece.shape[0]
            up_own[offset] = pieces
            up_other[offset] = [(ring.swap_core(p), a, b) for p, a, b in pieces]

        inputs = tokens_in.astype(f32)
        first_b = rms_norm(inputs, gains_f[0]).astype(bf16)
        first_o = ring.swap_core(first_b)
        cosine, sine = rotary_tables(length, head_size)
        pair_cols = jax.ShapeDtypeStruct((2 * length, half_cols), bf16)
        chip_arg = chip_of.astype(jnp.int32)

        def cost(flops, moved):
            return pl.CostEstimate(flops=flops, bytes_accessed=moved, transcendentals=0)

        query, key, value, mixed = pl.pallas_call(
            functools.partial(attend_kernel, chips, heads, score_scale),
            out_shape=[pair_cols] * 4,
            in_specs=[in_smem] * 2 + [in_vmem] * 5 + [in_any] * chips,
            out_specs=[in_vmem] * 4,
            scratch_shapes=[
                pltpu.VMEM((3, width, half_cols), bf16),
                pltpu.SemaphoreType.DMA((3 * chips,)),
            ],
            compiler_params=params(),
            cost_estimate=cost(2 * 2 * length * width * 3 * half_cols, 12 * 1024 * 1024),
            name="attend",
        )(chip_arg, prefix_pair, first_b, first_o, bias.reshape(1, -1), cosine, sine, *qkv_blocks)
        attn_own, attn_give = pl.pallas_call(
            functools.partial(project_kernel, chips),
            out_shape=[
                jax.ShapeDtypeStruct((length, width), f32),
                jax.ShapeDtypeStruct((length, width), bf16),
            ],
            in_specs=[in_smem, in_vmem] + [in_any] * chips,
            out_specs=[in_vmem] * 2,
            scratch_shapes=[
                pltpu.VMEM((1, width, half_cols), bf16),
                pltpu.SemaphoreType.DMA((chips,)),
            ],
            compiler_params=params(),
            cost_estimate=cost(2 * 2 * length * width * half_cols, 6 * 1024 * 1024),
            name="project",
        )(chip_arg, mixed, *out_blocks)
        attn_out = sum_tensor(attn_own + ring.swap_core(attn_give).astype(f32))
        residual = inputs + attn_out
        second_b = rms_norm(residual, gains_f[1]).astype(bf16)

        rows_own, rows_other = {}, {}
        for offset, pieces in ring.gather(second_b).items():
            starts = [sum(p.shape[0] for p in pieces[:j]) for j in range(len(pieces))]
            rows_own[offset] = [(p, a, a) for p, a in zip(pieces, starts, strict=True)]
            rows_other[offset] = [(ring.swap_core(p), a, a) for p, a, _ in rows_own[offset]]

        logits = mm(second_b, router_w)
        expert_range = jnp.arange(experts, dtype=jnp.int32)
        route_match = expert_ids[:, :, None] == expert_range[None, None, :]
        chosen = jnp.sum(jnp.where(route_match, logits[:, None, :], 0.0), axis=-1)
        gate_weights = jax.nn.softmax(chosen, axis=-1)
        shared_sigma = jax.nn.sigmoid(
            jnp.sum(second_b.astype(f32) * gate_vec.astype(f32)[None], axis=-1)
        )
        gate_dense = jnp.sum(jnp.where(route_match, gate_weights[:, :, None], 0.0), axis=1)
        gate_send = jnp.stack(
            [gate_dense.T, jnp.broadcast_to(shared_sigma[None], (experts, length))], axis=1
        )
        gate_all = lax.all_to_all(gate_send, "expert", split_axis=0, concat_axis=0, tiled=True)
        gate_all = gate_all[seq_of].reshape(chips, 2, 2, length)

        match = jnp.any(ids_all[seq_of] == me, axis=1)
        triangle = jnp.asarray(np.triu(np.ones((length, length), np.float32)), bf16)
        rank = jnp.where(match, mm(match.astype(bf16), triangle) - 1.0, no_slot)
        rank = rank.reshape(chips, 2, length)
        blank = jnp.zeros((chips, 3, length), f32)
        row_aux = jnp.concatenate([rank, gate_all[:, :, 0], gate_all[:, :1, 1], blank], axis=1)
        col_aux = jnp.concatenate(
            [rank, gate_all[:, :1, 1], jnp.zeros((chips, 5, length), f32)], axis=1
        ).transpose(0, 2, 1)

        ex_in = expert_in[0].transpose(1, 2, 0)
        ex_out = expert_out[0]
        part_units = ex_out.shape[0]
        sizes = (length, width, capacity, part_units, unit_chip)
        half_arg = half.astype(jnp.int32).reshape(1)
        kept = None
        moe, back, dot_rows = {}, {}, []
        for i, offset in enumerate(ring.offsets):
            pieces = [rows_own[offset], rows_other[offset], up_own[offset], up_other[offset]]
            kept, blocks, rows = moe_call(
                i, sizes, chips, pieces, half_arg, row_aux, col_aux, (ex_in, ex_out, sh_w), kept
            )
            moe[offset], back[offset] = blocks[:2], blocks[2:]
            dot_rows.append(rows)

        back_terms = {o: [a, ring.swap_core(b)] for o, (a, b) in back.items()}
        second_part = ring.reduce(back_terms)
        moe_terms = {o: [a, ring.swap_core(b)] for o, (a, b) in moe.items()}
        moe_part = ring.reduce(moe_terms)
        output = (residual + sum_tensor(moe_part)).astype(bf16)

        dots = jnp.stack(dot_rows, axis=0)
        sdots = jnp.concatenate([dots[:, 2:3], jnp.zeros_like(dots[:, 2:3])], axis=1)
        dot_send = jnp.stack([dots[:, :2], sdots], axis=2).reshape(devices, 2, length)[seq_inv]
        dot_got = lax.all_to_all(dot_send, "expert", split_axis=0, concat_axis=0, tiled=True)
        dot_got = jnp.concatenate([dot_got[:, 0], jnp.sum(dot_got[:, 1], axis=0)[None]], axis=0)
        dot_got = dot_got + swap_tensor(dot_got)
        gate_grad_dense, sigma_grad = dot_got[:experts].T, dot_got[experts]
        row_term = jnp.sum(gate_dense * gate_grad_dense, axis=-1, keepdims=True)
        logit_grad = (gate_dense * (gate_grad_dense - row_term)).astype(bf16)
        gate_logit_grad = sigma_grad * shared_sigma * (1.0 - shared_sigma)

        second_grad = sum_tensor(second_part)
        second_grad = second_grad + mm(logit_grad, router_w, 1, 1)
        second_grad = second_grad + gate_logit_grad[:, None] * gate_vec.astype(f32)[None]
        upstream = cotangent.astype(f32)
        residual_norm_grad, gain_two_grad = jax.vjp(rms_norm, residual, gains_f[1])[1](second_grad)
        residual_grad = upstream + residual_norm_grad
        attn_grad = residual_grad.astype(bf16)
        attn_grad_o = ring.swap_core(attn_grad)

        def by_chip(left, other, right):
            pair = jnp.concatenate([left, other], axis=0)
            return {
                offset: [
                    mm(lax.dynamic_slice_in_dim(pair, chip_of[i] * depth, depth, 1), right, 0, 0)
                ]
                for i, offset in enumerate(ring.offsets)
            }

        proj_grad, bias_grad = pl.pallas_call(
            functools.partial(attend_back_kernel, chips, heads, score_scale),
            out_shape=[
                jax.ShapeDtypeStruct((2 * length, 3 * half_cols), bf16),
                jax.ShapeDtypeStruct((1, 3 * half_cols), f32),
            ],
            in_specs=[in_smem] * 2 + [in_vmem] * 7 + [in_any] * chips,
            out_specs=[in_vmem] * 2,
            scratch_shapes=[
                pltpu.VMEM((1, width, half_cols), bf16),
                pltpu.SemaphoreType.DMA((chips,)),
            ],
            compiler_params=params(),
            cost_estimate=cost(2 * 2 * length * width * half_cols * 2, 8 * 1024 * 1024),
            name="attend_back",
        )(
            chip_arg,
            prefix_pair,
            attn_grad,
            attn_grad_o,
            query,
            key,
            value,
            cosine,
            sine,
            *out_blocks,
        )
        qkv_grad = ring.reduce(by_chip(first_b, first_o, proj_grad))
        out_grad = ring.reduce(by_chip(attn_grad, attn_grad_o, mixed))
        bias_grad = bias_grad[0]
        first_own, first_give = pl.pallas_call(
            functools.partial(project_back_kernel, chips),
            out_shape=[
                jax.ShapeDtypeStruct((length, width), f32),
                jax.ShapeDtypeStruct((length, width), bf16),
            ],
            in_specs=[in_smem, in_vmem] + [in_any] * chips,
            out_specs=[in_vmem] * 2,
            scratch_shapes=[
                pltpu.VMEM((3, width, half_cols), bf16),
                pltpu.SemaphoreType.DMA((3 * chips,)),
            ],
            compiler_params=params(),
            cost_estimate=cost(2 * 2 * length * width * 3 * half_cols, 12 * 1024 * 1024),
            name="project_back",
        )(chip_arg, proj_grad, *qkv_blocks)
        first_grad = sum_tensor(first_own + ring.swap_core(first_give).astype(f32))
        input_norm_grad, gain_one_grad = jax.vjp(rms_norm, inputs, gains_f[0])[1](first_grad)
        input_grad = (residual_grad + input_norm_grad).astype(bf16)

        def regroup(grad, parts):
            own, other = halves(grad, 0)
            own = own.astype(bf16).reshape(rows_dev, parts, half_cols)
            got = ring.swap_core(other.astype(bf16)).reshape(rows_dev, parts, half_cols)
            return by_core(own, got, 2).astype(f32)

        qkv_weight_grad = regroup(qkv_grad, 3)
        out_weight_grad = regroup(out_grad, 1)[:, 0].T

        rows_all, slots_all, hidden_all, gu_all, tok_all, y_all, s_hidden_all, s_gu_all = kept
        slot_count = chips * 2 * capacity
        rows_all = rows_all.reshape(slot_count, width)
        expert_out_grad = mm(
            hidden_all.reshape(slot_count, part_units), slots_all.reshape(slot_count, width), 0, 0
        )[None]
        expert_in_grad = mm(gu_all.reshape(2, slot_count, part_units), rows_all, 1, 0)
        expert_in_grad = expert_in_grad.transpose(2, 0, 1)[None]
        token_count = chips * length
        sh_in_grad = mm(
            s_gu_all.reshape(2, token_count, unit_chip), tok_all.reshape(token_count, width), 1, 0
        )
        sh_out_grad = mm(
            s_hidden_all.reshape(token_count, unit_chip), y_all.reshape(token_count, width), 0, 0
        )
        sh_grad = jnp.concatenate(
            [sh_in_grad.astype(bf16), sh_out_grad.astype(bf16)[None]], axis=0
        ).reshape(3 * unit_chip, chips, 2, rows_dev)
        sh_grad = sh_grad.transpose(2, 1, 0, 3)
        own, other = halves(sh_grad, 0)
        sh_sum = (own.astype(f32) + ring.swap_core(other).astype(f32)).astype(bf16)[0]
        sh_back = lax.all_to_all(
            sh_sum, "expert", split_axis=0, concat_axis=0, tiled=True, axis_index_groups=same_core
        )
        sh_back = sh_back.reshape(chips, 3, unit_chip, rows_dev).astype(f32)
        shared_in_grad = sh_back[:, :2].transpose(3, 1, 0, 2).reshape(rows_dev, 2, units)
        shared_out_grad = sh_back[:, 2].reshape(units, rows_dev)

        second_f = second_b.astype(f32)
        router_part = mm(second_b, logit_grad, 0, 0)
        shared_gate_part = jnp.sum(gate_logit_grad[:, None] * second_f, axis=0)
        early = jnp.concatenate(
            [router_part, shared_gate_part[:, None], gain_two_grad[:, None]], axis=1
        ).reshape(devices, rows_dev * (experts + 2))
        early = lax.all_to_all(early, "expert", split_axis=0, concat_axis=0, tiled=True)
        early = jnp.sum(early, axis=0).reshape(rows_dev, experts + 2)
        router_grad, shared_gate_grad = early[:, :experts], early[:, experts]
        bias_send = bias_grad.reshape(3 * heads, devices, hd_dev).transpose(1, 0, 2)
        late = jnp.concatenate(
            [gain_one_grad.reshape(devices, rows_dev), bias_send.reshape(devices, -1)], axis=1
        )
        late = lax.all_to_all(late, "expert", split_axis=0, concat_axis=0, tiled=True)
        gain_one = jnp.sum(late[:, :rows_dev], axis=0)
        bias_got = jnp.sum(late[:, rows_dev:].reshape(chips, 2, 3, heads, hd_dev), axis=0)
        qkv_bias_grad = bias_got.transpose(1, 0, 2, 3).reshape(3, heads_t, hd_dev)
        gains_grad = jnp.stack([gain_one, early[:, experts + 1]], axis=0)

        return (
            output,
            input_grad,
            gains_grad,
            qkv_weight_grad,
            qkv_bias_grad,
            out_weight_grad,
            router_grad,
            shared_gate_grad,
            shared_in_grad,
            shared_out_grad,
            expert_in_grad,
            expert_out_grad,
        )

    return local


def solution(mesh):
    ring = Ring(mesh.shape["expert"])
    return jax.shard_map(
        make_local(ring),
        mesh=mesh,
        in_specs=(
            P("expert", None),
            P("expert", None),
            P(None, "expert"),
            P("expert", None, "tensor"),
            P(None, "tensor", "expert"),
            P("tensor", "expert"),
            P("expert", None),
            P("expert"),
            P("expert", None, "tensor"),
            P("tensor", "expert"),
            P("expert", None, None, "tensor"),
            P("expert", "tensor", None),
            P("expert", None),
            P("expert"),
        ),
        out_specs=(
            P("expert", None),
            P("expert", None),
            P(None, "expert"),
            P("expert", None, "tensor"),
            P(None, "tensor", "expert"),
            P("tensor", "expert"),
            P("expert", None),
            P("expert"),
            P("expert", None, "tensor"),
            P("tensor", "expert"),
            P("expert", None, None, "tensor"),
            P("expert", "tensor", None),
        ),
        check_vma=False,
    )
```

```python
import functools

import jax
import jax.numpy as jnp
import numpy as np
from jax import lax
from jax.experimental import pallas as pl
from jax.experimental.pallas import tpu as pltpu
from jax.sharding import PartitionSpec as P

eps = 1e-06
theta_base = 1000000.0
neg_large = -1e30
no_slot = -100000.0
bf16 = jnp.bfloat16
f32 = jnp.float32
in_vmem = pl.BlockSpec(memory_space=pltpu.VMEM)
in_smem = pl.BlockSpec(memory_space=pltpu.SMEM)
in_any = pl.BlockSpec(memory_space=pl.ANY)


def rms_norm(values, gain_row):
    factor = lax.rsqrt(jnp.mean(values * values, axis=-1, keepdims=True) + eps)
    return values * factor * gain_row


def rotary_tables(length, head_size):
    half_size = head_size // 2
    frequency = np.float32(theta_base) ** (
        -(np.arange(half_size, dtype=np.float32) * np.float32(2.0)) / np.float32(head_size)
    )
    angles = np.arange(length, dtype=np.float32)[:, None] * frequency[None, :].astype(np.float32)
    cosine = np.concatenate([np.cos(angles), np.cos(angles)], axis=-1)
    sine = np.concatenate([-np.sin(angles), np.sin(angles)], axis=-1)
    return jnp.asarray(cosine, f32), jnp.asarray(sine, f32)


def chip_ring(chips):
    columns = chips // 4
    if chips % 4 or columns < 2 or columns % 2:
        return list(range(chips))
    walk = [(0, 0)]
    for column in range(columns):
        rows = range(1, 4) if column % 2 == 0 else range(3, 0, -1)
        walk += [(row, column) for row in rows]
    walk += [(0, column) for column in range(columns - 1, 0, -1)]
    return [row * columns + column for row, column in walk]


def mm(left, right, contract_left=1, contract_right=0):
    return lax.dot_general(
        left,
        right,
        (((contract_left,), (contract_right,)), ((), ())),
        preferred_element_type=f32,
    )


def nt(left, right):
    return mm(left, right, 1, 1)


def tiles(total, size):
    return [(lo, min(size, total - lo)) for lo in range(0, total, size)]


def params(mebibytes=56):
    return pltpu.CompilerParams(vmem_limit_bytes=mebibytes * 1024 * 1024)


def half_turn(values):
    return pltpu.roll(values, values.shape[1] // 2, 1)


def masked(scores, prefix_cut):
    length = scores.shape[0]
    row = lax.broadcasted_iota(jnp.int32, (length, length), 0)
    col = lax.broadcasted_iota(jnp.int32, (length, length), 1)
    return jnp.where((col <= row) | (col < prefix_cut), scores, neg_large)


def softmax_rows(scores):
    weights = jnp.exp(scores - jnp.max(scores, axis=-1, keepdims=True))
    return weights / jnp.sum(weights, axis=-1, keepdims=True)


def load_blocks(chip_ref, blocks, scratch, sem, first, last):
    whole = len(blocks) - 2
    depth = blocks[0].shape[0] // 4
    copies = []
    for i in range(whole + 1):
        start = pl.multiple_of(chip_ref[i] * depth, depth)
        for c in range(first, last):
            block, at = (blocks[i], c) if i < whole else (blocks[whole + c // 2], c % 2)
            copies.append(
                pltpu.make_async_copy(
                    block.at[pl.ds(at * depth, depth)],
                    scratch.at[c - first, pl.ds(start, depth)],
                    sem.at[len(copies)],
                )
            )
    for copy in copies:
        copy.start()
    return copies


def attend_kernel(count, heads, scale, *refs):
    chip_ref, prefix_ref, own, other, bias, cosine, sine = refs[:7]
    blocks = refs[7 : 7 + count]
    query, key, value, mixed, weight, sem = refs[7 + count :]
    copies = load_blocks(chip_ref, blocks, weight, sem, 0, 3)
    length, head_size = cosine.shape
    columns = heads * head_size
    for copy in copies:
        copy.wait()
    for c, out in enumerate((query, key, value)):
        for b, rows in enumerate((own, other)):
            for lo, size in tiles(columns, 2 * head_size):
                part = mm(rows[...], weight[c, :, lo : lo + size])
                part = part + bias[:, c * columns + lo : c * columns + lo + size]
                for at in range(0, size, head_size):
                    one = part[:, at : at + head_size]
                    if c < 2:
                        one = one * cosine[...] + half_turn(one) * sine[...]
                    out[b * length : (b + 1) * length, lo + at : lo + at + head_size] = one.astype(
                        bf16
                    )
    for b in range(2):
        rows = slice(b * length, (b + 1) * length)
        for h in range(heads):
            cols = slice(h * head_size, (h + 1) * head_size)
            scores = masked(nt(query[rows, cols], key[rows, cols]) * scale, prefix_ref[b])
            probs = softmax_rows(scores).astype(bf16)
            mixed[rows, cols] = mm(probs, value[rows, cols]).astype(bf16)


def project_kernel(count, *refs):
    chip_ref, mixed = refs[:2]
    blocks = refs[2 : 2 + count]
    own, other, weight, sem = refs[2 + count :]
    copies = load_blocks(chip_ref, blocks, weight, sem, 3, 4)
    for copy in copies:
        copy.wait()
    length, width = own.shape
    for lo, size in tiles(width, 512):
        part = nt(mixed[...], weight[0, lo : lo + size, :])
        own[:, lo : lo + size] = part[:length].astype(own.dtype)
        other[:, lo : lo + size] = part[length:].astype(other.dtype)


def attend_back_kernel(count, heads, scale, *refs):
    chip_ref, prefix_ref, own, other, query, key, value, cosine, sine = refs[:9]
    blocks = refs[9 : 9 + count]
    grad, bias, weight, sem = refs[9 + count :]
    copies = load_blocks(chip_ref, blocks, weight, sem, 3, 4)
    length, head_size = cosine.shape
    columns = heads * head_size
    for copy in copies:
        copy.wait()
    for b, up in enumerate((own, other)):
        rows = slice(b * length, (b + 1) * length)
        mixed_grad = mm(up[...], weight[0]).astype(bf16)
        for h in range(heads):
            cols = slice(h * head_size, (h + 1) * head_size)
            q, k, v = query[rows, cols], key[rows, cols], value[rows, cols]
            up_head = mixed_grad[:, cols]
            probs = softmax_rows(masked(nt(q, k) * scale, prefix_ref[b]))
            prob_grad = nt(up_head, v)
            row_term = jnp.sum(probs * prob_grad, axis=-1, keepdims=True)
            score_grad = (probs * (prob_grad - row_term)).astype(bf16)
            q_grad = mm(score_grad, k) * scale
            k_grad = mm(score_grad, q, 0, 0) * scale
            v_grad = mm(probs.astype(bf16), up_head, 0, 0)
            for c, one in enumerate((q_grad, k_grad, v_grad)):
                if c < 2:
                    one = one * cosine[...] - half_turn(one) * sine[...]
                one = one.astype(bf16)
                at = slice(c * columns + h * head_size, c * columns + (h + 1) * head_size)
                grad[rows, at] = one
                column_sum = jnp.sum(one.astype(f32), axis=0, keepdims=True)
                bias[:, at] = column_sum if b == 0 else bias[:, at] + column_sum


def project_back_kernel(count, *refs):
    chip_ref, grad = refs[:2]
    blocks = refs[2 : 2 + count]
    own, other, weight, sem = refs[2 + count :]
    copies = load_blocks(chip_ref, blocks, weight, sem, 0, 3)
    for copy in copies:
        copy.wait()
    length, width = own.shape
    columns = grad.shape[1] // 3
    for lo, size in tiles(width, 512):
        part = nt(grad[:, :columns], weight[0, lo : lo + size, :])
        for c in range(1, 3):
            part = part + nt(grad[:, c * columns : (c + 1) * columns], weight[c, lo : lo + size, :])
        own[:, lo : lo + size] = part[:length].astype(own.dtype)
        other[:, lo : lo + size] = part[length:].astype(other.dtype)


def moe_kernel(index, span, first, plan, sizes, *refs):
    length, width, capacity, units, shared_units = sizes
    count = sum(len(p) for p in plan)
    own_rows, slab = span * length, 2 * span * capacity
    half_ref, row_ref, col_ref = refs[:3]
    given = refs[3 : 3 + count]
    in_hbm, out_hbm, shared_hbm = refs[3 + count : 6 + count]
    rest = refs[6 + count + (0 if first else 8) :]
    kept, outs, dots = rest[:8], rest[8 : 8 + 4 * span], rest[8 + 4 * span]
    tok, up, rows, up_rows, slots, hidden, gu, y_grad, s_hidden, s_gu, made_out = rest[
        9 + 4 * span : 20 + 4 * span
    ]
    w_in, w_out, w_sh, load_sem, weight_sem, out_sem, keep_sem = rest[20 + 4 * span :]
    wide = min(512, width)
    columns = tiles(width, wide)

    loads = []
    for n, (lo, size_cols) in enumerate(columns):
        cols, number = slice(lo, lo + size_cols), 0
        loads.append([])
        for which, pieces in enumerate(plan):
            target, at = (tok, up)[which // (2 * span)], which % (2 * span) * length
            for start_zero, start_one, size in pieces:
                start = start_zero + half_ref[0] * (start_one - start_zero)
                start = pl.multiple_of(start + at, 16)
                copy = pltpu.make_async_copy(
                    given[number].at[:, cols],
                    target.at[pl.ds(start, size), cols],
                    load_sem.at[n, number],
                )
                copy.start()
                loads[-1].append(copy)
                number += 1

    weights = [
        pltpu.make_async_copy(a, b, weight_sem.at[i])
        for i, (a, b) in enumerate(((shared_hbm, w_sh), (in_hbm, w_in), (out_hbm, w_out)))
    ]
    for copy in weights:
        copy.start()

    def keep(slot, source):
        target = kept[slot]
        size = source.shape[-2]
        first_row = index * (size // span)
        if len(target.shape) == 3:
            target = target.at[:, pl.ds(first_row, size)]
        else:
            target = target.at[pl.ds(first_row, size)]
        copy = pltpu.make_async_copy(source, target, keep_sem.at[slot])
        copy.start()
        return copy

    slot = lax.broadcasted_iota(jnp.int32, (capacity, length), 0).astype(f32)
    lane = lax.broadcasted_iota(jnp.int32, (length, 2 * capacity), 1).astype(f32)
    picks, ones, places, gates, sigmas = [], [], [], [], []
    for j in range(span):
        for c in range(2):
            pick = slot == row_ref[index + j, c : c + 1, :]
            picks.append(pick)
            ones.append(jnp.where(pick, 1.0, 0.0).astype(bf16))
            gate = jnp.where(pick, row_ref[index + j, 2 + c : 3 + c, :], 0.0)
            gates.append(jnp.sum(gate, axis=1, keepdims=True))
        places.append(
            jnp.concatenate(
                [
                    jnp.where(
                        lane == col_ref[index + j, :, c : c + 1] + float(c * capacity), 1.0, 0.0
                    ).astype(bf16)
                    for c in range(2)
                ],
                axis=0,
            )
        )
        sigmas.append(col_ref[index + j, :, 2:3])
    gate_all = jnp.concatenate(gates, axis=0)
    sigma_all = jnp.concatenate(sigmas, axis=0)

    for n, (lo, size) in enumerate(columns):
        cols = slice(lo, lo + size)
        for copy in loads[n]:
            copy.wait()
        for j in range(span):
            for c in range(2):
                source = slice((c * span + j) * length, (c * span + j + 1) * length)
                target = slice((2 * j + c) * capacity, (2 * j + c + 1) * capacity)
                rows[target, cols] = mm(ones[2 * j + c], tok[source, cols]).astype(bf16)
                got = mm(ones[2 * j + c], up[source, cols])
                up_rows[target, cols] = got.astype(bf16)
                slots[target, cols] = (gates[2 * j + c] * got).astype(bf16)
        y_grad[:, cols] = (sigma_all * up[0:own_rows, cols].astype(f32)).astype(bf16)

    kept_copies = [keep(4, tok.at[0:own_rows]), keep(0, rows), keep(1, slots), keep(5, y_grad)]

    def gated(gate_part, up_part, grad):
        sig = 1.0 / (1.0 + jnp.exp(-gate_part))
        silu = gate_part * sig
        return (
            (silu * up_part).astype(bf16),
            (grad * up_part * (sig * (1.0 + gate_part * (1.0 - sig)))).astype(bf16),
            (grad * silu).astype(bf16),
        )

    weights[0].wait()
    for lo, size in tiles(shared_units, 256):
        at = slice(lo, lo + size)
        gate_part = nt(tok[0:own_rows, :], w_sh[0, at, :])
        up_part = nt(tok[0:own_rows, :], w_sh[1, at, :])
        grad = nt(y_grad[...], w_sh[2, at, :])
        s_hidden[:, at], s_gu[0, :, at], s_gu[1, :, at] = gated(gate_part, up_part, grad)
    kept_copies += [keep(6, s_hidden), keep(7, s_gu)]
    weights[1].wait()
    weights[2].wait()
    for lo, size in tiles(units, 256):
        at = slice(lo, lo + size)
        gate_part = nt(rows[...], w_in[0, at, :])
        up_part = nt(rows[...], w_in[1, at, :])
        grad = nt(slots[...], w_out[at, :])
        hidden[:, at], gu[0, :, at], gu[1, :, at] = gated(gate_part, up_part, grad)
    kept_copies += [keep(2, hidden), keep(3, gu)]

    slot_dots, sigma_dots = jnp.zeros((slab, 1), f32), jnp.zeros((own_rows, 1), f32)
    sent = []
    for n, (lo, size) in enumerate(columns):
        cols, turn = slice(lo, lo + size), n % 2
        if n >= 2:
            for copy in sent[n - 2]:
                copy.wait()
        made = mm(hidden[...], w_out[:, cols]).astype(bf16).astype(f32)
        slot_dots = slot_dots + jnp.sum(
            up_rows[:, cols].astype(f32) * made, axis=1, keepdims=True
        )
        made = (gate_all * made).astype(bf16)
        shared = mm(s_hidden[...], w_sh[2, :, cols])
        sigma_dots = sigma_dots + jnp.sum(
            up[0:own_rows, cols].astype(f32) * shared, axis=1, keepdims=True
        )
        shared = sigma_all * shared
        entry = (mm(gu[0], w_in[0, :, cols]) + mm(gu[1], w_in[1, :, cols])).astype(bf16)
        shared_back = mm(s_gu[0], w_sh[0, :, cols]) + mm(s_gu[1], w_sh[1, :, cols])
        sent.append([])
        for j in range(span):
            mine = slice(j * length, (j + 1) * length)
            theirs = slice(2 * j * capacity, 2 * (j + 1) * capacity)
            routed = mm(places[j], made[theirs])
            made_out[turn, 4 * j] = (routed[:length] + shared[mine]).astype(bf16)
            made_out[turn, 4 * j + 1] = routed[length:].astype(bf16)
            routed = mm(places[j], entry[theirs])
            made_out[turn, 4 * j + 2] = (routed[:length] + shared_back[mine]).astype(bf16)
            made_out[turn, 4 * j + 3] = routed[length:].astype(bf16)
            for k in range(4 * j, 4 * j + 4):
                pairs = [(made_out.at[turn, k], outs[k].at[:, cols])]
                if k % 4 < 2:
                    middle = length // 2
                    pairs = [
                        (
                            made_out.at[turn, k, pl.ds(pl.multiple_of(h * middle, 16), middle)],
                            outs[k].at[m * middle : (m + 1) * middle, cols],
                        )
                        for m, h in enumerate((half_ref[0], 1 - half_ref[0]))
                    ]
                for m, (source, target) in enumerate(pairs):
                    copy = pltpu.make_async_copy(source, target, out_sem.at[turn, k, m])
                    copy.start()
                    sent[-1].append(copy)
    row = lax.broadcasted_iota(jnp.int32, (length, length), 0)
    col = lax.broadcasted_iota(jnp.int32, (length, length), 1)
    for j in range(span):
        for c in range(2):
            part = slot_dots[(2 * j + c) * capacity : (2 * j + c + 1) * capacity]
            part = jnp.where(picks[2 * j + c], part, 0.0)
            dots[j, c : c + 1, :] = jnp.sum(part, axis=0, keepdims=True)
        part = jnp.where(row == col, sigma_dots[j * length : (j + 1) * length], 0.0)
        dots[j, 2:3, :] = jnp.sum(part, axis=0, keepdims=True)
        dots[j, 3:, :] = jnp.zeros((dots.shape[1] - 3, length), f32)
    for copy in kept_copies + [copy for group in sent[-2:] for copy in group]:
        copy.wait()


def moe_call(index, span, sizes, chips, pieces, half, row_aux, col_aux, weights, kept):
    length, width, capacity, units, shared_units = sizes
    plan = [[(a, b, piece.shape[0]) for piece, a, b in group] for group in pieces]
    arrays = [piece for group in pieces for piece, _, _ in group]
    first = kept is None
    own_rows, slab = span * length, 2 * span * capacity
    slots, tokens = chips * 2 * capacity, chips * length
    kept_shapes = [
        jax.ShapeDtypeStruct(shape, bf16)
        for shape in (
            (slots, width),
            (slots, width),
            (slots, units),
            (2, slots, units),
            (tokens, width),
            (tokens, width),
            (tokens, shared_units),
            (2, tokens, shared_units),
        )
    ]
    block = jax.ShapeDtypeStruct((length, width), bf16)
    operands = [half, row_aux, col_aux, *arrays, *weights] + ([] if first else list(kept))
    aliases = {} if first else {len(operands) - 8 + i: i for i in range(8)}
    flops = 2 * slab * width * units * 6 + 2 * own_rows * width * shared_units * 6
    out = pl.pallas_call(
        functools.partial(moe_kernel, index, span, first, plan, sizes),
        out_shape=kept_shapes
        + [block] * (4 * span)
        + [jax.ShapeDtypeStruct((span, 8, length), f32)],
        in_specs=[in_smem, in_vmem, in_vmem]
        + [in_any] * (len(arrays) + 3 + (0 if first else 8)),
        out_specs=[in_any] * (8 + 4 * span) + [in_vmem],
        scratch_shapes=[
            pltpu.VMEM((2 * own_rows, width), bf16),
            pltpu.VMEM((2 * own_rows, width), bf16),
            pltpu.VMEM((slab, width), bf16),
            pltpu.VMEM((slab, width), bf16),
            pltpu.VMEM((slab, width), bf16),
            pltpu.VMEM((slab, units), bf16),
            pltpu.VMEM((2, slab, units), bf16),
            pltpu.VMEM((own_rows, width), bf16),
            pltpu.VMEM((own_rows, shared_units), bf16),
            pltpu.VMEM((2, own_rows, shared_units), bf16),
            pltpu.VMEM((2, 4 * span, length, min(512, width)), bf16),
            pltpu.VMEM((2, units, width), bf16),
            pltpu.VMEM((units, width), bf16),
            pltpu.VMEM((3, shared_units, width), bf16),
            pltpu.SemaphoreType.DMA((len(tiles(width, min(512, width))), len(arrays))),
            pltpu.SemaphoreType.DMA((3,)),
            pltpu.SemaphoreType.DMA((2, 4 * span, 2)),
            pltpu.SemaphoreType.DMA((8,)),
        ],
        input_output_aliases=aliases,
        compiler_params=params(),
        cost_estimate=pl.CostEstimate(
            flops=flops, bytes_accessed=(16 + 12 * span) * 1024 * 1024, transcendentals=0
        ),
        name=f"experts_{index}",
    )(*operands)
    blocks = out[8 : 8 + 4 * span]
    return out[:8], [blocks[4 * j : 4 * j + 4] for j in range(span)], out[8 + 4 * span]


def spread_kernel(core_ref, own, other, out):
    parts, units, _ = out.shape
    count, _, rows = own.shape

    def spread(first, second):
        for i in range(count):
            for c in range(parts):
                at = slice(c * units, (c + 1) * units)
                both = jnp.concatenate([first[i, at, :], second[i, at, :]], axis=1)
                out[c, :, 2 * i * rows : 2 * (i + 1) * rows] = both

    @pl.when(core_ref[0] == 0)
    def _():
        spread(own, other)

    @pl.when(core_ref[0] == 1)
    def _():
        spread(other, own)


def shared_grad_kernel(tok, y_grad, hidden, gu, out):
    units = hidden.shape[1]
    rows = out.shape[3]
    for c in range(3):
        left = gu[c] if c < 2 else hidden[...]
        right = tok[...] if c < 2 else y_grad[...]
        part = mm(left, right, 0, 0).astype(bf16)
        for k in range(2):
            out[k, 0, c * units : (c + 1) * units, :] = part[:, k * rows : (k + 1) * rows]


class Ring:
    def __init__(self, devices):
        self.devices = devices
        self.chips = devices // 2
        order = chip_ring(self.chips)
        n = self.chips
        self.next = [
            (order[i] * 2 + c, order[(i + 1) % n] * 2 + c) for i in range(n) for c in range(2)
        ]
        self.prev = [(b, a) for a, b in self.next]
        self.core = [(e, e ^ 1) for e in range(devices)]
        half = n // 2
        offsets = [0]
        for k in range(1, half):
            offsets += [-k, k]
        self.offsets = offsets + [half]
        place = {chip: i for i, chip in enumerate(order)}
        self.chip_table = np.array(
            [
                [order[(place[e // 2] + o) % n] for o in self.offsets]
                for e in range(devices)
            ],
            np.int32,
        )
        self.seq_table = np.stack(
            [
                2 * self.chip_table + (np.arange(devices) % 2)[:, None],
                2 * self.chip_table + 1 - (np.arange(devices) % 2)[:, None],
            ],
            axis=-1,
        ).reshape(devices, devices)
        self.seq_inverse = np.argsort(self.seq_table, axis=1).astype(np.int32)

    def step(self, ahead, back=None, last=False):
        back = ahead if back is None else back
        if last:
            cut = ahead.shape[0] // 2
            ahead, back = ahead[:cut], back[cut:]
        return self.send_pair(ahead, back)

    def send_pair(self, ahead, back):
        return [
            lax.ppermute(ahead, "expert", self.next),
            lax.ppermute(back, "expert", self.prev),
        ]

    def gather(self, block):
        half = self.chips // 2
        found = {0: [block]}
        pair = [block]
        for k in range(1, half):
            pair = self.step(*pair)
            found[-k], found[k] = pair[:1], pair[1:]
        found[half] = self.step(*pair, last=True)
        return found

    def add_up(self, terms):
        out = None
        for term in terms:
            out = term.astype(f32) if out is None else out + term.astype(f32)
        return out

    def reduce_first(self, terms):
        total = self.add_up(terms).astype(bf16)
        return self.step(total, last=True)

    def reduce_terms(self, ahead_terms, back_terms, sending, first):
        mine, yours = self.add_up(ahead_terms), self.add_up(back_terms)
        ahead, back = (part.astype(f32) for part in sending)
        if first:
            cut = ahead.shape[0]
            mine = jnp.concatenate([mine[:cut] + ahead, mine[cut:]], axis=0)
            yours = jnp.concatenate([yours[:cut], yours[cut:] + back], axis=0)
        else:
            mine, yours = mine + ahead, yours + back
        return [mine.astype(bf16), yours.astype(bf16)]

    def reduce(self, terms):
        half = self.chips // 2
        sending = self.reduce_first(terms[half])
        for k in range(half - 1, 0, -1):
            send = self.reduce_terms(terms[k], terms[-k], sending, k == half - 1)
            sending = self.send_pair(*send)
        return self.add_up([*terms[0], *sending])

    def swap_core(self, block):
        return lax.ppermute(block, "expert", self.core)

    def gather_small(self, row, me):
        held = row[None]
        step = 1
        while step < self.devices:
            pairs = [(e, e ^ step) for e in range(self.devices)]
            other = lax.ppermute(held, "expert", pairs)
            upper = (me // step) % 2 == 1
            held = jnp.where(
                upper, jnp.concatenate([other, held]), jnp.concatenate([held, other])
            )
            step *= 2
        return held


def after(value, *others):
    return lax.optimization_barrier((value,) + others)[0]


def hold(*values):
    return list(lax.optimization_barrier(values))


def swap_tensor(block):
    return lax.ppermute(block, "tensor", [(0, 1), (1, 0)])


def sum_tensor(part):
    own = part.astype(bf16)
    return own.astype(f32) + swap_tensor(own).astype(f32)


def make_local(ring):
    devices, chips = ring.devices, ring.chips

    def local(
        tokens_in,
        cotangent,
        norm_gains,
        qkv_weight,
        qkv_bias,
        out_weight,
        router_weight,
        shared_gate,
        shared_in,
        shared_out,
        expert_in,
        expert_out,
        expert_ids,
        prefix_len,
    ):
        me = lax.axis_index("expert")
        core = me % 2
        half = lax.axis_index("tensor")
        length, width = tokens_in.shape
        top_count = expert_ids.shape[1]
        experts = router_weight.shape[1]
        capacity = length * top_count * 3 // (2 * experts)
        rows_dev = qkv_weight.shape[0]
        heads_t = qkv_bias.shape[1]
        heads = heads_t // 2
        hd_dev = qkv_bias.shape[2]
        head_size = hd_dev * devices
        half_cols = heads * head_size
        score_scale = head_size ** (-0.5)
        chip_of = jnp.asarray(ring.chip_table)[me]
        seq_of = jnp.asarray(ring.seq_table)[me]
        seq_inv = jnp.asarray(ring.seq_inverse)[me]

        pieces = [
            norm_gains.reshape(-1),
            qkv_bias.reshape(-1),
            router_weight.reshape(-1),
            shared_gate.reshape(-1),
            expert_ids.T.astype(bf16).reshape(-1),
            prefix_len.astype(bf16).reshape(-1),
        ]
        sizes = [p.shape[0] for p in pieces]
        total = sum(sizes)
        padded = -(-total // 1024) * 1024
        small = jnp.concatenate(pieces + [jnp.zeros((padded - total,), bf16)])
        small_all = ring.gather_small(small, me)
        cuts = np.cumsum([0] + sizes)
        found = [small_all[:, cuts[i] : cuts[i + 1]] for i in range(len(sizes))]
        gains_f = (
            found[0].reshape(devices, 2, rows_dev).transpose(1, 0, 2).reshape(2, width).astype(f32)
        )
        bias_all = (
            found[1].reshape(devices, 3, heads_t, hd_dev).transpose(1, 2, 0, 3)
            .reshape(3, 2, half_cols)
        )
        bias = lax.dynamic_index_in_dim(bias_all, core, 1, keepdims=False).astype(f32)
        router_w = found[2].reshape(width, experts)
        gate_vec = found[3].reshape(width)
        ids_all = found[4].reshape(devices, top_count, length).astype(jnp.int32)
        prefix_all = found[5].reshape(devices).astype(jnp.int32)
        prefix_pair = jnp.stack([prefix_all[me], prefix_all[me ^ 1]])

        def cost(flops, moved):
            return pl.CostEstimate(flops=flops, bytes_accessed=moved, transcendentals=0)

        depth = 2 * rows_dev

        def by_core(own, other, axis):
            return jnp.where(
                core == 0,
                jnp.concatenate([own, other], axis=axis),
                jnp.concatenate([other, own], axis=axis),
            )

        def halves(array, axis):
            size = array.shape[axis] // 2
            own = lax.dynamic_slice_in_dim(array, core * size, size, axis)
            return own, lax.dynamic_slice_in_dim(array, (1 - core) * size, size, axis)

        qkv_own, qkv_other = halves(qkv_weight.transpose(1, 0, 2), 2)
        out_own, out_other = halves(out_weight, 0)
        own = jnp.concatenate([qkv_own, out_own.T[None]], axis=0)
        other = jnp.concatenate([qkv_other, out_other.T[None]], axis=0)
        block = by_core(own, ring.swap_core(other), 1).reshape(4 * depth, half_cols)
        found = ring.gather(block)
        attn_w = [piece for offset in ring.offsets for piece in found[offset]]

        half_length = length // 2
        steps = chips // 2
        up_zero = lax.dynamic_slice_in_dim(cotangent, half * half_length, half_length, 0)
        up_cross = {0: [swap_tensor(up_zero)]}
        up_ring = {0: [up_zero], 1: ring.step(after(up_zero, attn_w[-3]), None)}

        units = shared_out.shape[0]
        unit_chip = units // chips
        sh_send = jnp.concatenate(
            [
                shared_in.transpose(1, 2, 0).reshape(2, chips, unit_chip, rows_dev),
                shared_out.reshape(1, chips, unit_chip, rows_dev),
            ],
            axis=0,
        ).transpose(1, 0, 2, 3)
        sh_send = after(sh_send.reshape(chips, 3 * unit_chip, rows_dev), attn_w[-3])
        same_core = [[2 * i + c for i in range(chips)] for c in range(2)]
        sh_mine = lax.all_to_all(
            sh_send, "expert", split_axis=0, concat_axis=0, tiled=True, axis_index_groups=same_core
        )
        inputs = tokens_in.astype(f32)
        first_b = rms_norm(inputs, gains_f[0]).astype(bf16)
        first_o = ring.swap_core(first_b)
        cosine, sine = rotary_tables(length, head_size)
        pair_cols = jax.ShapeDtypeStruct((2 * length, half_cols), bf16)
        chip_arg = chip_of.astype(jnp.int32)

        query, key, value, mixed = pl.pallas_call(
            functools.partial(attend_kernel, chips + 1, heads, score_scale),
            out_shape=[pair_cols] * 4,
            in_specs=[in_smem] * 2 + [in_vmem] * 5 + [in_any] * (chips + 1),
            out_specs=[in_vmem] * 4,
            scratch_shapes=[
                pltpu.VMEM((3, width, half_cols), bf16),
                pltpu.SemaphoreType.DMA((3 * chips,)),
            ],
            compiler_params=params(),
            cost_estimate=cost(2 * 2 * length * width * 3 * half_cols, 12 * 1024 * 1024),
            name="attend",
        )(chip_arg, prefix_pair, first_b, first_o, bias.reshape(1, -1), cosine, sine, *attn_w)
        attn_own, attn_give = pl.pallas_call(
            functools.partial(project_kernel, chips + 1),
            out_shape=[
                jax.ShapeDtypeStruct((length, width), f32),
                jax.ShapeDtypeStruct((length, width), bf16),
            ],
            in_specs=[in_smem, in_vmem] + [in_any] * (chips + 1),
            out_specs=[in_vmem] * 2,
            scratch_shapes=[
                pltpu.VMEM((1, width, half_cols), bf16),
                pltpu.SemaphoreType.DMA((chips,)),
            ],
            compiler_params=params(),
            cost_estimate=cost(2 * 2 * length * width * half_cols, 6 * 1024 * 1024),
            name="project",
        )(chip_arg, mixed, *attn_w)
        attn_own = (attn_own + ring.swap_core(attn_give).astype(f32)).astype(bf16)
        attn_got = swap_tensor(attn_own)
        attn_out = attn_own.astype(f32) + attn_got.astype(f32)
        residual = inputs + attn_out
        second_b = rms_norm(residual, gains_f[1]).astype(bf16)

        logits = mm(second_b, router_w)
        expert_range = jnp.arange(experts, dtype=jnp.int32)
        route_match = expert_ids[:, :, None] == expert_range[None, None, :]
        chosen = jnp.sum(jnp.where(route_match, logits[:, None, :], 0.0), axis=-1)
        gate_weights = jax.nn.softmax(chosen, axis=-1)
        shared_sigma = jax.nn.sigmoid(
            jnp.sum(second_b.astype(f32) * gate_vec.astype(f32)[None], axis=-1)
        )
        gate_dense = jnp.sum(jnp.where(route_match, gate_weights[:, :, None], 0.0), axis=1)
        gate_send = jnp.stack(
            [gate_dense.T, jnp.broadcast_to(shared_sigma[None], (experts, length))], axis=1
        )
        gate_all = lax.all_to_all(gate_send, "expert", split_axis=0, concat_axis=0, tiled=True)
        gate_all = gate_all[seq_of].reshape(chips, 2, 2, length)

        match = jnp.any(ids_all[seq_of] == me, axis=1)
        triangle = jnp.asarray(np.triu(np.ones((length, length), np.float32)), bf16)
        rank = jnp.where(match, mm(match.astype(bf16), triangle) - 1.0, no_slot)
        rank = rank.reshape(chips, 2, length)
        blank = jnp.zeros((chips, 3, length), f32)
        row_aux = jnp.concatenate([rank, gate_all[:, :, 0], gate_all[:, :1, 1], blank], axis=1)
        col_aux = jnp.concatenate(
            [rank, gate_all[:, :1, 1], jnp.zeros((chips, 5, length), f32)], axis=1
        ).transpose(0, 2, 1)

        ex_in = expert_in[0].transpose(1, 2, 0)
        ex_out = expert_out[0]
        part_units = ex_out.shape[0]
        sizes = (length, width, capacity, part_units, unit_chip)
        half_arg = half.astype(jnp.int32).reshape(1)
        core_arg = core.astype(jnp.int32).reshape(1)
        swap_core = ring.swap_core

        def each(function, items):
            return [function(item) for item in items]

        second_b, up_ring[1], sh_mine = hold(second_b, up_ring[1], sh_mine)
        rows_ring = {0: [second_b]}
        up_ring_o = {0: each(swap_core, up_ring[0])}
        up_cross_o = {}
        kept = None
        moe, back, moe_o, back_o, dot_rows = {}, {}, {}, {}, []
        sh_w = None
        for k in range(1, steps + 2):
            last = k == steps + 1
            now = []
            if not last:
                rows_ring[k] = ring.step(*rows_ring[k - 1], last=k == steps)
                now.append(rows_ring[k])
                if k < steps:
                    up_ring[k + 1] = ring.step(*up_ring[k], last=k + 1 == steps)
                    now.append(up_ring[k + 1])
                up_cross[k] = each(swap_tensor, up_ring[k])
                up_ring_o[k] = each(swap_core, up_ring[k])
                now += [up_cross[k], up_ring_o[k]]
            g = k - 1
            rows_o = each(swap_core, rows_ring[g])
            up_cross_o[g] = each(swap_core, up_cross[g])
            if sh_w is None:
                sh_w = pl.pallas_call(
                    spread_kernel,
                    out_shape=jax.ShapeDtypeStruct((3, unit_chip, width), bf16),
                    in_specs=[in_smem, in_vmem, in_vmem],
                    out_specs=in_vmem,
                    compiler_params=params(),
                    cost_estimate=cost(0, 16 * 1024 * 1024),
                    name="spread",
                )(core_arg, sh_mine, swap_core(sh_mine))

            def in_place(pieces, crossed):
                found = []
                for chip in [pieces] if g == steps else [[p] for p in pieces]:
                    at = 0
                    found.append([])
                    for piece in chip:
                        first = (at, at) if crossed is None else (at, half_length + at)
                        if crossed:
                            first = first[::-1]
                        found[-1].append((piece, *first))
                        at += piece.shape[0]
                return found

            def joined(straight, crossed):
                both = zip(in_place(straight, False), in_place(crossed, True), strict=True)
                return [a + b for a, b in both]

            index = 0 if g == 0 else 2 * g - 1
            offsets = ring.offsets[index : index + (1 if g in (0, steps) else 2)]
            pieces = (
                in_place(rows_ring[g], None)
                + in_place(rows_o, None)
                + joined(up_ring[g], up_cross[g])
                + joined(up_ring_o[g], up_cross_o[g])
            )
            kept, blocks, rows = moe_call(
                index,
                len(offsets),
                sizes,
                chips,
                pieces,
                half_arg,
                row_aux,
                col_aux,
                (ex_in, ex_out, sh_w),
                kept,
            )
            dot_rows.append(rows)
            if not last:
                *_, dot_rows[-1] = held = hold(*now, rows)
                rows_ring[k] = held[0]
                if k < steps:
                    up_ring[k + 1] = held[1]
                up_cross[k], up_ring_o[k] = held[-3:-1]
            for o, (moe_own, moe_give, back_own, back_give) in zip(offsets, blocks, strict=True):
                moe[o], back[o] = moe_own, back_own
                back_o[o] = swap_core(back_give)
                moe_o[o] = swap_core(moe_give)

        rows_all, slots_all, hidden_all, gu_all, tok_all, y_all, s_hidden_all, s_gu_all = kept
        slot_count = chips * 2 * capacity

        def crossing(o):
            mine = moe[o].astype(f32) + moe_o[o].astype(f32)
            return swap_tensor(mine[half_length:].astype(bf16))

        def moe_terms(o):
            return [moe[o][:half_length], moe_o[o][:half_length], moe_cross[o]]

        far = ring.offsets[-1]
        moe_cross = {}
        sending = ring.reduce_first([back[far], back_o[far]])
        moe_cross[far] = crossing(far)
        sending, moe_cross[far] = hold(sending, moe_cross[far])
        for k in range(steps - 1, 0, -1):
            send = ring.reduce_terms(
                [back[k], back_o[k]], [back[-k], back_o[-k]], sending, k == steps - 1
            )
            number = steps - 1 - k
            if number == 0:
                gu_all, *send = hold(gu_all, *send)
                expert_in_grad = mm(gu_all, rows_all, 1, 0).transpose(2, 0, 1)[None]
                token = expert_in_grad[:, :1, :1, :1]
            elif number == 1:
                s_hidden_all, *send = hold(s_hidden_all, *send)
                sh_grad = pl.pallas_call(
                    shared_grad_kernel,
                    grid=(chips,),
                    out_shape=jax.ShapeDtypeStruct((2, chips, 3 * unit_chip, rows_dev), bf16),
                    in_specs=[
                        pl.BlockSpec((chips * length, depth), lambda n: (0, n)),
                        pl.BlockSpec((chips * length, depth), lambda n: (0, n)),
                        pl.BlockSpec((chips * length, unit_chip), lambda n: (0, 0)),
                        pl.BlockSpec((2, chips * length, unit_chip), lambda n: (0, 0, 0)),
                    ],
                    out_specs=pl.BlockSpec((2, 1, 3 * unit_chip, rows_dev), lambda n: (0, n, 0, 0)),
                    compiler_params=params(),
                    cost_estimate=cost(
                        2 * chips * length * width * 3 * unit_chip, 26 * 1024 * 1024
                    ),
                    name="shared_grad",
                )(tok_all, y_all, s_hidden_all, s_gu_all)
                token = sh_grad[:, :1, :1, :1]
            elif number == 2:
                hidden_all, *send = hold(hidden_all, *send)
                expert_out_grad = mm(hidden_all, slots_all, 0, 0)[None]
                token = expert_out_grad[:, :1, :1]
            sending = ring.send_pair(*send)
            moe_cross[k], moe_cross[-k] = crossing(k), crossing(-k)
            sending, moe_cross[k], moe_cross[-k], token = hold(
                sending, moe_cross[k], moe_cross[-k], token
            )
        second_part = ring.add_up([back[0], back_o[0], *sending]).astype(bf16)
        moe_cross[0] = crossing(0)
        second_got = swap_tensor(second_part)
        sending = ring.reduce_first(moe_terms(far))
        second_got, moe_cross[0], sending = hold(second_got, moe_cross[0], sending)

        dots = jnp.concatenate(dot_rows, axis=0)
        sdots = jnp.concatenate([dots[:, 2:3], jnp.zeros_like(dots[:, 2:3])], axis=1)
        dot_send = jnp.stack([dots[:, :2], sdots], axis=2).reshape(devices, 2, length)[seq_inv]
        dot_got = lax.all_to_all(dot_send, "expert", split_axis=0, concat_axis=0, tiled=True)
        dot_got = jnp.concatenate([dot_got[:, 0], jnp.sum(dot_got[:, 1], axis=0)[None]], axis=0)
        dot_got = dot_got + swap_tensor(dot_got)
        gate_grad_dense, sigma_grad = dot_got[:experts].T, dot_got[experts]
        row_term = jnp.sum(gate_dense * gate_grad_dense, axis=-1, keepdims=True)
        logit_grad = (gate_dense * (gate_grad_dense - row_term)).astype(bf16)
        gate_logit_grad = sigma_grad * shared_sigma * (1.0 - shared_sigma)

        second_grad = second_part.astype(f32) + second_got.astype(f32)
        second_grad = second_grad + mm(logit_grad, router_w, 1, 1)
        second_grad = second_grad + gate_logit_grad[:, None] * gate_vec.astype(f32)[None]
        upstream = cotangent.astype(f32)
        residual_norm_grad, gain_two_grad = jax.vjp(rms_norm, residual, gains_f[1])[1](second_grad)
        residual_grad = upstream + residual_norm_grad
        attn_grad = residual_grad.astype(bf16)
        attn_grad_o = ring.swap_core(attn_grad)

        for k in range(steps - 1, 0, -1):
            send = ring.reduce_terms(moe_terms(k), moe_terms(-k), sending, k == steps - 1)
            sending = ring.send_pair(*send)
        moe_half = ring.add_up([*moe_terms(0), *sending])
        res_half = lax.dynamic_slice_in_dim(residual, half * half_length, half_length, 0)
        out_half = (res_half + moe_half).astype(bf16)
        out_got = swap_tensor(out_half)
        output = jnp.where(
            half == 0,
            jnp.concatenate([out_half, out_got], axis=0),
            jnp.concatenate([out_got, out_half], axis=0),
        )

        def by_chip(left, other, right):
            pair = jnp.concatenate([left, other], axis=0)
            return {
                offset: [
                    mm(lax.dynamic_slice_in_dim(pair, chip_of[i] * depth, depth, 1), right, 0, 0)
                ]
                for i, offset in enumerate(ring.offsets)
            }

        proj_grad, bias_grad = pl.pallas_call(
            functools.partial(attend_back_kernel, chips + 1, heads, score_scale),
            out_shape=[
                jax.ShapeDtypeStruct((2 * length, 3 * half_cols), bf16),
                jax.ShapeDtypeStruct((1, 3 * half_cols), f32),
            ],
            in_specs=[in_smem] * 2 + [in_vmem] * 7 + [in_any] * (chips + 1),
            out_specs=[in_vmem] * 2,
            scratch_shapes=[
                pltpu.VMEM((1, width, half_cols), bf16),
                pltpu.SemaphoreType.DMA((chips,)),
            ],
            compiler_params=params(),
            cost_estimate=cost(2 * 2 * length * width * half_cols * 2, 8 * 1024 * 1024),
            name="attend_back",
        )(
            chip_arg,
            prefix_pair,
            attn_grad,
            attn_grad_o,
            query,
            key,
            value,
            cosine,
            sine,
            *attn_w,
        )
        qkv_grad = ring.reduce(by_chip(first_b, first_o, proj_grad))
        out_grad = ring.reduce(by_chip(attn_grad, attn_grad_o, mixed))
        bias_grad = bias_grad[0]
        first_own, first_give = pl.pallas_call(
            functools.partial(project_back_kernel, chips + 1),
            out_shape=[
                jax.ShapeDtypeStruct((length, width), f32),
                jax.ShapeDtypeStruct((length, width), bf16),
            ],
            in_specs=[in_smem, in_vmem] + [in_any] * (chips + 1),
            out_specs=[in_vmem] * 2,
            scratch_shapes=[
                pltpu.VMEM((3, width, half_cols), bf16),
                pltpu.SemaphoreType.DMA((3 * chips,)),
            ],
            compiler_params=params(),
            cost_estimate=cost(2 * 2 * length * width * 3 * half_cols, 12 * 1024 * 1024),
            name="project_back",
        )(chip_arg, proj_grad, *attn_w)
        first_grad = sum_tensor(first_own + ring.swap_core(first_give).astype(f32))
        input_norm_grad, gain_one_grad = jax.vjp(rms_norm, inputs, gains_f[0])[1](first_grad)
        input_grad = (residual_grad + input_norm_grad).astype(bf16)

        def regroup(grad, parts):
            own, other = halves(grad, 0)
            own = own.astype(bf16).reshape(rows_dev, parts, half_cols)
            got = ring.swap_core(other.astype(bf16)).reshape(rows_dev, parts, half_cols)
            return by_core(own, got, 2).astype(f32)

        qkv_weight_grad = regroup(qkv_grad, 3)
        out_weight_grad = regroup(out_grad, 1)[:, 0].T

        own, other = halves(sh_grad, 0)
        sh_sum = (own.astype(f32) + ring.swap_core(other).astype(f32)).astype(bf16)[0]
        sh_back = lax.all_to_all(
            sh_sum, "expert", split_axis=0, concat_axis=0, tiled=True, axis_index_groups=same_core
        )
        sh_back = sh_back.reshape(chips, 3, unit_chip, rows_dev).astype(f32)
        shared_in_grad = sh_back[:, :2].transpose(3, 1, 0, 2).reshape(rows_dev, 2, units)
        shared_out_grad = sh_back[:, 2].reshape(units, rows_dev)

        second_f = second_b.astype(f32)
        router_part = mm(second_b, logit_grad, 0, 0)
        shared_gate_part = jnp.sum(gate_logit_grad[:, None] * second_f, axis=0)
        early = jnp.concatenate(
            [router_part, shared_gate_part[:, None], gain_two_grad[:, None]], axis=1
        ).reshape(devices, rows_dev * (experts + 2))
        early = lax.all_to_all(early, "expert", split_axis=0, concat_axis=0, tiled=True)
        early = jnp.sum(early, axis=0).reshape(rows_dev, experts + 2)
        router_grad, shared_gate_grad = early[:, :experts], early[:, experts]
        bias_send = bias_grad.reshape(3 * heads, devices, hd_dev).transpose(1, 0, 2)
        late = jnp.concatenate(
            [gain_one_grad.reshape(devices, rows_dev), bias_send.reshape(devices, -1)], axis=1
        )
        late = lax.all_to_all(late, "expert", split_axis=0, concat_axis=0, tiled=True)
        gain_one = jnp.sum(late[:, :rows_dev], axis=0)
        bias_got = jnp.sum(late[:, rows_dev:].reshape(chips, 2, 3, heads, hd_dev), axis=0)
        qkv_bias_grad = bias_got.transpose(1, 0, 2, 3).reshape(3, heads_t, hd_dev)
        gains_grad = jnp.stack([gain_one, early[:, experts + 1]], axis=0)

        return (
            output,
            input_grad,
            gains_grad,
            qkv_weight_grad,
            qkv_bias_grad,
            out_weight_grad,
            router_grad,
            shared_gate_grad,
            shared_in_grad,
            shared_out_grad,
            expert_in_grad,
            expert_out_grad,
        )

    return local


def solution(mesh):
    ring = Ring(mesh.shape["expert"])
    return jax.shard_map(
        make_local(ring),
        mesh=mesh,
        in_specs=(
            P("expert", None),
            P("expert", None),
            P(None, "expert"),
            P("expert", None, "tensor"),
            P(None, "tensor", "expert"),
            P("tensor", "expert"),
            P("expert", None),
            P("expert"),
            P("expert", None, "tensor"),
            P("tensor", "expert"),
            P("expert", None, None, "tensor"),
            P("expert", "tensor", None),
            P("expert", None),
            P("expert"),
        ),
        out_specs=(
            P("expert", None),
            P("expert", None),
            P(None, "expert"),
            P("expert", None, "tensor"),
            P(None, "tensor", "expert"),
            P("tensor", "expert"),
            P("expert", None),
            P("expert"),
            P("expert", None, "tensor"),
            P("tensor", "expert"),
            P("expert", None, None, "tensor"),
            P("expert", "tensor", None),
        ),
        check_vma=False,
    )
```

```python
import functools

import jax
import jax.numpy as jnp
import numpy as np
from jax import lax
from jax.experimental import pallas as pl
from jax.experimental.pallas import tpu as pltpu
from jax.sharding import PartitionSpec as P

eps = 1e-06
theta_base = 1000000.0
neg_large = -1e30
no_slot = -100000.0
bf16 = jnp.bfloat16
f32 = jnp.float32
in_vmem = pl.BlockSpec(memory_space=pltpu.VMEM)
in_smem = pl.BlockSpec(memory_space=pltpu.SMEM)
in_any = pl.BlockSpec(memory_space=pl.ANY)


def rms_norm(values, gain_row):
    factor = lax.rsqrt(jnp.mean(values * values, axis=-1, keepdims=True) + eps)
    return values * factor * gain_row


def rotary_tables(length, head_size):
    half_size = head_size // 2
    frequency = np.float32(theta_base) ** (
        -(np.arange(half_size, dtype=np.float32) * np.float32(2.0)) / np.float32(head_size)
    )
    angles = np.arange(length, dtype=np.float32)[:, None] * frequency[None, :].astype(np.float32)
    cosine = np.concatenate([np.cos(angles), np.cos(angles)], axis=-1)
    sine = np.concatenate([-np.sin(angles), np.sin(angles)], axis=-1)
    return jnp.asarray(cosine, f32), jnp.asarray(sine, f32)


def chip_ring(chips):
    columns = chips // 4
    if chips % 4 or columns < 2 or columns % 2:
        return list(range(chips))
    walk = [(0, 0)]
    for column in range(columns):
        rows = range(1, 4) if column % 2 == 0 else range(3, 0, -1)
        walk += [(row, column) for row in rows]
    walk += [(0, column) for column in range(columns - 1, 0, -1)]
    return [row * columns + column for row, column in walk]


def mm(left, right, contract_left=1, contract_right=0):
    return lax.dot_general(
        left,
        right,
        (((contract_left,), (contract_right,)), ((), ())),
        preferred_element_type=f32,
    )


def nt(left, right):
    return mm(left, right, 1, 1)


def tiles(total, size):
    return [(lo, min(size, total - lo)) for lo in range(0, total, size)]


def params(mebibytes=56):
    return pltpu.CompilerParams(vmem_limit_bytes=mebibytes * 1024 * 1024)


def half_turn(values):
    return pltpu.roll(values, values.shape[1] // 2, 1)


def masked(scores, prefix_cut):
    length = scores.shape[0]
    row = lax.broadcasted_iota(jnp.int32, (length, length), 0)
    col = lax.broadcasted_iota(jnp.int32, (length, length), 1)
    return jnp.where((col <= row) | (col < prefix_cut), scores, neg_large)


def softmax_rows(scores):
    weights = jnp.exp(scores - jnp.max(scores, axis=-1, keepdims=True))
    return weights / jnp.sum(weights, axis=-1, keepdims=True)


def load_blocks(chip_ref, blocks, scratch, sem, first, last):
    whole = len(blocks) - 2
    depth = blocks[0].shape[0] // 4
    copies = []
    for i in range(whole + 1):
        start = pl.multiple_of(chip_ref[i] * depth, depth)
        for c in range(first, last):
            block, at = (blocks[i], c) if i < whole else (blocks[whole + c // 2], c % 2)
            copies.append(
                pltpu.make_async_copy(
                    block.at[pl.ds(at * depth, depth)],
                    scratch.at[c - first, pl.ds(start, depth)],
                    sem.at[len(copies)],
                )
            )
    for copy in copies:
        copy.start()
    return copies


def attend_kernel(count, heads, scale, *refs):
    chip_ref, prefix_ref, own, other, bias, cosine, sine = refs[:7]
    blocks = refs[7 : 7 + count]
    query, key, value, mixed, weight, sem = refs[7 + count :]
    copies = load_blocks(chip_ref, blocks, weight, sem, 0, 3)
    length, head_size = cosine.shape
    columns = heads * head_size
    for copy in copies:
        copy.wait()
    for c, out in enumerate((query, key, value)):
        for b, rows in enumerate((own, other)):
            for lo, size in tiles(columns, 2 * head_size):
                part = mm(rows[...], weight[c, :, lo : lo + size])
                part = part + bias[:, c * columns + lo : c * columns + lo + size]
                for at in range(0, size, head_size):
                    one = part[:, at : at + head_size]
                    if c < 2:
                        one = one * cosine[...] + half_turn(one) * sine[...]
                    out[b * length : (b + 1) * length, lo + at : lo + at + head_size] = one.astype(
                        bf16
                    )
    for b in range(2):
        rows = slice(b * length, (b + 1) * length)
        for h in range(heads):
            cols = slice(h * head_size, (h + 1) * head_size)
            scores = masked(nt(query[rows, cols], key[rows, cols]) * scale, prefix_ref[b])
            probs = softmax_rows(scores).astype(bf16)
            mixed[rows, cols] = mm(probs, value[rows, cols]).astype(bf16)


def project_kernel(count, *refs):
    chip_ref, mixed = refs[:2]
    blocks = refs[2 : 2 + count]
    own, other, weight, sem = refs[2 + count :]
    copies = load_blocks(chip_ref, blocks, weight, sem, 3, 4)
    for copy in copies:
        copy.wait()
    length, width = own.shape
    for lo, size in tiles(width, 512):
        part = nt(mixed[...], weight[0, lo : lo + size, :])
        own[:, lo : lo + size] = part[:length].astype(own.dtype)
        other[:, lo : lo + size] = part[length:].astype(other.dtype)


def attend_back_kernel(count, heads, scale, *refs):
    chip_ref, prefix_ref, own, other, query, key, value, cosine, sine = refs[:9]
    blocks = refs[9 : 9 + count]
    grad, bias, weight, sem = refs[9 + count :]
    copies = load_blocks(chip_ref, blocks, weight, sem, 3, 4)
    length, head_size = cosine.shape
    columns = heads * head_size
    for copy in copies:
        copy.wait()
    for b, up in enumerate((own, other)):
        rows = slice(b * length, (b + 1) * length)
        mixed_grad = mm(up[...], weight[0]).astype(bf16)
        for h in range(heads):
            cols = slice(h * head_size, (h + 1) * head_size)
            q, k, v = query[rows, cols], key[rows, cols], value[rows, cols]
            up_head = mixed_grad[:, cols]
            probs = softmax_rows(masked(nt(q, k) * scale, prefix_ref[b]))
            prob_grad = nt(up_head, v)
            row_term = jnp.sum(probs * prob_grad, axis=-1, keepdims=True)
            score_grad = (probs * (prob_grad - row_term)).astype(bf16)
            q_grad = mm(score_grad, k) * scale
            k_grad = mm(score_grad, q, 0, 0) * scale
            v_grad = mm(probs.astype(bf16), up_head, 0, 0)
            for c, one in enumerate((q_grad, k_grad, v_grad)):
                if c < 2:
                    one = one * cosine[...] - half_turn(one) * sine[...]
                one = one.astype(bf16)
                at = slice(c * columns + h * head_size, c * columns + (h + 1) * head_size)
                grad[rows, at] = one
                column_sum = jnp.sum(one.astype(f32), axis=0, keepdims=True)
                bias[:, at] = column_sum if b == 0 else bias[:, at] + column_sum


def project_back_kernel(count, *refs):
    chip_ref, grad = refs[:2]
    blocks = refs[2 : 2 + count]
    own, other, weight, sem = refs[2 + count :]
    copies = load_blocks(chip_ref, blocks, weight, sem, 0, 3)
    for copy in copies:
        copy.wait()
    length, width = own.shape
    columns = grad.shape[1] // 3
    for lo, size in tiles(width, 512):
        part = nt(grad[:, :columns], weight[0, lo : lo + size, :])
        for c in range(1, 3):
            part = part + nt(grad[:, c * columns : (c + 1) * columns], weight[c, lo : lo + size, :])
        own[:, lo : lo + size] = part[:length].astype(own.dtype)
        other[:, lo : lo + size] = part[length:].astype(other.dtype)


def moe_kernel(index, span, first, plan, sizes, *refs):
    length, width, capacity, units, shared_units, experts, top_count = sizes
    count = sum(len(p) for p in plan)
    own_rows, slab = span * length, 2 * span * capacity
    half_ref, row_hbm, col_hbm, router_hbm = refs[:4]
    given = refs[4 : 4 + count]
    in_hbm, out_hbm, shared_hbm = refs[4 + count : 7 + count]
    rest = refs[7 + count + (0 if first else 8) :]
    kept, owns, give, dots = rest[:8], rest[8 : 8 + span], rest[8 + span], rest[9 + span]
    tok, up, rows, up_rows, slots, hidden, gu, y_grad, s_hidden, s_gu, made_out = rest[
        10 + span : 21 + span
    ]
    w_in, w_out, w_sh, row_ref, col_ref, router = rest[21 + span : 27 + span]
    load_sem, weight_sem, out_sem, keep_sem = rest[27 + span :]
    wide = min(512, width)
    columns = tiles(width, wide)

    tables = [
        pltpu.make_async_copy(a, b, weight_sem.at[3 + i])
        for i, (a, b) in enumerate(
            (
                (row_hbm.at[pl.ds(index, span)], row_ref),
                (col_hbm.at[pl.ds(index, span)], col_ref),
                (router_hbm, router),
            )
        )
    ]
    for copy in tables:
        copy.start()

    loads = []
    for n, (lo, size_cols) in enumerate(columns):
        cols, number = slice(lo, lo + size_cols), 0
        loads.append([])
        for which, pieces in enumerate(plan):
            target, at = (tok, up)[which // (2 * span)], which % (2 * span) * length
            for first_row, size, start_zero, start_one in pieces:
                start = start_zero + half_ref[0] * (start_one - start_zero)
                start = pl.multiple_of(start + at, 16)
                copy = pltpu.make_async_copy(
                    given[number].at[first_row : first_row + size, cols],
                    target.at[pl.ds(start, size), cols],
                    load_sem.at[n, number],
                )
                copy.start()
                loads[-1].append(copy)
                number += 1

    weights = [
        pltpu.make_async_copy(a, b, weight_sem.at[i])
        for i, (a, b) in enumerate(
            (
                (shared_hbm, w_sh),
                (in_hbm, w_in),
                (out_hbm, w_out),
            )
        )
    ]
    for copy in weights:
        copy.start()
    for copy in tables:
        copy.wait()

    def keep(slot, source):
        target = kept[slot]
        size = source.shape[-2]
        first_row = index * (size // span)
        if len(target.shape) == 3:
            target = target.at[:, pl.ds(first_row, size)]
        else:
            target = target.at[pl.ds(first_row, size)]
        copy = pltpu.make_async_copy(source, target, keep_sem.at[slot])
        copy.start()
        return copy

    slot = lax.broadcasted_iota(jnp.int32, (capacity, length), 0).astype(f32)
    lane = lax.broadcasted_iota(jnp.int32, (length, 2 * capacity), 1).astype(f32)
    picks, ones, places = [], [], []
    for j in range(span):
        place = []
        for c in range(2):
            pick = slot == row_ref[j, c : c + 1, :]
            picks.append(pick)
            ones.append(jnp.where(pick, 1.0, 0.0).astype(bf16))
            rank = col_ref[j, :, c : c + 1] + float(c * capacity)
            place.append(jnp.where(lane == rank, 1.0, 0.0))
        places.append(jnp.concatenate(place, axis=0))

    logits = jnp.zeros((2 * own_rows, router.shape[1]), f32)
    for n, (lo, size) in enumerate(columns):
        cols = slice(lo, lo + size)
        for copy in loads[n]:
            copy.wait()
        logits = logits + mm(tok[:, cols], router[cols, :])
        for j in range(span):
            for c in range(2):
                source = slice((c * span + j) * length, (c * span + j + 1) * length)
                target = slice((2 * j + c) * capacity, (2 * j + c + 1) * capacity)
                rows[target, cols] = mm(ones[2 * j + c], tok[source, cols]).astype(bf16)
                up_rows[target, cols] = mm(ones[2 * j + c], up[source, cols]).astype(bf16)

    expert = lax.broadcasted_iota(jnp.int32, (length, router.shape[1]), 1).astype(f32)
    mine = expert == half_ref[1].astype(f32)
    row = lax.broadcasted_iota(jnp.int32, (2 * capacity, 2 * capacity), 0)
    col = lax.broadcasted_iota(jnp.int32, (2 * capacity, 2 * capacity), 1)
    gates, sigmas = [], []
    for j in range(span):
        taken = []
        for c in range(2):
            part = logits[(c * span + j) * length : (c * span + j + 1) * length]
            first_id = 2 + c * top_count
            chosen = expert == col_ref[j, :, first_id : first_id + 1]
            for k in range(first_id + 1, first_id + top_count):
                chosen = chosen | (expert == col_ref[j, :, k : k + 1])
            peak = jnp.max(jnp.where(chosen, part, neg_large), axis=1, keepdims=True)
            weight = jnp.where(chosen, jnp.exp(part - peak), 0.0)
            weight = weight / jnp.sum(weight, axis=1, keepdims=True)
            taken.append(jnp.sum(jnp.where(mine, weight, 0.0), axis=1, keepdims=True))
            if c == 0:
                gate = expert == float(experts)
                gate = jnp.sum(jnp.where(gate, part, 0.0), axis=1, keepdims=True)
                sigmas.append(1.0 / (1.0 + jnp.exp(-gate)))
        slot_gates = jnp.sum(places[j] * jnp.concatenate(taken, axis=0), axis=0, keepdims=True)
        gates.append(jnp.sum(jnp.where(row == col, slot_gates, 0.0), axis=1, keepdims=True))
        places[j] = places[j].astype(bf16)
    gate_all = jnp.concatenate(gates, axis=0)
    sigma_all = jnp.concatenate(sigmas, axis=0)
    for lo, size in columns:
        cols = slice(lo, lo + size)
        slots[:, cols] = (gate_all * up_rows[:, cols].astype(f32)).astype(bf16)
        y_grad[:, cols] = (sigma_all * up[0:own_rows, cols].astype(f32)).astype(bf16)

    kept_copies = [keep(4, tok.at[0:own_rows]), keep(0, rows), keep(1, slots), keep(5, y_grad)]

    def gated(gate_part, up_part, grad):
        sig = 1.0 / (1.0 + jnp.exp(-gate_part))
        silu = gate_part * sig
        return (
            (silu * up_part).astype(bf16),
            (grad * up_part * (sig * (1.0 + gate_part * (1.0 - sig)))).astype(bf16),
            (grad * silu).astype(bf16),
        )

    weights[0].wait()
    for lo, size in tiles(shared_units, 256):
        at = slice(lo, lo + size)
        gate_part = nt(tok[0:own_rows, :], w_sh[0, at, :])
        up_part = nt(tok[0:own_rows, :], w_sh[1, at, :])
        grad = nt(y_grad[...], w_sh[2, at, :])
        s_hidden[:, at], s_gu[0, :, at], s_gu[1, :, at] = gated(gate_part, up_part, grad)
    kept_copies += [keep(6, s_hidden), keep(7, s_gu)]
    weights[1].wait()
    weights[2].wait()
    for lo, size in tiles(units, 256):
        at = slice(lo, lo + size)
        gate_part = nt(rows[...], w_in[0, at, :])
        up_part = nt(rows[...], w_in[1, at, :])
        grad = nt(slots[...], w_out[at, :])
        hidden[:, at], gu[0, :, at], gu[1, :, at] = gated(gate_part, up_part, grad)
    kept_copies += [keep(2, hidden), keep(3, gu)]

    slot_dots, sigma_dots = jnp.zeros((slab, 1), f32), jnp.zeros((own_rows, 1), f32)
    sent = []
    for n, (lo, size) in enumerate(columns):
        cols, turn = slice(lo, lo + size), n % 2
        if n >= 2:
            for copy in sent[n - 2]:
                copy.wait()
        made = mm(hidden[...], w_out[:, cols]).astype(bf16).astype(f32)
        slot_dots = slot_dots + jnp.sum(
            up_rows[:, cols].astype(f32) * made, axis=1, keepdims=True
        )
        made = (gate_all * made).astype(bf16)
        shared = mm(s_hidden[...], w_sh[2, :, cols])
        sigma_dots = sigma_dots + jnp.sum(
            up[0:own_rows, cols].astype(f32) * shared, axis=1, keepdims=True
        )
        shared = sigma_all * shared
        entry = (mm(gu[0], w_in[0, :, cols]) + mm(gu[1], w_in[1, :, cols])).astype(bf16)
        shared_back = mm(s_gu[0], w_sh[0, :, cols]) + mm(s_gu[1], w_sh[1, :, cols])
        sent.append([])
        for j in range(span):
            mine = slice(j * length, (j + 1) * length)
            theirs = slice(2 * j * capacity, 2 * (j + 1) * capacity)
            routed = mm(places[j], made[theirs])
            made_out[turn, 4 * j] = (routed[:length] + shared[mine]).astype(bf16)
            made_out[turn, 4 * j + 1] = routed[length:].astype(bf16)
            routed = mm(places[j], entry[theirs])
            made_out[turn, 4 * j + 2] = (routed[:length] + shared_back[mine]).astype(bf16)
            made_out[turn, 4 * j + 3] = routed[length:].astype(bf16)
            middle = length // 2
            for k in range(4):
                target, base = (owns[j], 0) if k % 2 == 0 else (give, 2 * j * length)
                base += (length, 0)[k // 2]
                for m, h in enumerate((half_ref[0], 1 - half_ref[0])):
                    source = made_out.at[
                        turn, 4 * j + k, pl.ds(pl.multiple_of(h * middle, 16), middle)
                    ]
                    at = base + m * middle
                    copy = pltpu.make_async_copy(
                        source, target.at[at : at + middle, cols], out_sem.at[turn, 4 * j + k, m]
                    )
                    copy.start()
                    sent[-1].append(copy)
    row = lax.broadcasted_iota(jnp.int32, (length, length), 0)
    col = lax.broadcasted_iota(jnp.int32, (length, length), 1)
    for j in range(span):
        for c in range(2):
            part = slot_dots[(2 * j + c) * capacity : (2 * j + c + 1) * capacity]
            part = jnp.where(picks[2 * j + c], part, 0.0)
            dots[j, c : c + 1, :] = jnp.sum(part, axis=0, keepdims=True)
        part = jnp.where(row == col, sigma_dots[j * length : (j + 1) * length], 0.0)
        dots[j, 2:3, :] = jnp.sum(part, axis=0, keepdims=True)
        dots[j, 3:, :] = jnp.zeros((dots.shape[1] - 3, length), f32)
    for copy in kept_copies + [copy for group in sent[-2:] for copy in group]:
        copy.wait()


def moe_call(index, span, sizes, chips, pieces, where, row_aux, col_aux, router, weights, kept):
    length, width, capacity, units, shared_units = sizes[:5]
    plan = [[place for _, place in group] for group in pieces]
    arrays = [piece for group in pieces for piece, _ in group]
    first = kept is None
    own_rows, slab = span * length, 2 * span * capacity
    slots, tokens = chips * 2 * capacity, chips * length
    kept_shapes = [
        jax.ShapeDtypeStruct(shape, bf16)
        for shape in (
            (slots, width),
            (slots, width),
            (slots, units),
            (2, slots, units),
            (tokens, width),
            (tokens, width),
            (tokens, shared_units),
            (2, tokens, shared_units),
        )
    ]
    own = jax.ShapeDtypeStruct((2 * length, width), bf16)
    give = jax.ShapeDtypeStruct((2 * own_rows, width), bf16)
    operands = [where, row_aux, col_aux, router, *arrays, *weights]
    operands += [] if first else list(kept)
    aliases = {} if first else {len(operands) - 8 + i: i for i in range(8)}
    flops = 2 * slab * width * units * 6 + 2 * own_rows * width * shared_units * 6
    out = pl.pallas_call(
        functools.partial(moe_kernel, index, span, first, plan, sizes),
        out_shape=kept_shapes
        + [own] * span
        + [give]
        + [jax.ShapeDtypeStruct((span, 8, length), f32)],
        in_specs=[in_smem] + [in_any] * 3
        + [in_any] * (len(arrays) + 3 + (0 if first else 8)),
        out_specs=[in_any] * (9 + span) + [in_vmem],
        scratch_shapes=[
            pltpu.VMEM((2 * own_rows, width), bf16),
            pltpu.VMEM((2 * own_rows, width), bf16),
            pltpu.VMEM((slab, width), bf16),
            pltpu.VMEM((slab, width), bf16),
            pltpu.VMEM((slab, width), bf16),
            pltpu.VMEM((slab, units), bf16),
            pltpu.VMEM((2, slab, units), bf16),
            pltpu.VMEM((own_rows, width), bf16),
            pltpu.VMEM((own_rows, shared_units), bf16),
            pltpu.VMEM((2, own_rows, shared_units), bf16),
            pltpu.VMEM((2, 4 * span, length, min(512, width)), bf16),
            pltpu.VMEM((2, units, width), bf16),
            pltpu.VMEM((units, width), bf16),
            pltpu.VMEM((3, shared_units, width), bf16),
            pltpu.VMEM((span, *row_aux.shape[1:]), f32),
            pltpu.VMEM((span, *col_aux.shape[1:]), f32),
            pltpu.VMEM(router.shape, bf16),
            pltpu.SemaphoreType.DMA((len(tiles(width, min(512, width))), len(arrays))),
            pltpu.SemaphoreType.DMA((6,)),
            pltpu.SemaphoreType.DMA((2, 4 * span, 2)),
            pltpu.SemaphoreType.DMA((8,)),
        ],
        input_output_aliases=aliases,
        compiler_params=params(),
        cost_estimate=pl.CostEstimate(
            flops=flops // 64, bytes_accessed=span * 512 * 1024, transcendentals=0
        ),
        name=f"experts_{index}",
    )(*operands)
    return out[:8], out[8 : 8 + span], out[8 + span], out[9 + span]


def spread_kernel(core_ref, own, other, out):
    parts, units, _ = out.shape
    count, _, rows = own.shape

    def spread(first, second):
        for i in range(count):
            for c in range(parts):
                at = slice(c * units, (c + 1) * units)
                both = jnp.concatenate([first[i, at, :], second[i, at, :]], axis=1)
                out[c, :, 2 * i * rows : 2 * (i + 1) * rows] = both

    @pl.when(core_ref[0] == 0)
    def _():
        spread(own, other)

    @pl.when(core_ref[0] == 1)
    def _():
        spread(other, own)


def shared_grad_kernel(tok, y_grad, hidden, gu, out):
    units = hidden.shape[1]
    rows = out.shape[3]
    for c in range(3):
        left = gu[c] if c < 2 else hidden[...]
        right = tok[...] if c < 2 else y_grad[...]
        part = mm(left, right, 0, 0).astype(bf16)
        for k in range(2):
            out[k, 0, c * units : (c + 1) * units, :] = part[:, k * rows : (k + 1) * rows]


class Ring:
    def __init__(self, devices):
        self.devices = devices
        self.chips = devices // 2
        order = chip_ring(self.chips)
        n = self.chips
        self.next = [
            (order[i] * 2 + c, order[(i + 1) % n] * 2 + c) for i in range(n) for c in range(2)
        ]
        self.prev = [(b, a) for a, b in self.next]
        self.core = [(e, e ^ 1) for e in range(devices)]
        half = n // 2
        offsets = [0]
        for k in range(1, half):
            offsets += [-k, k]
        self.offsets = offsets + [half]
        place = {chip: i for i, chip in enumerate(order)}
        self.chip_table = np.array(
            [
                [order[(place[e // 2] + o) % n] for o in self.offsets]
                for e in range(devices)
            ],
            np.int32,
        )
        self.seq_table = np.stack(
            [
                2 * self.chip_table + (np.arange(devices) % 2)[:, None],
                2 * self.chip_table + 1 - (np.arange(devices) % 2)[:, None],
            ],
            axis=-1,
        ).reshape(devices, devices)
        self.seq_inverse = np.argsort(self.seq_table, axis=1).astype(np.int32)

    def step(self, ahead, back=None, last=False):
        back = ahead if back is None else back
        if last:
            cut = ahead.shape[0] // 2
            ahead, back = ahead[:cut], back[cut:]
        return self.send_pair(ahead, back)

    def send_pair(self, ahead, back):
        return [
            lax.ppermute(ahead, "expert", self.next),
            lax.ppermute(back, "expert", self.prev),
        ]

    def add_up(self, terms):
        out = None
        for term in terms:
            out = term.astype(f32) if out is None else out + term.astype(f32)
        return out

    def reduce_first(self, terms):
        total = self.add_up(terms).astype(bf16)
        return self.step(total, last=True)

    def reduce_terms(self, ahead_terms, back_terms, sending, first):
        mine, yours = self.add_up(ahead_terms), self.add_up(back_terms)
        ahead, back = (part.astype(f32) for part in sending)
        if first:
            cut = ahead.shape[0]
            mine = jnp.concatenate([mine[:cut] + ahead, mine[cut:]], axis=0)
            yours = jnp.concatenate([yours[:cut], yours[cut:] + back], axis=0)
        else:
            mine, yours = mine + ahead, yours + back
        return [mine.astype(bf16), yours.astype(bf16)]

    def reduce(self, terms):
        half = self.chips // 2
        sending = self.reduce_first(terms[half])
        for k in range(half - 1, 0, -1):
            send = self.reduce_terms(terms[k], terms[-k], sending, k == half - 1)
            sending = self.send_pair(*send)
        return self.add_up([*terms[0], *sending])

    def swap_core(self, block):
        return lax.ppermute(block, "expert", self.core)

    def double_small(self, held, me, step):
        pairs = [(e, e ^ step) for e in range(self.devices)]
        other = lax.ppermute(held, "expert", pairs)
        upper = (me // step) % 2 == 1
        return jnp.where(upper, jnp.concatenate([other, held]), jnp.concatenate([held, other]))


def after(value, *others):
    return lax.optimization_barrier((value,) + others)[0]


def after_all(values, *others):
    return lax.optimization_barrier((list(values),) + others)[0]


def hold(*values):
    return list(lax.optimization_barrier(values))


def swap_tensor(block):
    return lax.ppermute(block, "tensor", [(0, 1), (1, 0)])


def sum_tensor(part):
    own = part.astype(bf16)
    return own.astype(f32) + swap_tensor(own).astype(f32)


def make_local(ring):
    devices, chips = ring.devices, ring.chips

    def local(
        tokens_in,
        cotangent,
        norm_gains,
        qkv_weight,
        qkv_bias,
        out_weight,
        router_weight,
        shared_gate,
        shared_in,
        shared_out,
        expert_in,
        expert_out,
        expert_ids,
        prefix_len,
    ):
        me = lax.axis_index("expert")
        core = me % 2
        half = lax.axis_index("tensor")
        length, width = tokens_in.shape
        top_count = expert_ids.shape[1]
        experts = router_weight.shape[1]
        capacity = length * top_count * 3 // (2 * experts)
        rows_dev = qkv_weight.shape[0]
        heads_t = qkv_bias.shape[1]
        heads = heads_t // 2
        hd_dev = qkv_bias.shape[2]
        head_size = hd_dev * devices
        half_cols = heads * head_size
        score_scale = head_size ** (-0.5)
        chip_of = jnp.asarray(ring.chip_table)[me]
        seq_of = jnp.asarray(ring.seq_table)[me]
        seq_inv = jnp.asarray(ring.seq_inverse)[me]

        pieces = [
            norm_gains.reshape(-1),
            qkv_bias.reshape(-1),
            router_weight.reshape(-1),
            shared_gate.reshape(-1),
            expert_ids.T.astype(bf16).reshape(-1),
            prefix_len.astype(bf16).reshape(-1),
        ]
        sizes = [p.shape[0] for p in pieces]
        total = sum(sizes)
        padded = -(-total // 1024) * 1024
        small = jnp.concatenate(pieces + [jnp.zeros((padded - total,), bf16)])
        swap_core = ring.swap_core

        def cost(flops, moved):
            return pl.CostEstimate(
                flops=flops // 64, bytes_accessed=moved // 64, transcendentals=0
            )

        depth = 2 * rows_dev

        def by_core(own, other, axis):
            return jnp.where(
                core == 0,
                jnp.concatenate([own, other], axis=axis),
                jnp.concatenate([other, own], axis=axis),
            )

        def halves(array, axis):
            size = array.shape[axis] // 2
            own = lax.dynamic_slice_in_dim(array, core * size, size, axis)
            return own, lax.dynamic_slice_in_dim(array, (1 - core) * size, size, axis)

        qkv_own, qkv_other = halves(qkv_weight.transpose(1, 0, 2), 2)
        out_own, out_other = halves(out_weight, 0)
        own = jnp.concatenate([qkv_own, out_own.T[None]], axis=0)
        other = jnp.concatenate([qkv_other, out_other.T[None]], axis=0)
        block = by_core(own, ring.swap_core(other), 1).reshape(4 * depth, half_cols)
        half_length = length // 2
        steps = chips // 2
        up_zero = lax.dynamic_slice_in_dim(cotangent, half * half_length, half_length, 0)
        small_all = small[None]
        for k in range(devices.bit_length() - 1):
            small_all = ring.double_small(small_all, me, 1 << k)
        pair = ring.step(block)
        attn_w = [block]
        for k in range(1, steps + 1):
            if k > 1:
                pair = ring.step(*pair, last=k == steps)
            attn_w += pair

        cuts = np.cumsum([0] + sizes)
        found = [small_all[:, cuts[i] : cuts[i + 1]] for i in range(len(sizes))]
        gains_f = (
            found[0].reshape(devices, 2, rows_dev).transpose(1, 0, 2).reshape(2, width).astype(f32)
        )
        bias_all = (
            found[1].reshape(devices, 3, heads_t, hd_dev).transpose(1, 2, 0, 3)
            .reshape(3, 2, half_cols)
        )
        bias = lax.dynamic_index_in_dim(bias_all, core, 1, keepdims=False).astype(f32)
        router_w = found[2].reshape(width, experts)
        gate_vec = found[3].reshape(width)
        ids_all = found[4].reshape(devices, top_count, length).astype(jnp.int32)
        prefix_all = found[5].reshape(devices).astype(jnp.int32)
        prefix_pair = jnp.stack([prefix_all[me], prefix_all[me ^ 1]])


        match = jnp.any(ids_all[seq_of] == me, axis=1)
        triangle = jnp.asarray(np.triu(np.ones((length, length), np.float32)), bf16)
        rank = jnp.where(match, mm(match.astype(bf16), triangle) - 1.0, no_slot)
        rank = rank.reshape(chips, 2, length)
        row_aux = jnp.concatenate([rank, jnp.zeros((chips, 6, length), f32)], axis=1)
        ids_ring = ids_all[seq_of].reshape(chips, 2 * top_count, length).astype(f32)
        blank = jnp.zeros((chips, -(2 + 2 * top_count) % 8, length), f32)
        col_aux = jnp.concatenate([rank, ids_ring, blank], axis=1).transpose(0, 2, 1)
        router_all = jnp.concatenate(
            [
                router_w,
                gate_vec[:, None],
                jnp.zeros((width, -(experts + 1) % 128), bf16),
            ],
            axis=1,
        )

        units = shared_out.shape[0]
        unit_chip = units // chips
        sh_send = jnp.concatenate(
            [
                shared_in.transpose(1, 2, 0).reshape(2, chips, unit_chip, rows_dev),
                shared_out.reshape(1, chips, unit_chip, rows_dev),
            ],
            axis=0,
        ).transpose(1, 0, 2, 3)
        sh_send = sh_send.reshape(chips, 3 * unit_chip, rows_dev)

        up_cross = {0: swap_tensor(up_zero)}
        attn_w[-4:-2], sh_send, up_cross[0] = hold(attn_w[-4:-2], sh_send, up_cross[0])
        up_next = ring.step(after(up_zero, attn_w[-3]))
        same_core = [[2 * i + c for i in range(chips)] for c in range(2)]
        inputs = tokens_in.astype(f32)
        first_b = rms_norm(inputs, gains_f[0]).astype(bf16)
        first_o = ring.swap_core(first_b)
        cosine, sine = rotary_tables(length, head_size)
        pair_cols = jax.ShapeDtypeStruct((2 * length, half_cols), bf16)
        chip_arg = chip_of.astype(jnp.int32)

        query, key, value, mixed = pl.pallas_call(
            functools.partial(attend_kernel, chips + 1, heads, score_scale),
            out_shape=[pair_cols] * 4,
            in_specs=[in_smem] * 2 + [in_vmem] * 5 + [in_any] * (chips + 1),
            out_specs=[in_vmem] * 4,
            scratch_shapes=[
                pltpu.VMEM((3, width, half_cols), bf16),
                pltpu.SemaphoreType.DMA((3 * chips,)),
            ],
            compiler_params=params(),
            cost_estimate=cost(2 * 2 * length * width * 3 * half_cols, 12 * 1024 * 1024),
            name="attend",
        )(chip_arg, prefix_pair, first_b, first_o, bias.reshape(1, -1), cosine, sine, *attn_w)
        mixed, up_next = hold(mixed, up_next)
        sh_mine = lax.all_to_all(
            after(sh_send, up_next[0]), "expert", split_axis=0, concat_axis=0, tiled=True, axis_index_groups=same_core
        )
        attn_own, attn_give = pl.pallas_call(
            functools.partial(project_kernel, chips + 1),
            out_shape=[
                jax.ShapeDtypeStruct((length, width), f32),
                jax.ShapeDtypeStruct((length, width), bf16),
            ],
            in_specs=[in_smem, in_vmem] + [in_any] * (chips + 1),
            out_specs=[in_vmem] * 2,
            scratch_shapes=[
                pltpu.VMEM((1, width, half_cols), bf16),
                pltpu.SemaphoreType.DMA((chips,)),
            ],
            compiler_params=params(),
            cost_estimate=cost(2 * 2 * length * width * half_cols, 6 * 1024 * 1024),
            name="project",
        )(chip_arg, mixed, *attn_w)
        attn_own = (attn_own + ring.swap_core(attn_give).astype(f32)).astype(bf16)
        attn_got = swap_tensor(attn_own)
        attn_out = attn_own.astype(f32) + attn_got.astype(f32)
        residual = inputs + attn_out
        second_b = rms_norm(residual, gains_f[1]).astype(bf16)

        second_b, up_next, sh_mine, row_aux, col_aux, router_all = hold(
            second_b, up_next, sh_mine, row_aux, col_aux, router_all
        )
        pair = {
            0: [
                jnp.concatenate([second_b, up_next[0]], axis=0),
                jnp.concatenate([up_next[1], second_b], axis=0),
            ]
        }
        pair_o = {0: [swap_core(pair[0][0]), swap_core(up_next[1])]}
        up_zero_o = swap_core(up_zero)
        cross_o = {}

        logits = mm(second_b, router_w)
        expert_range = jnp.arange(experts, dtype=jnp.int32)
        route_match = expert_ids[:, :, None] == expert_range[None, None, :]
        chosen = jnp.sum(jnp.where(route_match, logits[:, None, :], 0.0), axis=-1)
        gate_weights = jax.nn.softmax(chosen, axis=-1)
        shared_sigma = jax.nn.sigmoid(
            jnp.sum(second_b.astype(f32) * gate_vec.astype(f32)[None], axis=-1)
        )
        gate_dense = jnp.sum(jnp.where(route_match, gate_weights[:, :, None], 0.0), axis=1)
        ex_in = expert_in[0].transpose(1, 2, 0)
        ex_out = expert_out[0]
        part_units = ex_out.shape[0]
        sizes = (length, width, capacity, part_units, unit_chip, experts, top_count)
        half_arg = jnp.stack([half, me]).astype(jnp.int32)
        core_arg = core.astype(jnp.int32).reshape(1)

        sh_w = pl.pallas_call(
            spread_kernel,
            out_shape=jax.ShapeDtypeStruct((3, unit_chip, width), bf16),
            in_specs=[in_smem, in_vmem, in_vmem],
            out_specs=in_vmem,
            compiler_params=params(),
            cost_estimate=cost(0, 16 * 1024 * 1024),
            name="spread",
        )(core_arg, sh_mine, swap_core(sh_mine))

        def row_pieces(found, own_zero, g):
            full, part = length, length // 2
            if g == 0:
                return [[(own_zero, (0, full, 0, 0))]]
            if g == steps:
                ahead, back = found[g]
                return [[(ahead, (0, part, 0, 0)), (back, (0, part, part, part))]]
            return [[(found[g][0], (0, full, 0, 0))], [(found[g][1], (half_length, full, 0, 0))]]

        def up_pieces(found, own_zero, crossed, g):
            whole, part = half_length, half_length // 2
            if g == 0:
                straight = [[(own_zero, (0, whole, 0, whole))]]
            elif g == steps:
                ahead, back = found[g - 1]
                straight = [
                    [
                        (ahead, (length, part, 0, whole)),
                        (back, (part, part, part, whole + part)),
                    ]
                ]
            else:
                ahead, back = found[g - 1]
                straight = [
                    [(ahead, (length, whole, 0, whole))],
                    [(back, (0, whole, 0, whole))],
                ]
            for j, chip in enumerate(straight):
                chip.append((crossed, (j * whole, whole, whole, 0)))
            return straight

        kept = None
        own_terms, give_terms, dot_rows = {}, {}, []
        terms, crossed = {}, {}

        def receive(g):
            index, count = (0, 1) if g == 0 else (2 * g - 1, 1 if g == steps else 2)
            crossing = []
            for j in range(count):
                own, got, at = own_terms[g][j], give_got[g], 2 * j * length
                parts = []
                for i in range(4):
                    lo, hi = i * half_length, (i + 1) * half_length
                    parts.append([own[lo:hi], got[at + lo : at + hi]])
                terms[ring.offsets[index + j]] = [parts[0], parts[2]]
                crossing.append(ring.add_up(parts[1]).astype(bf16))
                out_gives.setdefault(g, []).append(parts[3])
            return crossing[0] if count == 1 else jnp.concatenate(crossing, axis=0)

        def receive_outs(g):
            parts = [ring.add_up(part).astype(bf16) for part in out_gives[g]]
            return parts[0] if len(parts) == 1 else jnp.concatenate(parts, axis=0)

        def place_crossed(which, g, got):
            index, count = (0, 1) if g == 0 else (2 * g - 1, 1 if g == steps else 2)
            for j in range(count):
                crossed[which, ring.offsets[index + j]] = got[
                    j * half_length : (j + 1) * half_length
                ]

        out_gives, give_got = {}, {}
        for k in range(1, steps + 2):
            g = k - 1
            now = []
            if k <= steps:
                ahead, back = pair[g]
                cut = half_length // 2
                if k == steps:
                    ahead, back = ahead[: length // 2], back[half_length + length // 2 :]
                pair[k] = ring.send_pair(ahead, back)
                first, second = pair[g][0][length:], pair[g][1][:half_length]
                if k == steps:
                    first, second = first[:cut], second[cut:]
                up_cross[k] = swap_tensor(jnp.concatenate([first, second], axis=0))
                now = [pair[k], up_cross[k]]
            if g > 0:
                pair_o[g] = [swap_core(x) for x in pair[g]]
            if g > 0:
                cross_o[g] = swap_core(after(up_cross[g], *pair_o[g]))
            else:
                cross_o[g] = swap_core(up_cross[g])
            if g >= 1:
                give_got[g - 1] = swap_core(after(give_terms[g - 1], cross_o[g]))
                now.append(give_got[g - 1])
            if g >= 2:
                grads = receive(g - 2)
                grads, pair_o[g] = hold(grads, pair_o[g])
                now.append(swap_tensor(grads))
            pieces = (
                row_pieces(pair, second_b, g)
                + row_pieces(pair_o, pair_o[0][0], g)
                + up_pieces(pair, up_zero, up_cross[g], g)
                + up_pieces(pair_o, up_zero_o, cross_o[g], g)
            )
            span = 1 if g in (0, steps) else 2
            kept, own_terms[g], give_terms[g], rows = moe_call(
                0 if g == 0 else 2 * g - 1,
                span,
                sizes,
                chips,
                pieces,
                half_arg,
                row_aux,
                col_aux,
                router_all,
                (ex_in, ex_out, sh_w),
                kept,
            )
            dot_rows.append(rows)
            *now, dot_rows[-1], give_terms[g] = hold(*now, rows, give_terms[g])
            if k <= steps:
                pair[k], up_cross[k], *now = now
            if g >= 1:
                give_got[g - 1] = now[0]
            if g >= 2:
                place_crossed(0, g - 2, now[1])

        rows_all, slots_all, hidden_all, gu_all, tok_all, y_all, s_hidden_all, s_gu_all = kept
        give_got[steps] = swap_core(give_terms[steps])
        near_far = receive(steps - 1)
        near_far, give_got[steps] = hold(near_far, give_got[steps])
        grads = receive(steps)
        s_hidden_all, grads = hold(s_hidden_all, grads)
        far = ring.offsets[-1]
        grads = swap_tensor(grads)
        sh_grad = pl.pallas_call(
            shared_grad_kernel,
            grid=(chips,),
            out_shape=jax.ShapeDtypeStruct((2, chips, 3 * unit_chip, rows_dev), bf16),
            in_specs=[
                pl.BlockSpec((chips * length, depth), lambda n: (0, n)),
                pl.BlockSpec((chips * length, depth), lambda n: (0, n)),
                pl.BlockSpec((chips * length, unit_chip), lambda n: (0, 0)),
                pl.BlockSpec((2, chips * length, unit_chip), lambda n: (0, 0, 0)),
            ],
            out_specs=pl.BlockSpec((2, 1, 3 * unit_chip, rows_dev), lambda n: (0, n, 0, 0)),
            compiler_params=params(),
            cost_estimate=cost(2 * chips * length * width * 3 * unit_chip, 26 * 1024 * 1024),
            name="shared_grad",
        )(tok_all, y_all, s_hidden_all, s_gu_all)
        near_got = swap_tensor(near_far)
        grads, sh_grad = hold(grads, sh_grad)
        place_crossed(0, steps, grads)

        def ring_terms(which, o):
            return [*terms[o][which], crossed[which, o]]

        sending = ring.reduce_first(ring_terms(0, far))
        own, other = halves(sh_grad, 0)
        sh_got = swap_core(other)
        gu_all = after(gu_all, grads)
        sh_sum = (own.astype(f32) + sh_got.astype(f32)).astype(bf16)[0]
        expert_in_grad = mm(gu_all, rows_all, 1, 0).transpose(2, 0, 1)[None]
        near_got, sending, sh_sum, expert_in_grad = hold(
            near_got, sending, sh_sum, expert_in_grad
        )
        place_crossed(0, steps - 1, near_got)
        out_sent = {}
        for k in range(steps - 1, 0, -1):
            send = ring.reduce_terms(
                ring_terms(0, k), ring_terms(0, -k), sending, k == steps - 1
            )
            now = []
            if k == steps - 1:
                hidden_all, send, far_outs = hold(hidden_all, send, receive_outs(steps))
                expert_out_grad = mm(hidden_all, slots_all, 0, 0)[None]
                out_sent[steps] = swap_tensor(far_outs)
                dots = jnp.concatenate(after_all(dot_rows, send[0]), axis=0)
                sdots = jnp.concatenate([dots[:, 2:3], jnp.zeros_like(dots[:, 2:3])], axis=1)
                dot_send = jnp.stack([dots[:, :2], sdots], axis=2)
                dot_send = dot_send.reshape(devices, 2, length)[seq_inv]
                dot_got = lax.all_to_all(
                    dot_send, "expert", split_axis=0, concat_axis=0, tiled=True
                )
                dot_got = jnp.concatenate(
                    [dot_got[:, 0], jnp.sum(dot_got[:, 1], axis=0)[None]], axis=0
                )
                now = [out_sent[steps], dot_got, expert_out_grad]
            sending = ring.send_pair(*send)
            sending, *now = hold(sending, *now)
            if k == steps - 1:
                out_sent[steps], dot_got, expert_out_grad = now
        place_crossed(1, steps, out_sent[steps])
        dot_got = dot_got + swap_tensor(dot_got)
        second_half = ring.add_up([*ring_terms(0, 0), *sending]).astype(bf16)
        sh_back = lax.all_to_all(
            after(sh_sum, second_half),
            "expert",
            split_axis=0,
            concat_axis=0,
            tiled=True,
            axis_index_groups=same_core,
        )
        second_got = swap_tensor(second_half)
        out_sending = ring.reduce_first(ring_terms(1, far))
        second_got, out_sending = hold(second_got, out_sending)

        def both_halves(own, other):
            return jnp.where(
                half == 0,
                jnp.concatenate([own, other], axis=0),
                jnp.concatenate([other, own], axis=0),
            )

        second_part = both_halves(second_half, second_got)

        gate_grad_dense, sigma_grad = dot_got[:experts].T, dot_got[experts]
        row_term = jnp.sum(gate_dense * gate_grad_dense, axis=-1, keepdims=True)
        logit_grad = (gate_dense * (gate_grad_dense - row_term)).astype(bf16)
        gate_logit_grad = sigma_grad * shared_sigma * (1.0 - shared_sigma)

        second_grad = second_part.astype(f32)
        second_grad = second_grad + mm(logit_grad, router_w, 1, 1)
        second_grad = second_grad + gate_logit_grad[:, None] * gate_vec.astype(f32)[None]
        upstream = cotangent.astype(f32)
        residual_norm_grad, gain_two_grad = jax.vjp(rms_norm, residual, gains_f[1])[1](second_grad)
        residual_grad = upstream + residual_norm_grad
        attn_grad = residual_grad.astype(bf16)
        attn_grad_o = ring.swap_core(attn_grad)

        def by_chip(left, right, wanted=tuple(ring.offsets)):
            return {
                offset: [
                    mm(lax.dynamic_slice_in_dim(left, chip_of[i] * depth, depth, 1), right, 0, 0)
                ]
                for i, offset in enumerate(ring.offsets)
                if offset in wanted
            }

        proj_grad, bias_grad = pl.pallas_call(
            functools.partial(attend_back_kernel, chips + 1, heads, score_scale),
            out_shape=[
                jax.ShapeDtypeStruct((2 * length, 3 * half_cols), bf16),
                jax.ShapeDtypeStruct((1, 3 * half_cols), f32),
            ],
            in_specs=[in_smem] * 2 + [in_vmem] * 7 + [in_any] * (chips + 1),
            out_specs=[in_vmem] * 2,
            scratch_shapes=[
                pltpu.VMEM((1, width, half_cols), bf16),
                pltpu.SemaphoreType.DMA((chips,)),
            ],
            compiler_params=params(),
            cost_estimate=cost(2 * 2 * length * width * half_cols * 2, 8 * 1024 * 1024),
            name="attend_back",
        )(
            chip_arg,
            prefix_pair,
            attn_grad,
            attn_grad_o,
            query,
            key,
            value,
            cosine,
            sine,
            *attn_w,
        )
        crossing = swap_tensor(receive_outs(steps - 1))
        first_pair = jnp.concatenate([first_b, first_o], axis=0)
        attn_grad_pair = jnp.concatenate([attn_grad, attn_grad_o], axis=0)
        out_parts = by_chip(attn_grad_pair, mixed)
        far_out = out_parts[steps][0].astype(bf16)
        far_out, proj_grad, sh_back = hold(far_out, proj_grad, sh_back)
        far_part = by_chip(first_pair, proj_grad, [steps])[steps][0].astype(bf16)
        far_part = jnp.concatenate([far_part, far_out], axis=1)
        cut = depth // 2
        proj_grad, ahead, back = hold(proj_grad, far_part[:cut], far_part[cut:])
        going = ring.send_pair(ahead, back)
        qkv_parts = by_chip(first_pair, proj_grad, ring.offsets[:-1])
        attn_parts = {
            o: [
                jnp.concatenate(
                    [qkv_parts[o][0].astype(bf16), out_parts[o][0].astype(bf16)], axis=1
                )
            ]
            for o in qkv_parts
        }
        bias_grad = bias_grad[0]
        first_own, first_give = pl.pallas_call(
            functools.partial(project_back_kernel, chips + 1),
            out_shape=[
                jax.ShapeDtypeStruct((length, width), f32),
                jax.ShapeDtypeStruct((length, width), bf16),
            ],
            in_specs=[in_smem, in_vmem] + [in_any] * (chips + 1),
            out_specs=[in_vmem] * 2,
            scratch_shapes=[
                pltpu.VMEM((3, width, half_cols), bf16),
                pltpu.SemaphoreType.DMA((3 * chips,)),
            ],
            compiler_params=params(),
            cost_estimate=cost(2 * 2 * length * width * 3 * half_cols, 12 * 1024 * 1024),
            name="project_back",
        )(chip_arg, proj_grad, *attn_w)
        first_own = (first_own + swap_core(first_give).astype(f32)).astype(bf16)
        def send_outs(k, going):
            return ring.send_pair(
                *ring.reduce_terms(ring_terms(1, k), ring_terms(1, -k), going, k == steps - 1)
            )

        second_f = second_b.astype(f32)
        router_part = mm(second_b, logit_grad, 0, 0)
        shared_gate_part = jnp.sum(gate_logit_grad[:, None] * second_f, axis=0)
        early = jnp.concatenate(
            [router_part, shared_gate_part[:, None], gain_two_grad[:, None]], axis=1
        ).reshape(devices, rows_dev * (experts + 2))

        def send_next(k, going):
            return ring.send_pair(
                *ring.reduce_terms(attn_parts[k], attn_parts[-k], going, k == steps - 1)
            )

        pieces = [attn_parts[o][0] for o in ring.offsets[:-1]]
        going, crossing, first_own, pieces = hold(going, crossing, first_own, pieces)
        for o, piece in zip(ring.offsets[:-1], pieces, strict=True):
            attn_parts[o] = [piece]
        place_crossed(1, steps - 1, crossing)
        for k in range(steps - 1, -1, -1):
            if k > 0:
                going = send_next(k, going)
                out_sending = send_outs(k, out_sending)
            now = []
            if k > 0:
                now.append(swap_tensor(receive_outs(k - 1)))
            if k == steps - 2:
                now.append(swap_tensor(first_own))
            if k == 0:
                res_half = lax.dynamic_slice_in_dim(residual, half * half_length, half_length, 0)
                out_half = ring.add_up([res_half, *ring_terms(1, 0), *out_sending]).astype(bf16)
                output = both_halves(out_half, swap_tensor(out_half))
                break
            if k == 2:
                now.append(sh_back)
            going, out_sending, *now = hold(going, out_sending, *now)
            place_crossed(1, k - 1, now[0])
            if k == 2:
                sh_back = now[-1]
            if k == steps - 2:
                first_got = now[1]
        attn_grads = ring.add_up([*attn_parts[0], *going])
        first_grad = first_own.astype(f32) + first_got.astype(f32)
        input_norm_grad, gain_one_grad = jax.vjp(rms_norm, inputs, gains_f[0])[1](first_grad)
        input_grad = (residual_grad + input_norm_grad).astype(bf16)

        own, other = halves(attn_grads.astype(bf16), 0)
        both = by_core(
            own.reshape(rows_dev, 4, half_cols),
            swap_core(other).reshape(rows_dev, 4, half_cols),
            2,
        ).astype(f32)
        qkv_weight_grad = both[:, :3]
        out_weight_grad = both[:, 3].T

        sh_back = sh_back.reshape(chips, 3, unit_chip, rows_dev).astype(f32)
        shared_in_grad = sh_back[:, :2].transpose(3, 1, 0, 2).reshape(rows_dev, 2, units)
        shared_out_grad = sh_back[:, 2].reshape(units, rows_dev)

        bias_send = bias_grad.reshape(3 * heads, devices, hd_dev).transpose(1, 0, 2)
        late = jnp.concatenate(
            [gain_one_grad.reshape(devices, rows_dev), bias_send.reshape(devices, -1), early],
            axis=1,
        )
        late = lax.all_to_all(late, "expert", split_axis=0, concat_axis=0, tiled=True)
        gain_one = jnp.sum(late[:, :rows_dev], axis=0)
        count = 3 * heads * hd_dev
        early = late[:, rows_dev + count :]
        early = jnp.sum(early, axis=0).reshape(rows_dev, experts + 2)
        router_grad, shared_gate_grad = early[:, :experts], early[:, experts]
        bias_got = jnp.sum(late[:, rows_dev : rows_dev + count].reshape(chips, 2, 3, heads, hd_dev), axis=0)
        qkv_bias_grad = bias_got.transpose(1, 0, 2, 3).reshape(3, heads_t, hd_dev)
        gains_grad = jnp.stack([gain_one, early[:, experts + 1]], axis=0)

        return (
            output,
            input_grad,
            gains_grad,
            qkv_weight_grad,
            qkv_bias_grad,
            out_weight_grad,
            router_grad,
            shared_gate_grad,
            shared_in_grad,
            shared_out_grad,
            expert_in_grad,
            expert_out_grad,
        )

    return local


def solution(mesh):
    ring = Ring(mesh.shape["expert"])
    return jax.shard_map(
        make_local(ring),
        mesh=mesh,
        in_specs=(
            P("expert", None),
            P("expert", None),
            P(None, "expert"),
            P("expert", None, "tensor"),
            P(None, "tensor", "expert"),
            P("tensor", "expert"),
            P("expert", None),
            P("expert"),
            P("expert", None, "tensor"),
            P("tensor", "expert"),
            P("expert", None, None, "tensor"),
            P("expert", "tensor", None),
            P("expert", None),
            P("expert"),
        ),
        out_specs=(
            P("expert", None),
            P("expert", None),
            P(None, "expert"),
            P("expert", None, "tensor"),
            P(None, "tensor", "expert"),
            P("tensor", "expert"),
            P("expert", None),
            P("expert"),
            P("expert", None, "tensor"),
            P("tensor", "expert"),
            P("expert", None, None, "tensor"),
            P("expert", "tensor", None),
        ),
        check_vma=False,
    )
```

```python
import functools

import jax
import jax.numpy as jnp
import numpy as np
from jax import lax
from jax.experimental import pallas as pl
from jax.experimental.pallas import tpu as pltpu
from jax.sharding import PartitionSpec as P

eps = 1e-06
theta_base = 1000000.0
neg_large = -1e30
no_slot = -100000.0
bf16 = jnp.bfloat16
f32 = jnp.float32
in_vmem = pl.BlockSpec(memory_space=pltpu.VMEM)
in_smem = pl.BlockSpec(memory_space=pltpu.SMEM)
in_any = pl.BlockSpec(memory_space=pl.ANY)


def rms_norm(values, gain_row):
    factor = lax.rsqrt(jnp.mean(values * values, axis=-1, keepdims=True) + eps)
    return values * factor * gain_row


def rotary_tables(length, head_size):
    half_size = head_size // 2
    frequency = np.float32(theta_base) ** (
        -(np.arange(half_size, dtype=np.float32) * np.float32(2.0)) / np.float32(head_size)
    )
    angles = np.arange(length, dtype=np.float32)[:, None] * frequency[None, :].astype(np.float32)
    cosine = np.concatenate([np.cos(angles), np.cos(angles)], axis=-1)
    sine = np.concatenate([-np.sin(angles), np.sin(angles)], axis=-1)
    return jnp.asarray(cosine, f32), jnp.asarray(sine, f32)


def chip_ring(chips):
    columns = chips // 4
    if chips % 4 or columns < 2 or columns % 2:
        return list(range(chips))
    walk = [(0, 0)]
    for column in range(columns):
        rows = range(1, 4) if column % 2 == 0 else range(3, 0, -1)
        walk += [(row, column) for row in rows]
    walk += [(0, column) for column in range(columns - 1, 0, -1)]
    return [row * columns + column for row, column in walk]


def mm(left, right, contract_left=1, contract_right=0):
    return lax.dot_general(
        left,
        right,
        (((contract_left,), (contract_right,)), ((), ())),
        preferred_element_type=f32,
    )


def nt(left, right):
    return mm(left, right, 1, 1)


def tiles(total, size):
    return [(lo, min(size, total - lo)) for lo in range(0, total, size)]


def params(mebibytes=56):
    return pltpu.CompilerParams(vmem_limit_bytes=mebibytes * 1024 * 1024)


def half_turn(values):
    return pltpu.roll(values, values.shape[1] // 2, 1)


def masked(scores, prefix_cut):
    length = scores.shape[0]
    row = lax.broadcasted_iota(jnp.int32, (length, length), 0)
    col = lax.broadcasted_iota(jnp.int32, (length, length), 1)
    return jnp.where((col <= row) | (col < prefix_cut), scores, neg_large)


def softmax_rows(scores):
    weights = jnp.exp(scores - jnp.max(scores, axis=-1, keepdims=True))
    return weights / jnp.sum(weights, axis=-1, keepdims=True)


def load_blocks(chip_ref, blocks, scratch, sem, first, last):
    whole = len(blocks) - 2
    depth = blocks[0].shape[0] // 4
    copies = []
    for i in range(whole + 1):
        start = pl.multiple_of(chip_ref[i] * depth, depth)
        for c in range(first, last):
            block, at = (blocks[i], c) if i < whole else (blocks[whole + c // 2], c % 2)
            copies.append(
                pltpu.make_async_copy(
                    block.at[pl.ds(at * depth, depth)],
                    scratch.at[c - first, pl.ds(start, depth)],
                    sem.at[len(copies)],
                )
            )
    for copy in copies:
        copy.start()
    return copies


def attend_kernel(count, heads, scale, *refs):
    chip_ref, prefix_ref, own, other, bias, cosine, sine = refs[:7]
    blocks = refs[7 : 7 + count]
    query, key, value, mixed, weight, sem = refs[7 + count :]
    copies = load_blocks(chip_ref, blocks, weight, sem, 0, 3)
    length, head_size = cosine.shape
    columns = heads * head_size
    for copy in copies:
        copy.wait()
    for c, out in enumerate((query, key, value)):
        for b, rows in enumerate((own, other)):
            for lo, size in tiles(columns, 2 * head_size):
                part = mm(rows[...], weight[c, :, lo : lo + size])
                part = part + bias[:, c * columns + lo : c * columns + lo + size]
                for at in range(0, size, head_size):
                    one = part[:, at : at + head_size]
                    if c < 2:
                        one = one * cosine[...] + half_turn(one) * sine[...]
                    out[b * length : (b + 1) * length, lo + at : lo + at + head_size] = one.astype(
                        bf16
                    )
    for b in range(2):
        rows = slice(b * length, (b + 1) * length)
        for h in range(heads):
            cols = slice(h * head_size, (h + 1) * head_size)
            scores = masked(nt(query[rows, cols], key[rows, cols]) * scale, prefix_ref[b])
            probs = softmax_rows(scores).astype(bf16)
            mixed[rows, cols] = mm(probs, value[rows, cols]).astype(bf16)


def project_kernel(count, *refs):
    chip_ref, mixed = refs[:2]
    blocks = refs[2 : 2 + count]
    own, other, weight, sem = refs[2 + count :]
    copies = load_blocks(chip_ref, blocks, weight, sem, 3, 4)
    for copy in copies:
        copy.wait()
    length, width = own.shape
    for lo, size in tiles(width, 512):
        part = nt(mixed[...], weight[0, lo : lo + size, :])
        own[:, lo : lo + size] = part[:length].astype(own.dtype)
        other[:, lo : lo + size] = part[length:].astype(other.dtype)


def attend_back_kernel(count, heads, scale, *refs):
    chip_ref, prefix_ref, own, other, query, key, value, cosine, sine = refs[:9]
    blocks = refs[9 : 9 + count]
    grad, bias, weight, sem = refs[9 + count :]
    copies = load_blocks(chip_ref, blocks, weight, sem, 3, 4)
    length, head_size = cosine.shape
    columns = heads * head_size
    for copy in copies:
        copy.wait()
    for b, up in enumerate((own, other)):
        rows = slice(b * length, (b + 1) * length)
        mixed_grad = mm(up[...], weight[0]).astype(bf16)
        for h in range(heads):
            cols = slice(h * head_size, (h + 1) * head_size)
            q, k, v = query[rows, cols], key[rows, cols], value[rows, cols]
            up_head = mixed_grad[:, cols]
            probs = softmax_rows(masked(nt(q, k) * scale, prefix_ref[b]))
            prob_grad = nt(up_head, v)
            row_term = jnp.sum(probs * prob_grad, axis=-1, keepdims=True)
            score_grad = (probs * (prob_grad - row_term)).astype(bf16)
            q_grad = mm(score_grad, k) * scale
            k_grad = mm(score_grad, q, 0, 0) * scale
            v_grad = mm(probs.astype(bf16), up_head, 0, 0)
            for c, one in enumerate((q_grad, k_grad, v_grad)):
                if c < 2:
                    one = one * cosine[...] - half_turn(one) * sine[...]
                one = one.astype(bf16)
                at = slice(c * columns + h * head_size, c * columns + (h + 1) * head_size)
                grad[rows, at] = one
                column_sum = jnp.sum(one.astype(f32), axis=0, keepdims=True)
                bias[:, at] = column_sum if b == 0 else bias[:, at] + column_sum


def project_back_kernel(count, *refs):
    chip_ref, grad = refs[:2]
    blocks = refs[2 : 2 + count]
    own, other, weight, sem = refs[2 + count :]
    copies = load_blocks(chip_ref, blocks, weight, sem, 0, 3)
    for copy in copies:
        copy.wait()
    length, width = own.shape
    columns = grad.shape[1] // 3
    for lo, size in tiles(width, 512):
        part = nt(grad[:, :columns], weight[0, lo : lo + size, :])
        for c in range(1, 3):
            part = part + nt(grad[:, c * columns : (c + 1) * columns], weight[c, lo : lo + size, :])
        own[:, lo : lo + size] = part[:length].astype(own.dtype)
        other[:, lo : lo + size] = part[length:].astype(other.dtype)


def moe_kernel(index, span, first, plan, sizes, *refs):
    length, width, capacity, units, shared_units, experts, top_count = sizes
    count = sum(len(p) for p in plan)
    own_rows, slab = span * length, 2 * span * capacity
    half_ref, row_hbm, col_hbm, router_hbm = refs[:4]
    given = refs[4 : 4 + count]
    in_hbm, out_hbm, shared_hbm = refs[4 + count : 7 + count]
    rest = refs[7 + count + (0 if first else 8) :]
    kept, owns, give, dots = rest[:8], rest[8 : 8 + span], rest[8 + span], rest[9 + span]
    tok, up, rows, up_rows, slots, hidden, gu, y_grad, s_hidden, s_gu, made_out = rest[
        10 + span : 21 + span
    ]
    w_in, w_out, w_sh, row_ref, col_ref, router = rest[21 + span : 27 + span]
    load_sem, weight_sem, out_sem, keep_sem = rest[27 + span :]
    wide = min(512, width)
    columns = tiles(width, wide)

    tables = [
        pltpu.make_async_copy(a, b, weight_sem.at[3 + i])
        for i, (a, b) in enumerate(
            (
                (row_hbm.at[pl.ds(index, span)], row_ref),
                (col_hbm.at[pl.ds(index, span)], col_ref),
                (router_hbm, router),
            )
        )
    ]
    for copy in tables:
        copy.start()

    loads = []
    for n, (lo, size_cols) in enumerate(columns):
        cols, number = slice(lo, lo + size_cols), 0
        loads.append([])
        for which, pieces in enumerate(plan):
            target, at = (tok, up)[which // (2 * span)], which % (2 * span) * length
            for first_row, size, start_zero, start_one in pieces:
                start = start_zero + half_ref[0] * (start_one - start_zero)
                start = pl.multiple_of(start + at, 16)
                copy = pltpu.make_async_copy(
                    given[number].at[first_row : first_row + size, cols],
                    target.at[pl.ds(start, size), cols],
                    load_sem.at[n, number],
                )
                copy.start()
                loads[-1].append(copy)
                number += 1

    weights = [
        pltpu.make_async_copy(a, b, weight_sem.at[i])
        for i, (a, b) in enumerate(
            (
                (shared_hbm, w_sh),
                (in_hbm, w_in),
                (out_hbm, w_out),
            )
        )
    ]
    for copy in weights:
        copy.start()
    for copy in tables:
        copy.wait()

    def keep(slot, source):
        target = kept[slot]
        size = source.shape[-2]
        first_row = index * (size // span)
        if len(target.shape) == 3:
            target = target.at[:, pl.ds(first_row, size)]
        else:
            target = target.at[pl.ds(first_row, size)]
        copy = pltpu.make_async_copy(source, target, keep_sem.at[slot])
        copy.start()
        return copy

    slot = lax.broadcasted_iota(jnp.int32, (capacity, length), 0).astype(f32)
    lane = lax.broadcasted_iota(jnp.int32, (length, 2 * capacity), 1).astype(f32)
    picks, ones, places = [], [], []
    for j in range(span):
        place = []
        for c in range(2):
            pick = slot == row_ref[j, c : c + 1, :]
            picks.append(pick)
            ones.append(jnp.where(pick, 1.0, 0.0).astype(bf16))
            rank = col_ref[j, :, c : c + 1] + float(c * capacity)
            place.append(jnp.where(lane == rank, 1.0, 0.0))
        places.append(jnp.concatenate(place, axis=0))

    logits = jnp.zeros((2 * own_rows, router.shape[1]), f32)
    for n, (lo, size) in enumerate(columns):
        cols = slice(lo, lo + size)
        for copy in loads[n]:
            copy.wait()
        logits = logits + mm(tok[:, cols], router[cols, :])
        for j in range(span):
            for c in range(2):
                source = slice((c * span + j) * length, (c * span + j + 1) * length)
                target = slice((2 * j + c) * capacity, (2 * j + c + 1) * capacity)
                rows[target, cols] = mm(ones[2 * j + c], tok[source, cols]).astype(bf16)
                up_rows[target, cols] = mm(ones[2 * j + c], up[source, cols]).astype(bf16)

    expert = lax.broadcasted_iota(jnp.int32, (length, router.shape[1]), 1).astype(f32)
    mine = expert == half_ref[1].astype(f32)
    row = lax.broadcasted_iota(jnp.int32, (2 * capacity, 2 * capacity), 0)
    col = lax.broadcasted_iota(jnp.int32, (2 * capacity, 2 * capacity), 1)
    gates, sigmas = [], []
    for j in range(span):
        taken = []
        for c in range(2):
            part = logits[(c * span + j) * length : (c * span + j + 1) * length]
            first_id = 2 + c * top_count
            chosen = expert == col_ref[j, :, first_id : first_id + 1]
            for k in range(first_id + 1, first_id + top_count):
                chosen = chosen | (expert == col_ref[j, :, k : k + 1])
            peak = jnp.max(jnp.where(chosen, part, neg_large), axis=1, keepdims=True)
            weight = jnp.where(chosen, jnp.exp(part - peak), 0.0)
            weight = weight / jnp.sum(weight, axis=1, keepdims=True)
            taken.append(jnp.sum(jnp.where(mine, weight, 0.0), axis=1, keepdims=True))
            if c == 0:
                gate = expert == float(experts)
                gate = jnp.sum(jnp.where(gate, part, 0.0), axis=1, keepdims=True)
                sigmas.append(1.0 / (1.0 + jnp.exp(-gate)))
        slot_gates = jnp.sum(places[j] * jnp.concatenate(taken, axis=0), axis=0, keepdims=True)
        gates.append(jnp.sum(jnp.where(row == col, slot_gates, 0.0), axis=1, keepdims=True))
        places[j] = places[j].astype(bf16)
    gate_all = jnp.concatenate(gates, axis=0)
    sigma_all = jnp.concatenate(sigmas, axis=0)
    for lo, size in columns:
        cols = slice(lo, lo + size)
        slots[:, cols] = (gate_all * up_rows[:, cols].astype(f32)).astype(bf16)
        y_grad[:, cols] = (sigma_all * up[0:own_rows, cols].astype(f32)).astype(bf16)

    kept_copies = [keep(4, tok.at[0:own_rows]), keep(0, rows), keep(1, slots), keep(5, y_grad)]

    def gated(gate_part, up_part, grad):
        sig = 1.0 / (1.0 + jnp.exp(-gate_part))
        silu = gate_part * sig
        return (
            (silu * up_part).astype(bf16),
            (grad * up_part * (sig * (1.0 + gate_part * (1.0 - sig)))).astype(bf16),
            (grad * silu).astype(bf16),
        )

    weights[0].wait()
    for lo, size in tiles(shared_units, 256):
        at = slice(lo, lo + size)
        gate_part = nt(tok[0:own_rows, :], w_sh[0, at, :])
        up_part = nt(tok[0:own_rows, :], w_sh[1, at, :])
        grad = nt(y_grad[...], w_sh[2, at, :])
        s_hidden[:, at], s_gu[0, :, at], s_gu[1, :, at] = gated(gate_part, up_part, grad)
    kept_copies += [keep(6, s_hidden), keep(7, s_gu)]
    weights[1].wait()
    weights[2].wait()
    for lo, size in tiles(units, 256):
        at = slice(lo, lo + size)
        gate_part = nt(rows[...], w_in[0, at, :])
        up_part = nt(rows[...], w_in[1, at, :])
        grad = nt(slots[...], w_out[at, :])
        hidden[:, at], gu[0, :, at], gu[1, :, at] = gated(gate_part, up_part, grad)
    kept_copies += [keep(2, hidden), keep(3, gu)]

    slot_dots, sigma_dots = jnp.zeros((slab, 1), f32), jnp.zeros((own_rows, 1), f32)
    sent = []
    for n, (lo, size) in enumerate(columns):
        cols, turn = slice(lo, lo + size), n % 2
        if n >= 2:
            for copy in sent[n - 2]:
                copy.wait()
        made = mm(hidden[...], w_out[:, cols]).astype(bf16).astype(f32)
        slot_dots = slot_dots + jnp.sum(
            up_rows[:, cols].astype(f32) * made, axis=1, keepdims=True
        )
        made = (gate_all * made).astype(bf16)
        shared = mm(s_hidden[...], w_sh[2, :, cols])
        sigma_dots = sigma_dots + jnp.sum(
            up[0:own_rows, cols].astype(f32) * shared, axis=1, keepdims=True
        )
        shared = sigma_all * shared
        entry = (mm(gu[0], w_in[0, :, cols]) + mm(gu[1], w_in[1, :, cols])).astype(bf16)
        shared_back = mm(s_gu[0], w_sh[0, :, cols]) + mm(s_gu[1], w_sh[1, :, cols])
        sent.append([])
        for j in range(span):
            mine = slice(j * length, (j + 1) * length)
            theirs = slice(2 * j * capacity, 2 * (j + 1) * capacity)
            routed = mm(places[j], made[theirs])
            made_out[turn, 4 * j] = (routed[:length] + shared[mine]).astype(bf16)
            made_out[turn, 4 * j + 1] = routed[length:].astype(bf16)
            routed = mm(places[j], entry[theirs])
            made_out[turn, 4 * j + 2] = (routed[:length] + shared_back[mine]).astype(bf16)
            made_out[turn, 4 * j + 3] = routed[length:].astype(bf16)
            middle = length // 2
            for k in range(4):
                target, base = (owns[j], 0) if k % 2 == 0 else (give, 2 * j * length)
                base += (length, 0)[k // 2]
                for m, h in enumerate((half_ref[0], 1 - half_ref[0])):
                    source = made_out.at[
                        turn, 4 * j + k, pl.ds(pl.multiple_of(h * middle, 16), middle)
                    ]
                    at = base + m * middle
                    copy = pltpu.make_async_copy(
                        source, target.at[at : at + middle, cols], out_sem.at[turn, 4 * j + k, m]
                    )
                    copy.start()
                    sent[-1].append(copy)
    row = lax.broadcasted_iota(jnp.int32, (length, length), 0)
    col = lax.broadcasted_iota(jnp.int32, (length, length), 1)
    for j in range(span):
        for c in range(2):
            part = slot_dots[(2 * j + c) * capacity : (2 * j + c + 1) * capacity]
            part = jnp.where(picks[2 * j + c], part, 0.0)
            dots[j, c : c + 1, :] = jnp.sum(part, axis=0, keepdims=True)
        part = jnp.where(row == col, sigma_dots[j * length : (j + 1) * length], 0.0)
        dots[j, 2:3, :] = jnp.sum(part, axis=0, keepdims=True)
        dots[j, 3:, :] = jnp.zeros((dots.shape[1] - 3, length), f32)
    for copy in kept_copies + [copy for group in sent[-2:] for copy in group]:
        copy.wait()


def moe_call(index, span, sizes, chips, pieces, where, row_aux, col_aux, router, weights, kept):
    length, width, capacity, units, shared_units = sizes[:5]
    plan = [[place for _, place in group] for group in pieces]
    arrays = [piece for group in pieces for piece, _ in group]
    first = kept is None
    own_rows, slab = span * length, 2 * span * capacity
    slots, tokens = chips * 2 * capacity, chips * length
    kept_shapes = [
        jax.ShapeDtypeStruct(shape, bf16)
        for shape in (
            (slots, width),
            (slots, width),
            (slots, units),
            (2, slots, units),
            (tokens, width),
            (tokens, width),
            (tokens, shared_units),
            (2, tokens, shared_units),
        )
    ]
    own = jax.ShapeDtypeStruct((2 * length, width), bf16)
    give = jax.ShapeDtypeStruct((2 * own_rows, width), bf16)
    operands = [where, row_aux, col_aux, router, *arrays, *weights]
    operands += [] if first else list(kept)
    aliases = {} if first else {len(operands) - 8 + i: i for i in range(8)}
    flops = 2 * slab * width * units * 6 + 2 * own_rows * width * shared_units * 6
    out = pl.pallas_call(
        functools.partial(moe_kernel, index, span, first, plan, sizes),
        out_shape=kept_shapes
        + [own] * span
        + [give]
        + [jax.ShapeDtypeStruct((span, 8, length), f32)],
        in_specs=[in_smem] + [in_any] * 3
        + [in_any] * (len(arrays) + 3 + (0 if first else 8)),
        out_specs=[in_any] * (9 + span) + [in_vmem],
        scratch_shapes=[
            pltpu.VMEM((2 * own_rows, width), bf16),
            pltpu.VMEM((2 * own_rows, width), bf16),
            pltpu.VMEM((slab, width), bf16),
            pltpu.VMEM((slab, width), bf16),
            pltpu.VMEM((slab, width), bf16),
            pltpu.VMEM((slab, units), bf16),
            pltpu.VMEM((2, slab, units), bf16),
            pltpu.VMEM((own_rows, width), bf16),
            pltpu.VMEM((own_rows, shared_units), bf16),
            pltpu.VMEM((2, own_rows, shared_units), bf16),
            pltpu.VMEM((2, 4 * span, length, min(512, width)), bf16),
            pltpu.VMEM((2, units, width), bf16),
            pltpu.VMEM((units, width), bf16),
            pltpu.VMEM((3, shared_units, width), bf16),
            pltpu.VMEM((span, *row_aux.shape[1:]), f32),
            pltpu.VMEM((span, *col_aux.shape[1:]), f32),
            pltpu.VMEM(router.shape, bf16),
            pltpu.SemaphoreType.DMA((len(tiles(width, min(512, width))), len(arrays))),
            pltpu.SemaphoreType.DMA((6,)),
            pltpu.SemaphoreType.DMA((2, 4 * span, 2)),
            pltpu.SemaphoreType.DMA((8,)),
        ],
        input_output_aliases=aliases,
        compiler_params=params(),
        cost_estimate=pl.CostEstimate(
            flops=flops // 64, bytes_accessed=span * 512 * 1024, transcendentals=0
        ),
        name=f"experts_{index}",
    )(*operands)
    return out[:8], out[8 : 8 + span], out[8 + span], out[9 + span]


def spread_kernel(core_ref, own, other, out):
    parts, units, _ = out.shape
    count, _, rows = own.shape

    def spread(first, second):
        for i in range(count):
            for c in range(parts):
                at = slice(c * units, (c + 1) * units)
                both = jnp.concatenate([first[i, at, :], second[i, at, :]], axis=1)
                out[c, :, 2 * i * rows : 2 * (i + 1) * rows] = both

    @pl.when(core_ref[0] == 0)
    def _():
        spread(own, other)

    @pl.when(core_ref[0] == 1)
    def _():
        spread(other, own)


def shared_grad_kernel(tok, y_grad, hidden, gu, out):
    units = hidden.shape[1]
    rows = out.shape[3]
    for c in range(3):
        left = gu[c] if c < 2 else hidden[...]
        right = tok[...] if c < 2 else y_grad[...]
        part = mm(left, right, 0, 0).astype(bf16)
        for k in range(2):
            out[k, 0, c * units : (c + 1) * units, :] = part[:, k * rows : (k + 1) * rows]


class Ring:
    def __init__(self, devices):
        self.devices = devices
        self.chips = devices // 2
        order = chip_ring(self.chips)
        n = self.chips
        self.next = [
            (order[i] * 2 + c, order[(i + 1) % n] * 2 + c) for i in range(n) for c in range(2)
        ]
        self.prev = [(b, a) for a, b in self.next]
        self.core = [(e, e ^ 1) for e in range(devices)]
        half = n // 2
        offsets = [0]
        for k in range(1, half):
            offsets += [-k, k]
        self.offsets = offsets + [half]
        place = {chip: i for i, chip in enumerate(order)}
        self.chip_table = np.array(
            [
                [order[(place[e // 2] + o) % n] for o in self.offsets]
                for e in range(devices)
            ],
            np.int32,
        )
        self.seq_table = np.stack(
            [
                2 * self.chip_table + (np.arange(devices) % 2)[:, None],
                2 * self.chip_table + 1 - (np.arange(devices) % 2)[:, None],
            ],
            axis=-1,
        ).reshape(devices, devices)
        self.seq_inverse = np.argsort(self.seq_table, axis=1).astype(np.int32)

    def step(self, ahead, back=None, last=False):
        back = ahead if back is None else back
        if last:
            cut = ahead.shape[0] // 2
            ahead, back = ahead[:cut], back[cut:]
        return self.send_pair(ahead, back)

    def send_pair(self, ahead, back):
        return [
            lax.ppermute(ahead, "expert", self.next),
            lax.ppermute(back, "expert", self.prev),
        ]

    def add_up(self, terms):
        out = None
        for term in terms:
            out = term.astype(f32) if out is None else out + term.astype(f32)
        return out

    def reduce_first(self, terms):
        total = self.add_up(terms).astype(bf16)
        return self.step(total, last=True)

    def reduce_terms(self, ahead_terms, back_terms, sending, first):
        mine, yours = self.add_up(ahead_terms), self.add_up(back_terms)
        ahead, back = (part.astype(f32) for part in sending)
        if first:
            cut = ahead.shape[0]
            mine = jnp.concatenate([mine[:cut] + ahead, mine[cut:]], axis=0)
            yours = jnp.concatenate([yours[:cut], yours[cut:] + back], axis=0)
        else:
            mine, yours = mine + ahead, yours + back
        return [mine.astype(bf16), yours.astype(bf16)]

    def reduce(self, terms):
        half = self.chips // 2
        sending = self.reduce_first(terms[half])
        for k in range(half - 1, 0, -1):
            send = self.reduce_terms(terms[k], terms[-k], sending, k == half - 1)
            sending = self.send_pair(*send)
        return self.add_up([*terms[0], *sending])

    def swap_core(self, block):
        return lax.ppermute(block, "expert", self.core)

    def double_small(self, held, me, step):
        pairs = [(e, e ^ step) for e in range(self.devices)]
        other = lax.ppermute(held, "expert", pairs)
        upper = (me // step) % 2 == 1
        return jnp.where(upper, jnp.concatenate([other, held]), jnp.concatenate([held, other]))


def after(value, *others):
    return lax.optimization_barrier((value,) + others)[0]


def after_all(values, *others):
    return lax.optimization_barrier((list(values),) + others)[0]


def hold(*values):
    return list(lax.optimization_barrier(values))


def swap_tensor(block):
    return lax.ppermute(block, "tensor", [(0, 1), (1, 0)])


def sum_tensor(part):
    own = part.astype(bf16)
    return own.astype(f32) + swap_tensor(own).astype(f32)


def make_local(ring):
    devices, chips = ring.devices, ring.chips

    def local(
        tokens_in,
        cotangent,
        norm_gains,
        qkv_weight,
        qkv_bias,
        out_weight,
        router_weight,
        shared_gate,
        shared_in,
        shared_out,
        expert_in,
        expert_out,
        expert_ids,
        prefix_len,
    ):
        me = lax.axis_index("expert")
        core = me % 2
        half = lax.axis_index("tensor")
        length, width = tokens_in.shape
        top_count = expert_ids.shape[1]
        experts = router_weight.shape[1]
        capacity = length * top_count * 3 // (2 * experts)
        rows_dev = qkv_weight.shape[0]
        heads_t = qkv_bias.shape[1]
        heads = heads_t // 2
        hd_dev = qkv_bias.shape[2]
        head_size = hd_dev * devices
        half_cols = heads * head_size
        score_scale = head_size ** (-0.5)
        chip_of = jnp.asarray(ring.chip_table)[me]
        seq_of = jnp.asarray(ring.seq_table)[me]
        seq_inv = jnp.asarray(ring.seq_inverse)[me]

        pieces = [
            norm_gains.reshape(-1),
            qkv_bias.reshape(-1),
            router_weight.reshape(-1),
            shared_gate.reshape(-1),
            expert_ids.T.astype(bf16).reshape(-1),
            prefix_len.astype(bf16).reshape(-1),
        ]
        sizes = [p.shape[0] for p in pieces]
        total = sum(sizes)
        padded = -(-total // 1024) * 1024
        small = jnp.concatenate(pieces + [jnp.zeros((padded - total,), bf16)])
        swap_core = ring.swap_core

        def cost(flops, moved):
            return pl.CostEstimate(
                flops=flops // 64, bytes_accessed=moved // 64, transcendentals=0
            )

        depth = 2 * rows_dev

        def by_core(own, other, axis):
            return jnp.where(
                core == 0,
                jnp.concatenate([own, other], axis=axis),
                jnp.concatenate([other, own], axis=axis),
            )

        def halves(array, axis):
            size = array.shape[axis] // 2
            own = lax.dynamic_slice_in_dim(array, core * size, size, axis)
            return own, lax.dynamic_slice_in_dim(array, (1 - core) * size, size, axis)

        qkv_own, qkv_other = halves(qkv_weight.transpose(1, 0, 2), 2)
        out_own, out_other = halves(out_weight, 0)
        own = jnp.concatenate([qkv_own, out_own.T[None]], axis=0)
        other = jnp.concatenate([qkv_other, out_other.T[None]], axis=0)
        block = by_core(own, ring.swap_core(other), 1).reshape(4 * depth, half_cols)
        half_length = length // 2
        steps = chips // 2
        up_zero = lax.dynamic_slice_in_dim(cotangent, half * half_length, half_length, 0)
        small_all = small[None]
        for k in range(devices.bit_length() - 1):
            small_all = ring.double_small(small_all, me, 1 << k)
        pair = ring.step(block)
        attn_w = [block]
        for k in range(1, steps + 1):
            if k > 1:
                pair = ring.step(*pair, last=k == steps)
            attn_w += pair

        cuts = np.cumsum([0] + sizes)
        found = [small_all[:, cuts[i] : cuts[i + 1]] for i in range(len(sizes))]
        gains_f = (
            found[0].reshape(devices, 2, rows_dev).transpose(1, 0, 2).reshape(2, width).astype(f32)
        )
        bias_all = (
            found[1].reshape(devices, 3, heads_t, hd_dev).transpose(1, 2, 0, 3)
            .reshape(3, 2, half_cols)
        )
        bias = lax.dynamic_index_in_dim(bias_all, core, 1, keepdims=False).astype(f32)
        router_w = found[2].reshape(width, experts)
        gate_vec = found[3].reshape(width)
        ids_all = found[4].reshape(devices, top_count, length).astype(jnp.int32)
        prefix_all = found[5].reshape(devices).astype(jnp.int32)
        prefix_pair = jnp.stack([prefix_all[me], prefix_all[me ^ 1]])


        match = jnp.any(ids_all[seq_of] == me, axis=1)
        triangle = jnp.asarray(np.triu(np.ones((length, length), np.float32)), bf16)
        rank = jnp.where(match, mm(match.astype(bf16), triangle) - 1.0, no_slot)
        rank = rank.reshape(chips, 2, length)
        row_aux = jnp.concatenate([rank, jnp.zeros((chips, 6, length), f32)], axis=1)
        ids_ring = ids_all[seq_of].reshape(chips, 2 * top_count, length).astype(f32)
        blank = jnp.zeros((chips, -(2 + 2 * top_count) % 8, length), f32)
        col_aux = jnp.concatenate([rank, ids_ring, blank], axis=1).transpose(0, 2, 1)
        router_all = jnp.concatenate(
            [
                router_w,
                gate_vec[:, None],
                jnp.zeros((width, -(experts + 1) % 128), bf16),
            ],
            axis=1,
        )

        units = shared_out.shape[0]
        unit_chip = units // chips
        sh_send = jnp.concatenate(
            [
                shared_in.transpose(1, 2, 0).reshape(2, chips, unit_chip, rows_dev),
                shared_out.reshape(1, chips, unit_chip, rows_dev),
            ],
            axis=0,
        ).transpose(1, 0, 2, 3)
        sh_send = sh_send.reshape(chips, 3 * unit_chip, rows_dev)

        up_cross = {0: swap_tensor(up_zero)}
        attn_w[-4:-2], sh_send, up_cross[0] = hold(attn_w[-4:-2], sh_send, up_cross[0])
        up_next = ring.step(after(up_zero, *attn_w[-2:]))
        same_core = [[2 * i + c for i in range(chips)] for c in range(2)]
        inputs = tokens_in.astype(f32)
        first_b = rms_norm(inputs, gains_f[0]).astype(bf16)
        first_o = ring.swap_core(first_b)
        cosine, sine = rotary_tables(length, head_size)
        pair_cols = jax.ShapeDtypeStruct((2 * length, half_cols), bf16)
        chip_arg = chip_of.astype(jnp.int32)

        query, key, value, mixed = pl.pallas_call(
            functools.partial(attend_kernel, chips + 1, heads, score_scale),
            out_shape=[pair_cols] * 4,
            in_specs=[in_smem] * 2 + [in_vmem] * 5 + [in_any] * (chips + 1),
            out_specs=[in_vmem] * 4,
            scratch_shapes=[
                pltpu.VMEM((3, width, half_cols), bf16),
                pltpu.SemaphoreType.DMA((3 * chips,)),
            ],
            compiler_params=params(),
            cost_estimate=cost(2 * 2 * length * width * 3 * half_cols, 12 * 1024 * 1024),
            name="attend",
        )(chip_arg, prefix_pair, first_b, first_o, bias.reshape(1, -1), cosine, sine, *attn_w)
        sh_mine = lax.all_to_all(
            after(sh_send, *attn_w[-2:]),
            "expert",
            split_axis=0,
            concat_axis=0,
            tiled=True,
            axis_index_groups=same_core,
        )
        attn_own, attn_give = pl.pallas_call(
            functools.partial(project_kernel, chips + 1),
            out_shape=[
                jax.ShapeDtypeStruct((length, width), f32),
                jax.ShapeDtypeStruct((length, width), bf16),
            ],
            in_specs=[in_smem, in_vmem] + [in_any] * (chips + 1),
            out_specs=[in_vmem] * 2,
            scratch_shapes=[
                pltpu.VMEM((1, width, half_cols), bf16),
                pltpu.SemaphoreType.DMA((chips,)),
            ],
            compiler_params=params(),
            cost_estimate=cost(2 * 2 * length * width * half_cols, 6 * 1024 * 1024),
            name="project",
        )(chip_arg, mixed, *attn_w)
        attn_own = (attn_own + ring.swap_core(attn_give).astype(f32)).astype(bf16)
        attn_got = swap_tensor(attn_own)
        attn_got, sh_mine, up_next = hold(attn_got, sh_mine, up_next)
        attn_out = attn_own.astype(f32) + attn_got.astype(f32)
        residual = inputs + attn_out
        second_b = rms_norm(residual, gains_f[1]).astype(bf16)

        second_b, up_next, sh_mine, row_aux, col_aux, router_all = hold(
            second_b, up_next, sh_mine, row_aux, col_aux, router_all
        )
        pair = {
            0: [
                jnp.concatenate([second_b, up_next[0]], axis=0),
                jnp.concatenate([up_next[1], second_b], axis=0),
            ]
        }
        pair_o = {0: [swap_core(pair[0][0]), swap_core(up_next[1])]}
        up_zero_o = swap_core(up_zero)
        cross_o = {}

        logits = mm(second_b, router_w)
        expert_range = jnp.arange(experts, dtype=jnp.int32)
        route_match = expert_ids[:, :, None] == expert_range[None, None, :]
        chosen = jnp.sum(jnp.where(route_match, logits[:, None, :], 0.0), axis=-1)
        gate_weights = jax.nn.softmax(chosen, axis=-1)
        shared_sigma = jax.nn.sigmoid(
            jnp.sum(second_b.astype(f32) * gate_vec.astype(f32)[None], axis=-1)
        )
        gate_dense = jnp.sum(jnp.where(route_match, gate_weights[:, :, None], 0.0), axis=1)
        ex_in = expert_in[0].transpose(1, 2, 0)
        ex_out = expert_out[0]
        part_units = ex_out.shape[0]
        sizes = (length, width, capacity, part_units, unit_chip, experts, top_count)
        half_arg = jnp.stack([half, me]).astype(jnp.int32)
        core_arg = core.astype(jnp.int32).reshape(1)

        sh_w = pl.pallas_call(
            spread_kernel,
            out_shape=jax.ShapeDtypeStruct((3, unit_chip, width), bf16),
            in_specs=[in_smem, in_vmem, in_vmem],
            out_specs=in_vmem,
            compiler_params=params(),
            cost_estimate=cost(0, 16 * 1024 * 1024),
            name="spread",
        )(core_arg, sh_mine, swap_core(sh_mine))

        def row_pieces(found, own_zero, g):
            full, part = length, length // 2
            if g == 0:
                return [[(own_zero, (0, full, 0, 0))]]
            if g == steps:
                ahead, back = found[g]
                return [[(ahead, (0, part, 0, 0)), (back, (0, part, part, part))]]
            return [[(found[g][0], (0, full, 0, 0))], [(found[g][1], (half_length, full, 0, 0))]]

        def up_pieces(found, own_zero, crossed, g):
            whole, part = half_length, half_length // 2
            if g == 0:
                straight = [[(own_zero, (0, whole, 0, whole))]]
            elif g == steps:
                ahead, back = found[g - 1]
                straight = [
                    [
                        (ahead, (length, part, 0, whole)),
                        (back, (part, part, part, whole + part)),
                    ]
                ]
            else:
                ahead, back = found[g - 1]
                straight = [
                    [(ahead, (length, whole, 0, whole))],
                    [(back, (0, whole, 0, whole))],
                ]
            for j, chip in enumerate(straight):
                chip.append((crossed, (j * whole, whole, whole, 0)))
            return straight

        kept = None
        own_terms, give_terms, dot_rows = {}, {}, []
        terms, crossed = {}, {}

        def receive(g):
            index, count = (0, 1) if g == 0 else (2 * g - 1, 1 if g == steps else 2)
            crossing = []
            for j in range(count):
                own, got, at = own_terms[g][j], give_got[g], 2 * j * length
                parts = []
                for i in range(4):
                    lo, hi = i * half_length, (i + 1) * half_length
                    parts.append([own[lo:hi], got[at + lo : at + hi]])
                terms[ring.offsets[index + j]] = [parts[0], parts[2]]
                crossing.append(ring.add_up(parts[1]).astype(bf16))
                out_gives.setdefault(g, []).append(parts[3])
            return crossing[0] if count == 1 else jnp.concatenate(crossing, axis=0)

        def receive_outs(g):
            parts = [ring.add_up(part).astype(bf16) for part in out_gives[g]]
            return parts[0] if len(parts) == 1 else jnp.concatenate(parts, axis=0)

        def place_crossed(which, g, got):
            index, count = (0, 1) if g == 0 else (2 * g - 1, 1 if g == steps else 2)
            for j in range(count):
                crossed[which, ring.offsets[index + j]] = got[
                    j * half_length : (j + 1) * half_length
                ]

        out_gives, give_got = {}, {}
        for k in range(1, steps + 2):
            g = k - 1
            now = []
            if k <= steps:
                ahead, back = pair[g]
                cut = half_length // 2
                if k == steps:
                    ahead, back = ahead[: length // 2], back[half_length + length // 2 :]
                pair[k] = ring.send_pair(ahead, back)
                first, second = pair[g][0][length:], pair[g][1][:half_length]
                if k == steps:
                    first, second = first[:cut], second[cut:]
                up_cross[k] = swap_tensor(jnp.concatenate([first, second], axis=0))
                now = [pair[k], up_cross[k]]
            if g > 0:
                pair_o[g] = [swap_core(x) for x in pair[g]]
            if g > 0:
                cross_o[g] = swap_core(after(up_cross[g], *pair_o[g]))
            else:
                cross_o[g] = swap_core(up_cross[g])
            if g >= 1:
                give_got[g - 1] = swap_core(after(give_terms[g - 1], cross_o[g]))
                now.append(give_got[g - 1])
            if g >= 3:
                grads = receive(g - 2)
                grads, pair_o[g] = hold(grads, pair_o[g])
                now.append(swap_tensor(grads))
            pieces = (
                row_pieces(pair, second_b, g)
                + row_pieces(pair_o, pair_o[0][0], g)
                + up_pieces(pair, up_zero, up_cross[g], g)
                + up_pieces(pair_o, up_zero_o, cross_o[g], g)
            )
            span = 1 if g in (0, steps) else 2
            kept, own_terms[g], give_terms[g], rows = moe_call(
                0 if g == 0 else 2 * g - 1,
                span,
                sizes,
                chips,
                pieces,
                half_arg,
                row_aux,
                col_aux,
                router_all,
                (ex_in, ex_out, sh_w),
                kept,
            )
            dot_rows.append(rows)
            *now, dot_rows[-1], give_terms[g] = hold(*now, rows, give_terms[g])
            if k <= steps:
                pair[k], up_cross[k], *now = now
            if g >= 1:
                give_got[g - 1] = now[0]
            if g >= 3:
                place_crossed(0, g - 2, now[1])

        rows_all, slots_all, hidden_all, gu_all, tok_all, y_all, s_hidden_all, s_gu_all = kept
        give_got[steps] = swap_core(give_terms[steps])
        near_far = receive(steps - 1)
        grads = receive(steps)
        s_hidden_all, grads = hold(s_hidden_all, grads)
        far = ring.offsets[-1]
        grads = swap_tensor(grads)
        sh_grad = pl.pallas_call(
            shared_grad_kernel,
            grid=(chips,),
            out_shape=jax.ShapeDtypeStruct((2, chips, 3 * unit_chip, rows_dev), bf16),
            in_specs=[
                pl.BlockSpec((chips * length, depth), lambda n: (0, n)),
                pl.BlockSpec((chips * length, depth), lambda n: (0, n)),
                pl.BlockSpec((chips * length, unit_chip), lambda n: (0, 0)),
                pl.BlockSpec((2, chips * length, unit_chip), lambda n: (0, 0, 0)),
            ],
            out_specs=pl.BlockSpec((2, 1, 3 * unit_chip, rows_dev), lambda n: (0, n, 0, 0)),
            compiler_params=params(),
            cost_estimate=cost(2 * chips * length * width * 3 * unit_chip, 26 * 1024 * 1024),
            name="shared_grad",
        )(tok_all, y_all, s_hidden_all, s_gu_all)
        near_got = swap_tensor(near_far)
        grads, sh_grad = hold(grads, sh_grad)
        place_crossed(0, steps, grads)

        def ring_terms(which, o):
            return [*terms[o][which], crossed[which, o]]

        zero_got = swap_tensor(after(receive(0), grads))
        sending = ring.reduce_first(ring_terms(0, far))
        own, other = halves(sh_grad, 0)
        sh_got = swap_core(other)
        gu_all = after(gu_all, grads)
        sh_sum = (own.astype(f32) + sh_got.astype(f32)).astype(bf16)[0]
        expert_in_grad = mm(gu_all, rows_all, 1, 0).transpose(2, 0, 1)[None]
        near_got, zero_got, sending, sh_sum, expert_in_grad = hold(
            near_got, zero_got, sending, sh_sum, expert_in_grad
        )
        place_crossed(0, 0, zero_got)
        place_crossed(0, steps - 1, near_got)
        out_sent = {}
        for k in range(steps - 1, 0, -1):
            send = ring.reduce_terms(
                ring_terms(0, k), ring_terms(0, -k), sending, k == steps - 1
            )
            now = []
            if k == steps - 1:
                hidden_all, send, far_outs = hold(hidden_all, send, receive_outs(steps))
                expert_out_grad = mm(hidden_all, slots_all, 0, 0)[None]
                out_sent[steps] = swap_tensor(far_outs)
                dots = jnp.concatenate(after_all(dot_rows, send[0]), axis=0)
                sdots = jnp.concatenate([dots[:, 2:3], jnp.zeros_like(dots[:, 2:3])], axis=1)
                dot_send = jnp.stack([dots[:, :2], sdots], axis=2)
                dot_send = dot_send.reshape(devices, 2, length)[seq_inv]
                dot_got = lax.all_to_all(
                    dot_send, "expert", split_axis=0, concat_axis=0, tiled=True
                )
                dot_got = jnp.concatenate(
                    [dot_got[:, 0], jnp.sum(dot_got[:, 1], axis=0)[None]], axis=0
                )
                now = [out_sent[steps], dot_got, expert_out_grad]
            sending = ring.send_pair(*send)
            sending, *now = hold(sending, *now)
            if k == steps - 1:
                out_sent[steps], dot_got, expert_out_grad = now
        place_crossed(1, steps, out_sent[steps])
        dot_got = dot_got + swap_tensor(dot_got)
        second_half = ring.add_up([*ring_terms(0, 0), *sending]).astype(bf16)
        sh_back = lax.all_to_all(
            after(sh_sum, second_half),
            "expert",
            split_axis=0,
            concat_axis=0,
            tiled=True,
            axis_index_groups=same_core,
        )
        second_got = swap_tensor(second_half)
        out_sending = ring.reduce_first(ring_terms(1, far))
        second_got, out_sending = hold(second_got, out_sending)

        def both_halves(own, other):
            return jnp.where(
                half == 0,
                jnp.concatenate([own, other], axis=0),
                jnp.concatenate([other, own], axis=0),
            )

        second_part = both_halves(second_half, second_got)

        gate_grad_dense, sigma_grad = dot_got[:experts].T, dot_got[experts]
        row_term = jnp.sum(gate_dense * gate_grad_dense, axis=-1, keepdims=True)
        logit_grad = (gate_dense * (gate_grad_dense - row_term)).astype(bf16)
        gate_logit_grad = sigma_grad * shared_sigma * (1.0 - shared_sigma)

        second_grad = second_part.astype(f32)
        second_grad = second_grad + mm(logit_grad, router_w, 1, 1)
        second_grad = second_grad + gate_logit_grad[:, None] * gate_vec.astype(f32)[None]
        upstream = cotangent.astype(f32)
        residual_norm_grad, gain_two_grad = jax.vjp(rms_norm, residual, gains_f[1])[1](second_grad)
        residual_grad = upstream + residual_norm_grad
        attn_grad = residual_grad.astype(bf16)
        attn_grad_o = ring.swap_core(attn_grad)

        def by_chip(left, right, wanted=tuple(ring.offsets)):
            return {
                offset: [
                    mm(lax.dynamic_slice_in_dim(left, chip_of[i] * depth, depth, 1), right, 0, 0)
                ]
                for i, offset in enumerate(ring.offsets)
                if offset in wanted
            }

        proj_grad, bias_grad = pl.pallas_call(
            functools.partial(attend_back_kernel, chips + 1, heads, score_scale),
            out_shape=[
                jax.ShapeDtypeStruct((2 * length, 3 * half_cols), bf16),
                jax.ShapeDtypeStruct((1, 3 * half_cols), f32),
            ],
            in_specs=[in_smem] * 2 + [in_vmem] * 7 + [in_any] * (chips + 1),
            out_specs=[in_vmem] * 2,
            scratch_shapes=[
                pltpu.VMEM((1, width, half_cols), bf16),
                pltpu.SemaphoreType.DMA((chips,)),
            ],
            compiler_params=params(),
            cost_estimate=cost(2 * 2 * length * width * half_cols * 2, 8 * 1024 * 1024),
            name="attend_back",
        )(
            chip_arg,
            prefix_pair,
            attn_grad,
            attn_grad_o,
            query,
            key,
            value,
            cosine,
            sine,
            *attn_w,
        )
        crossing = swap_tensor(receive_outs(steps - 1))
        first_pair = jnp.concatenate([first_b, first_o], axis=0)
        attn_grad_pair = jnp.concatenate([attn_grad, attn_grad_o], axis=0)
        out_parts = by_chip(attn_grad_pair, mixed)
        far_out = out_parts[steps][0].astype(bf16)
        far_out, proj_grad, sh_back = hold(far_out, proj_grad, sh_back)
        far_part = by_chip(first_pair, proj_grad, [steps])[steps][0].astype(bf16)
        far_part = jnp.concatenate([far_part, far_out], axis=1)
        cut = depth // 2
        proj_grad, ahead, back = hold(proj_grad, far_part[:cut], far_part[cut:])
        going = ring.send_pair(ahead, back)
        qkv_parts = by_chip(first_pair, proj_grad, ring.offsets[:-1])
        attn_parts = {
            o: [
                jnp.concatenate(
                    [qkv_parts[o][0].astype(bf16), out_parts[o][0].astype(bf16)], axis=1
                )
            ]
            for o in qkv_parts
        }
        bias_grad = bias_grad[0]
        def send_outs(k, going):
            return ring.send_pair(
                *ring.reduce_terms(ring_terms(1, k), ring_terms(1, -k), going, k == steps - 1)
            )

        second_f = second_b.astype(f32)
        router_part = mm(second_b, logit_grad, 0, 0)
        shared_gate_part = jnp.sum(gate_logit_grad[:, None] * second_f, axis=0)
        early = jnp.concatenate(
            [router_part, shared_gate_part[:, None], gain_two_grad[:, None]], axis=1
        ).reshape(devices, rows_dev * (experts + 2))

        def send_next(k, going):
            return ring.send_pair(
                *ring.reduce_terms(attn_parts[k], attn_parts[-k], going, k == steps - 1)
            )

        pieces = [attn_parts[o][0] for o in ring.offsets[:-1]]
        going, crossing, proj_grad, pieces = hold(going, crossing, proj_grad, pieces)
        for o, piece in zip(ring.offsets[:-1], pieces, strict=True):
            attn_parts[o] = [piece]
        place_crossed(1, steps - 1, crossing)
        send = ring.reduce_terms(
            attn_parts[steps - 1], attn_parts[1 - steps], going, steps > 1
        )
        proj_grad, *send = hold(proj_grad, *send)
        first_own, first_give = pl.pallas_call(
            functools.partial(project_back_kernel, chips + 1),
            out_shape=[
                jax.ShapeDtypeStruct((length, width), f32),
                jax.ShapeDtypeStruct((length, width), bf16),
            ],
            in_specs=[in_smem, in_vmem] + [in_any] * (chips + 1),
            out_specs=[in_vmem] * 2,
            scratch_shapes=[
                pltpu.VMEM((3, width, half_cols), bf16),
                pltpu.SemaphoreType.DMA((3 * chips,)),
            ],
            compiler_params=params(),
            cost_estimate=cost(2 * 2 * length * width * 3 * half_cols, 12 * 1024 * 1024),
            name="project_back",
        )(chip_arg, proj_grad, *attn_w)
        first_own = (first_own + swap_core(first_give).astype(f32)).astype(bf16)
        for k in range(steps - 1, -1, -1):
            if k > 0:
                going = ring.send_pair(*send) if k == steps - 1 else send_next(k, going)
                out_sending = send_outs(k, out_sending)
            now = []
            if k > 0:
                now.append(swap_tensor(receive_outs(k - 1)))
            if k == steps - 2:
                now.append(swap_tensor(first_own))
            if k == 0:
                res_half = lax.dynamic_slice_in_dim(residual, half * half_length, half_length, 0)
                out_half = ring.add_up([res_half, *ring_terms(1, 0), *out_sending]).astype(bf16)
                output = both_halves(out_half, swap_tensor(out_half))
                break
            if k == 2:
                now.append(sh_back)
            going, out_sending, *now = hold(going, out_sending, *now)
            place_crossed(1, k - 1, now[0])
            if k == 2:
                sh_back = now[-1]
            if k == steps - 2:
                first_got = now[1]
        attn_grads = ring.add_up([*attn_parts[0], *going])
        first_grad = first_own.astype(f32) + first_got.astype(f32)
        input_norm_grad, gain_one_grad = jax.vjp(rms_norm, inputs, gains_f[0])[1](first_grad)
        input_grad = (residual_grad + input_norm_grad).astype(bf16)

        own, other = halves(attn_grads.astype(bf16), 0)
        both = by_core(
            own.reshape(rows_dev, 4, half_cols),
            swap_core(other).reshape(rows_dev, 4, half_cols),
            2,
        ).astype(f32)
        qkv_weight_grad = both[:, :3]
        out_weight_grad = both[:, 3].T

        sh_back = sh_back.reshape(chips, 3, unit_chip, rows_dev).astype(f32)
        shared_in_grad = sh_back[:, :2].transpose(3, 1, 0, 2).reshape(rows_dev, 2, units)
        shared_out_grad = sh_back[:, 2].reshape(units, rows_dev)

        bias_send = bias_grad.reshape(3 * heads, devices, hd_dev).transpose(1, 0, 2)
        late = jnp.concatenate(
            [gain_one_grad.reshape(devices, rows_dev), bias_send.reshape(devices, -1), early],
            axis=1,
        )
        late = lax.all_to_all(late, "expert", split_axis=0, concat_axis=0, tiled=True)
        gain_one = jnp.sum(late[:, :rows_dev], axis=0)
        count = 3 * heads * hd_dev
        early = late[:, rows_dev + count :]
        early = jnp.sum(early, axis=0).reshape(rows_dev, experts + 2)
        router_grad, shared_gate_grad = early[:, :experts], early[:, experts]
        bias_got = late[:, rows_dev : rows_dev + count].reshape(chips, 2, 3, heads, hd_dev)
        bias_got = jnp.sum(bias_got, axis=0)
        qkv_bias_grad = bias_got.transpose(1, 0, 2, 3).reshape(3, heads_t, hd_dev)
        gains_grad = jnp.stack([gain_one, early[:, experts + 1]], axis=0)

        return (
            output,
            input_grad,
            gains_grad,
            qkv_weight_grad,
            qkv_bias_grad,
            out_weight_grad,
            router_grad,
            shared_gate_grad,
            shared_in_grad,
            shared_out_grad,
            expert_in_grad,
            expert_out_grad,
        )

    return local


def solution(mesh):
    ring = Ring(mesh.shape["expert"])
    return jax.shard_map(
        make_local(ring),
        mesh=mesh,
        in_specs=(
            P("expert", None),
            P("expert", None),
            P(None, "expert"),
            P("expert", None, "tensor"),
            P(None, "tensor", "expert"),
            P("tensor", "expert"),
            P("expert", None),
            P("expert"),
            P("expert", None, "tensor"),
            P("tensor", "expert"),
            P("expert", None, None, "tensor"),
            P("expert", "tensor", None),
            P("expert", None),
            P("expert"),
        ),
        out_specs=(
            P("expert", None),
            P("expert", None),
            P(None, "expert"),
            P("expert", None, "tensor"),
            P(None, "tensor", "expert"),
            P("tensor", "expert"),
            P("expert", None),
            P("expert"),
            P("expert", None, "tensor"),
            P("tensor", "expert"),
            P("expert", None, None, "tensor"),
            P("expert", "tensor", None),
        ),
        check_vma=False,
    )
```

```python
import functools

import jax
import jax.numpy as jnp
import numpy as np
from jax import lax
from jax.experimental import pallas as pl
from jax.experimental.pallas import tpu as pltpu
from jax.sharding import PartitionSpec as P

eps = 1e-06
theta_base = 1000000.0
neg_large = -1e30
no_slot = -100000.0
bf16 = jnp.bfloat16
f32 = jnp.float32
in_vmem = pl.BlockSpec(memory_space=pltpu.VMEM)
in_smem = pl.BlockSpec(memory_space=pltpu.SMEM)
in_any = pl.BlockSpec(memory_space=pl.ANY)


def rms_norm(values, gain_row):
    factor = lax.rsqrt(jnp.mean(values * values, axis=-1, keepdims=True) + eps)
    return values * factor * gain_row


def rotary_tables(length, head_size):
    half_size = head_size // 2
    frequency = np.float32(theta_base) ** (
        -(np.arange(half_size, dtype=np.float32) * np.float32(2.0)) / np.float32(head_size)
    )
    angles = np.arange(length, dtype=np.float32)[:, None] * frequency[None, :].astype(np.float32)
    cosine = np.concatenate([np.cos(angles), np.cos(angles)], axis=-1)
    sine = np.concatenate([-np.sin(angles), np.sin(angles)], axis=-1)
    return jnp.asarray(cosine, f32), jnp.asarray(sine, f32)


def chip_ring(chips):
    columns = chips // 4
    if chips % 4 or columns < 2 or columns % 2:
        return list(range(chips))
    walk = [(0, 0)]
    for column in range(columns):
        rows = range(1, 4) if column % 2 == 0 else range(3, 0, -1)
        walk += [(row, column) for row in rows]
    walk += [(0, column) for column in range(columns - 1, 0, -1)]
    return [row * columns + column for row, column in walk]


def mm(left, right, contract_left=1, contract_right=0):
    return lax.dot_general(
        left,
        right,
        (((contract_left,), (contract_right,)), ((), ())),
        preferred_element_type=f32,
    )


def nt(left, right):
    return mm(left, right, 1, 1)


def tiles(total, size):
    return [(lo, min(size, total - lo)) for lo in range(0, total, size)]


def params(mebibytes=56):
    return pltpu.CompilerParams(vmem_limit_bytes=mebibytes * 1024 * 1024)


def half_turn(values):
    return pltpu.roll(values, values.shape[1] // 2, 1)


def masked(scores, prefix_cut):
    length = scores.shape[0]
    row = lax.broadcasted_iota(jnp.int32, (length, length), 0)
    col = lax.broadcasted_iota(jnp.int32, (length, length), 1)
    return jnp.where((col <= row) | (col < prefix_cut), scores, neg_large)


def softmax_rows(scores):
    weights = jnp.exp(scores - jnp.max(scores, axis=-1, keepdims=True))
    return weights / jnp.sum(weights, axis=-1, keepdims=True)


def load_blocks(chip_ref, blocks, scratch, sem, first, last):
    whole = len(blocks) - 2
    depth = blocks[0].shape[0] // 4
    copies = []
    for i in range(whole + 1):
        start = pl.multiple_of(chip_ref[i] * depth, depth)
        for c in range(first, last):
            block, at = (blocks[i], c) if i < whole else (blocks[whole + c // 2], c % 2)
            copies.append(
                pltpu.make_async_copy(
                    block.at[pl.ds(at * depth, depth)],
                    scratch.at[c - first, pl.ds(start, depth)],
                    sem.at[len(copies)],
                )
            )
    for copy in copies:
        copy.start()
    return copies


def attend_kernel(count, heads, scale, *refs):
    chip_ref, prefix_ref, own, other, bias, cosine, sine = refs[:7]
    blocks = refs[7 : 7 + count]
    query, key, value, mixed, weight, sem = refs[7 + count :]
    copies = load_blocks(chip_ref, blocks, weight, sem, 0, 3)
    length, head_size = cosine.shape
    columns = heads * head_size
    for copy in copies:
        copy.wait()
    for c, out in enumerate((query, key, value)):
        for b, rows in enumerate((own, other)):
            for lo, size in tiles(columns, 2 * head_size):
                part = mm(rows[...], weight[c, :, lo : lo + size])
                part = part + bias[:, c * columns + lo : c * columns + lo + size]
                for at in range(0, size, head_size):
                    one = part[:, at : at + head_size]
                    if c < 2:
                        one = one * cosine[...] + half_turn(one) * sine[...]
                    out[b * length : (b + 1) * length, lo + at : lo + at + head_size] = one.astype(
                        bf16
                    )
    for b in range(2):
        rows = slice(b * length, (b + 1) * length)
        for h in range(heads):
            cols = slice(h * head_size, (h + 1) * head_size)
            scores = masked(nt(query[rows, cols], key[rows, cols]) * scale, prefix_ref[b])
            probs = softmax_rows(scores).astype(bf16)
            mixed[rows, cols] = mm(probs, value[rows, cols]).astype(bf16)


def project_kernel(count, *refs):
    chip_ref, mixed = refs[:2]
    blocks = refs[2 : 2 + count]
    own, other, weight, sem = refs[2 + count :]
    copies = load_blocks(chip_ref, blocks, weight, sem, 3, 4)
    for copy in copies:
        copy.wait()
    length, width = own.shape
    for lo, size in tiles(width, 512):
        part = nt(mixed[...], weight[0, lo : lo + size, :])
        own[:, lo : lo + size] = part[:length].astype(own.dtype)
        other[:, lo : lo + size] = part[length:].astype(other.dtype)


def attend_back_kernel(count, heads, scale, *refs):
    chip_ref, prefix_ref, own, other, query, key, value, cosine, sine = refs[:9]
    blocks = refs[9 : 9 + count]
    grad, bias, weight, sem = refs[9 + count :]
    copies = load_blocks(chip_ref, blocks, weight, sem, 3, 4)
    length, head_size = cosine.shape
    columns = heads * head_size
    for copy in copies:
        copy.wait()
    for b, up in enumerate((own, other)):
        rows = slice(b * length, (b + 1) * length)
        mixed_grad = mm(up[...], weight[0]).astype(bf16)
        for h in range(heads):
            cols = slice(h * head_size, (h + 1) * head_size)
            q, k, v = query[rows, cols], key[rows, cols], value[rows, cols]
            up_head = mixed_grad[:, cols]
            probs = softmax_rows(masked(nt(q, k) * scale, prefix_ref[b]))
            prob_grad = nt(up_head, v)
            row_term = jnp.sum(probs * prob_grad, axis=-1, keepdims=True)
            score_grad = (probs * (prob_grad - row_term)).astype(bf16)
            q_grad = mm(score_grad, k) * scale
            k_grad = mm(score_grad, q, 0, 0) * scale
            v_grad = mm(probs.astype(bf16), up_head, 0, 0)
            for c, one in enumerate((q_grad, k_grad, v_grad)):
                if c < 2:
                    one = one * cosine[...] - half_turn(one) * sine[...]
                one = one.astype(bf16)
                at = slice(c * columns + h * head_size, c * columns + (h + 1) * head_size)
                grad[rows, at] = one
                column_sum = jnp.sum(one.astype(f32), axis=0, keepdims=True)
                bias[:, at] = column_sum if b == 0 else bias[:, at] + column_sum


def project_back_kernel(count, *refs):
    chip_ref, grad = refs[:2]
    blocks = refs[2 : 2 + count]
    own, other, weight, sem = refs[2 + count :]
    copies = load_blocks(chip_ref, blocks, weight, sem, 0, 3)
    for copy in copies:
        copy.wait()
    length, width = own.shape
    columns = grad.shape[1] // 3
    for lo, size in tiles(width, 512):
        part = nt(grad[:, :columns], weight[0, lo : lo + size, :])
        for c in range(1, 3):
            part = part + nt(grad[:, c * columns : (c + 1) * columns], weight[c, lo : lo + size, :])
        own[:, lo : lo + size] = part[:length].astype(own.dtype)
        other[:, lo : lo + size] = part[length:].astype(other.dtype)


def moe_kernel(index, span, first, plan, sizes, *refs):
    length, width, capacity, units, shared_units, experts, top_count = sizes
    count = sum(len(p) for p in plan)
    own_rows, slab = span * length, 2 * span * capacity
    half_ref, row_hbm, col_hbm, router_hbm = refs[:4]
    given = refs[4 : 4 + count]
    in_hbm, out_hbm, shared_hbm = refs[4 + count : 7 + count]
    rest = refs[7 + count + (0 if first else 8) :]
    kept, owns, give, dots = rest[:8], rest[8 : 8 + span], rest[8 + span], rest[9 + span]
    tok, up, rows, up_rows, slots, hidden, gu, y_grad, s_hidden, s_gu, made_out = rest[
        10 + span : 21 + span
    ]
    w_in, w_out, w_sh, row_ref, col_ref, router = rest[21 + span : 27 + span]
    load_sem, weight_sem, out_sem, keep_sem = rest[27 + span :]
    wide = min(512, width)
    columns = tiles(width, wide)

    tables = [
        pltpu.make_async_copy(a, b, weight_sem.at[3 + i])
        for i, (a, b) in enumerate(
            (
                (row_hbm.at[pl.ds(index, span)], row_ref),
                (col_hbm.at[pl.ds(index, span)], col_ref),
                (router_hbm, router),
            )
        )
    ]
    for copy in tables:
        copy.start()

    loads = []
    for n, (lo, size_cols) in enumerate(columns):
        cols, number = slice(lo, lo + size_cols), 0
        loads.append([])
        for which, pieces in enumerate(plan):
            target, at = (tok, up)[which // (2 * span)], which % (2 * span) * length
            for first_row, size, start_zero, start_one in pieces:
                start = start_zero + half_ref[0] * (start_one - start_zero)
                start = pl.multiple_of(start + at, 16)
                copy = pltpu.make_async_copy(
                    given[number].at[first_row : first_row + size, cols],
                    target.at[pl.ds(start, size), cols],
                    load_sem.at[n, number],
                )
                copy.start()
                loads[-1].append(copy)
                number += 1

    weights = [
        pltpu.make_async_copy(a, b, weight_sem.at[i])
        for i, (a, b) in enumerate(
            (
                (shared_hbm, w_sh),
                (in_hbm, w_in),
                (out_hbm, w_out),
            )
        )
    ]
    for copy in weights:
        copy.start()
    for copy in tables:
        copy.wait()

    def keep(slot, source):
        target = kept[slot]
        size = source.shape[-2]
        first_row = index * (size // span)
        if len(target.shape) == 3:
            target = target.at[:, pl.ds(first_row, size)]
        else:
            target = target.at[pl.ds(first_row, size)]
        copy = pltpu.make_async_copy(source, target, keep_sem.at[slot])
        copy.start()
        return copy

    slot = lax.broadcasted_iota(jnp.int32, (capacity, length), 0).astype(f32)
    lane = lax.broadcasted_iota(jnp.int32, (length, 2 * capacity), 1).astype(f32)
    picks, ones, places = [], [], []
    for j in range(span):
        place = []
        for c in range(2):
            pick = slot == row_ref[j, c : c + 1, :]
            picks.append(pick)
            ones.append(jnp.where(pick, 1.0, 0.0).astype(bf16))
            rank = col_ref[j, :, c : c + 1] + float(c * capacity)
            place.append(jnp.where(lane == rank, 1.0, 0.0))
        places.append(jnp.concatenate(place, axis=0))

    logits = jnp.zeros((2 * own_rows, router.shape[1]), f32)
    for n, (lo, size) in enumerate(columns):
        cols = slice(lo, lo + size)
        for copy in loads[n]:
            copy.wait()
        logits = logits + mm(tok[:, cols], router[cols, :])
        for j in range(span):
            for c in range(2):
                source = slice((c * span + j) * length, (c * span + j + 1) * length)
                target = slice((2 * j + c) * capacity, (2 * j + c + 1) * capacity)
                rows[target, cols] = mm(ones[2 * j + c], tok[source, cols]).astype(bf16)
                up_rows[target, cols] = mm(ones[2 * j + c], up[source, cols]).astype(bf16)

    expert = lax.broadcasted_iota(jnp.int32, (length, router.shape[1]), 1).astype(f32)
    mine = expert == half_ref[1].astype(f32)
    row = lax.broadcasted_iota(jnp.int32, (2 * capacity, 2 * capacity), 0)
    col = lax.broadcasted_iota(jnp.int32, (2 * capacity, 2 * capacity), 1)
    gates, sigmas = [], []
    for j in range(span):
        taken = []
        for c in range(2):
            part = logits[(c * span + j) * length : (c * span + j + 1) * length]
            first_id = 2 + c * top_count
            chosen = expert == col_ref[j, :, first_id : first_id + 1]
            for k in range(first_id + 1, first_id + top_count):
                chosen = chosen | (expert == col_ref[j, :, k : k + 1])
            peak = jnp.max(jnp.where(chosen, part, neg_large), axis=1, keepdims=True)
            weight = jnp.where(chosen, jnp.exp(part - peak), 0.0)
            weight = weight / jnp.sum(weight, axis=1, keepdims=True)
            taken.append(jnp.sum(jnp.where(mine, weight, 0.0), axis=1, keepdims=True))
            if c == 0:
                gate = expert == float(experts)
                gate = jnp.sum(jnp.where(gate, part, 0.0), axis=1, keepdims=True)
                sigmas.append(1.0 / (1.0 + jnp.exp(-gate)))
        slot_gates = jnp.sum(places[j] * jnp.concatenate(taken, axis=0), axis=0, keepdims=True)
        gates.append(jnp.sum(jnp.where(row == col, slot_gates, 0.0), axis=1, keepdims=True))
        places[j] = places[j].astype(bf16)
    gate_all = jnp.concatenate(gates, axis=0)
    sigma_all = jnp.concatenate(sigmas, axis=0)
    for lo, size in columns:
        cols = slice(lo, lo + size)
        slots[:, cols] = (gate_all * up_rows[:, cols].astype(f32)).astype(bf16)
        y_grad[:, cols] = (sigma_all * up[0:own_rows, cols].astype(f32)).astype(bf16)

    kept_copies = [keep(4, tok.at[0:own_rows]), keep(0, rows), keep(1, slots), keep(5, y_grad)]

    def gated(gate_part, up_part, grad):
        sig = 1.0 / (1.0 + jnp.exp(-gate_part))
        silu = gate_part * sig
        return (
            (silu * up_part).astype(bf16),
            (grad * up_part * (sig * (1.0 + gate_part * (1.0 - sig)))).astype(bf16),
            (grad * silu).astype(bf16),
        )

    weights[0].wait()
    for lo, size in tiles(shared_units, 256):
        at = slice(lo, lo + size)
        gate_part = nt(tok[0:own_rows, :], w_sh[0, at, :])
        up_part = nt(tok[0:own_rows, :], w_sh[1, at, :])
        grad = nt(y_grad[...], w_sh[2, at, :])
        s_hidden[:, at], s_gu[0, :, at], s_gu[1, :, at] = gated(gate_part, up_part, grad)
    kept_copies += [keep(6, s_hidden), keep(7, s_gu)]
    weights[1].wait()
    weights[2].wait()
    for lo, size in tiles(units, 256):
        at = slice(lo, lo + size)
        gate_part = nt(rows[...], w_in[0, at, :])
        up_part = nt(rows[...], w_in[1, at, :])
        grad = nt(slots[...], w_out[at, :])
        hidden[:, at], gu[0, :, at], gu[1, :, at] = gated(gate_part, up_part, grad)
    kept_copies += [keep(2, hidden), keep(3, gu)]

    slot_dots, sigma_dots = jnp.zeros((slab, 1), f32), jnp.zeros((own_rows, 1), f32)
    sent = []
    for n, (lo, size) in enumerate(columns):
        cols, turn = slice(lo, lo + size), n % 2
        if n >= 2:
            for copy in sent[n - 2]:
                copy.wait()
        made = mm(hidden[...], w_out[:, cols]).astype(bf16).astype(f32)
        slot_dots = slot_dots + jnp.sum(
            up_rows[:, cols].astype(f32) * made, axis=1, keepdims=True
        )
        made = (gate_all * made).astype(bf16)
        shared = mm(s_hidden[...], w_sh[2, :, cols])
        sigma_dots = sigma_dots + jnp.sum(
            up[0:own_rows, cols].astype(f32) * shared, axis=1, keepdims=True
        )
        shared = sigma_all * shared
        entry = (mm(gu[0], w_in[0, :, cols]) + mm(gu[1], w_in[1, :, cols])).astype(bf16)
        shared_back = mm(s_gu[0], w_sh[0, :, cols]) + mm(s_gu[1], w_sh[1, :, cols])
        sent.append([])
        for j in range(span):
            mine = slice(j * length, (j + 1) * length)
            theirs = slice(2 * j * capacity, 2 * (j + 1) * capacity)
            routed = mm(places[j], made[theirs])
            made_out[turn, 4 * j] = (routed[:length] + shared[mine]).astype(bf16)
            made_out[turn, 4 * j + 1] = routed[length:].astype(bf16)
            routed = mm(places[j], entry[theirs])
            made_out[turn, 4 * j + 2] = (routed[:length] + shared_back[mine]).astype(bf16)
            made_out[turn, 4 * j + 3] = routed[length:].astype(bf16)
            middle = length // 2
            for k in range(4):
                target, base = (owns[j], 0) if k % 2 == 0 else (give, 2 * j * length)
                base += (length, 0)[k // 2]
                for m, h in enumerate((half_ref[0], 1 - half_ref[0])):
                    source = made_out.at[
                        turn, 4 * j + k, pl.ds(pl.multiple_of(h * middle, 16), middle)
                    ]
                    at = base + m * middle
                    copy = pltpu.make_async_copy(
                        source, target.at[at : at + middle, cols], out_sem.at[turn, 4 * j + k, m]
                    )
                    copy.start()
                    sent[-1].append(copy)
    row = lax.broadcasted_iota(jnp.int32, (length, length), 0)
    col = lax.broadcasted_iota(jnp.int32, (length, length), 1)
    for j in range(span):
        for c in range(2):
            part = slot_dots[(2 * j + c) * capacity : (2 * j + c + 1) * capacity]
            part = jnp.where(picks[2 * j + c], part, 0.0)
            dots[j, c : c + 1, :] = jnp.sum(part, axis=0, keepdims=True)
        part = jnp.where(row == col, sigma_dots[j * length : (j + 1) * length], 0.0)
        dots[j, 2:3, :] = jnp.sum(part, axis=0, keepdims=True)
        dots[j, 3:, :] = jnp.zeros((dots.shape[1] - 3, length), f32)
    for copy in kept_copies + [copy for group in sent[-2:] for copy in group]:
        copy.wait()


def moe_call(index, span, sizes, chips, pieces, where, row_aux, col_aux, router, weights, kept):
    length, width, capacity, units, shared_units = sizes[:5]
    plan = [[place for _, place in group] for group in pieces]
    arrays = [piece for group in pieces for piece, _ in group]
    first = kept is None
    own_rows, slab = span * length, 2 * span * capacity
    slots, tokens = chips * 2 * capacity, chips * length
    kept_shapes = [
        jax.ShapeDtypeStruct(shape, bf16)
        for shape in (
            (slots, width),
            (slots, width),
            (slots, units),
            (2, slots, units),
            (tokens, width),
            (tokens, width),
            (tokens, shared_units),
            (2, tokens, shared_units),
        )
    ]
    own = jax.ShapeDtypeStruct((2 * length, width), bf16)
    give = jax.ShapeDtypeStruct((2 * own_rows, width), bf16)
    operands = [where, row_aux, col_aux, router, *arrays, *weights]
    operands += [] if first else list(kept)
    aliases = {} if first else {len(operands) - 8 + i: i for i in range(8)}
    flops = 2 * slab * width * units * 6 + 2 * own_rows * width * shared_units * 6
    out = pl.pallas_call(
        functools.partial(moe_kernel, index, span, first, plan, sizes),
        out_shape=kept_shapes
        + [own] * span
        + [give]
        + [jax.ShapeDtypeStruct((span, 8, length), f32)],
        in_specs=[in_smem] + [in_any] * 3
        + [in_any] * (len(arrays) + 3 + (0 if first else 8)),
        out_specs=[in_any] * (9 + span) + [in_vmem],
        scratch_shapes=[
            pltpu.VMEM((2 * own_rows, width), bf16),
            pltpu.VMEM((2 * own_rows, width), bf16),
            pltpu.VMEM((slab, width), bf16),
            pltpu.VMEM((slab, width), bf16),
            pltpu.VMEM((slab, width), bf16),
            pltpu.VMEM((slab, units), bf16),
            pltpu.VMEM((2, slab, units), bf16),
            pltpu.VMEM((own_rows, width), bf16),
            pltpu.VMEM((own_rows, shared_units), bf16),
            pltpu.VMEM((2, own_rows, shared_units), bf16),
            pltpu.VMEM((2, 4 * span, length, min(512, width)), bf16),
            pltpu.VMEM((2, units, width), bf16),
            pltpu.VMEM((units, width), bf16),
            pltpu.VMEM((3, shared_units, width), bf16),
            pltpu.VMEM((span, *row_aux.shape[1:]), f32),
            pltpu.VMEM((span, *col_aux.shape[1:]), f32),
            pltpu.VMEM(router.shape, bf16),
            pltpu.SemaphoreType.DMA((len(tiles(width, min(512, width))), len(arrays))),
            pltpu.SemaphoreType.DMA((6,)),
            pltpu.SemaphoreType.DMA((2, 4 * span, 2)),
            pltpu.SemaphoreType.DMA((8,)),
        ],
        input_output_aliases=aliases,
        compiler_params=params(),
        cost_estimate=pl.CostEstimate(
            flops=flops // 64, bytes_accessed=span * 512 * 1024, transcendentals=0
        ),
        name=f"experts_{index}",
    )(*operands)
    return out[:8], out[8 : 8 + span], out[8 + span], out[9 + span]


def spread_kernel(core_ref, own, other, out):
    parts, units, _ = out.shape
    count, _, rows = own.shape

    def spread(first, second):
        for i in range(count):
            for c in range(parts):
                at = slice(c * units, (c + 1) * units)
                both = jnp.concatenate([first[i, at, :], second[i, at, :]], axis=1)
                out[c, :, 2 * i * rows : 2 * (i + 1) * rows] = both

    @pl.when(core_ref[0] == 0)
    def _():
        spread(own, other)

    @pl.when(core_ref[0] == 1)
    def _():
        spread(other, own)


def shared_grad_kernel(tok, y_grad, hidden, gu, out):
    units = hidden.shape[1]
    rows = out.shape[3]
    for c in range(3):
        left = gu[c] if c < 2 else hidden[...]
        right = tok[...] if c < 2 else y_grad[...]
        part = mm(left, right, 0, 0).astype(bf16)
        for k in range(2):
            out[k, 0, c * units : (c + 1) * units, :] = part[:, k * rows : (k + 1) * rows]


class Ring:
    def __init__(self, devices):
        self.devices = devices
        self.chips = devices // 2
        order = chip_ring(self.chips)
        n = self.chips
        self.next = [
            (order[i] * 2 + c, order[(i + 1) % n] * 2 + c) for i in range(n) for c in range(2)
        ]
        self.prev = [(b, a) for a, b in self.next]
        self.core = [(e, e ^ 1) for e in range(devices)]
        half = n // 2
        offsets = [0]
        for k in range(1, half):
            offsets += [-k, k]
        self.offsets = offsets + [half]
        place = {chip: i for i, chip in enumerate(order)}
        self.chip_table = np.array(
            [
                [order[(place[e // 2] + o) % n] for o in self.offsets]
                for e in range(devices)
            ],
            np.int32,
        )
        self.seq_table = np.stack(
            [
                2 * self.chip_table + (np.arange(devices) % 2)[:, None],
                2 * self.chip_table + 1 - (np.arange(devices) % 2)[:, None],
            ],
            axis=-1,
        ).reshape(devices, devices)
        self.seq_inverse = np.argsort(self.seq_table, axis=1).astype(np.int32)

    def step(self, ahead, back=None, last=False):
        back = ahead if back is None else back
        if last:
            cut = ahead.shape[0] // 2
            ahead, back = ahead[:cut], back[cut:]
        return self.send_pair(ahead, back)

    def send_pair(self, ahead, back):
        return [
            lax.ppermute(ahead, "expert", self.next),
            lax.ppermute(back, "expert", self.prev),
        ]

    def add_up(self, terms):
        out = None
        for term in terms:
            out = term.astype(f32) if out is None else out + term.astype(f32)
        return out

    def reduce_first(self, terms):
        total = self.add_up(terms).astype(bf16)
        return self.step(total, last=True)

    def reduce_terms(self, ahead_terms, back_terms, sending, first):
        mine, yours = self.add_up(ahead_terms), self.add_up(back_terms)
        ahead, back = (part.astype(f32) for part in sending)
        if first:
            cut = ahead.shape[0]
            mine = jnp.concatenate([mine[:cut] + ahead, mine[cut:]], axis=0)
            yours = jnp.concatenate([yours[:cut], yours[cut:] + back], axis=0)
        else:
            mine, yours = mine + ahead, yours + back
        return [mine.astype(bf16), yours.astype(bf16)]

    def reduce(self, terms):
        half = self.chips // 2
        sending = self.reduce_first(terms[half])
        for k in range(half - 1, 0, -1):
            send = self.reduce_terms(terms[k], terms[-k], sending, k == half - 1)
            sending = self.send_pair(*send)
        return self.add_up([*terms[0], *sending])

    def swap_core(self, block):
        return lax.ppermute(block, "expert", self.core)

    def double_small(self, held, me, step):
        pairs = [(e, e ^ step) for e in range(self.devices)]
        other = lax.ppermute(held, "expert", pairs)
        upper = (me // step) % 2 == 1
        return jnp.where(upper, jnp.concatenate([other, held]), jnp.concatenate([held, other]))


def after(value, *others):
    return lax.optimization_barrier((value,) + others)[0]


def after_all(values, *others):
    return lax.optimization_barrier((list(values),) + others)[0]


def hold(*values):
    return list(lax.optimization_barrier(values))


def swap_tensor(block):
    return lax.ppermute(block, "tensor", [(0, 1), (1, 0)])


def sum_tensor(part):
    own = part.astype(bf16)
    return own.astype(f32) + swap_tensor(own).astype(f32)


def make_local(ring):
    devices, chips = ring.devices, ring.chips

    def local(
        tokens_in,
        cotangent,
        norm_gains,
        qkv_weight,
        qkv_bias,
        out_weight,
        router_weight,
        shared_gate,
        shared_in,
        shared_out,
        expert_in,
        expert_out,
        expert_ids,
        prefix_len,
    ):
        me = lax.axis_index("expert")
        core = me % 2
        half = lax.axis_index("tensor")
        length, width = tokens_in.shape
        top_count = expert_ids.shape[1]
        experts = router_weight.shape[1]
        capacity = length * top_count * 3 // (2 * experts)
        rows_dev = qkv_weight.shape[0]
        heads_t = qkv_bias.shape[1]
        heads = heads_t // 2
        hd_dev = qkv_bias.shape[2]
        head_size = hd_dev * devices
        half_cols = heads * head_size
        score_scale = head_size ** (-0.5)
        chip_of = jnp.asarray(ring.chip_table)[me]
        seq_of = jnp.asarray(ring.seq_table)[me]
        seq_inv = jnp.asarray(ring.seq_inverse)[me]

        pieces = [
            norm_gains.reshape(-1),
            qkv_bias.reshape(-1),
            router_weight.reshape(-1),
            shared_gate.reshape(-1),
            expert_ids.T.astype(bf16).reshape(-1),
            prefix_len.astype(bf16).reshape(-1),
        ]
        sizes = [p.shape[0] for p in pieces]
        total = sum(sizes)
        padded = -(-total // 1024) * 1024
        small = jnp.concatenate(pieces + [jnp.zeros((padded - total,), bf16)])
        swap_core = ring.swap_core

        def cost(flops, moved):
            return pl.CostEstimate(
                flops=flops // 64, bytes_accessed=moved // 64, transcendentals=0
            )

        depth = 2 * rows_dev

        def by_core(own, other, axis):
            return jnp.where(
                core == 0,
                jnp.concatenate([own, other], axis=axis),
                jnp.concatenate([other, own], axis=axis),
            )

        def halves(array, axis):
            size = array.shape[axis] // 2
            own = lax.dynamic_slice_in_dim(array, core * size, size, axis)
            return own, lax.dynamic_slice_in_dim(array, (1 - core) * size, size, axis)

        qkv_own, qkv_other = halves(qkv_weight.transpose(1, 0, 2), 2)
        out_own, out_other = halves(out_weight, 0)
        own = jnp.concatenate([qkv_own, out_own.T[None]], axis=0)
        other = jnp.concatenate([qkv_other, out_other.T[None]], axis=0)
        block = by_core(own, ring.swap_core(other), 1).reshape(4 * depth, half_cols)
        half_length = length // 2
        steps = chips // 2
        up_zero = lax.dynamic_slice_in_dim(cotangent, half * half_length, half_length, 0)
        small_all = small[None]
        for k in range(devices.bit_length() - 1):
            small_all = ring.double_small(small_all, me, 1 << k)
        pair = ring.step(block)
        attn_w = [block]
        for k in range(1, steps + 1):
            if k > 1:
                pair = ring.step(*pair, last=k == steps)
            attn_w += pair

        cuts = np.cumsum([0] + sizes)
        found = [small_all[:, cuts[i] : cuts[i + 1]] for i in range(len(sizes))]
        gains_f = (
            found[0].reshape(devices, 2, rows_dev).transpose(1, 0, 2).reshape(2, width).astype(f32)
        )
        bias_all = (
            found[1].reshape(devices, 3, heads_t, hd_dev).transpose(1, 2, 0, 3)
            .reshape(3, 2, half_cols)
        )
        bias = lax.dynamic_index_in_dim(bias_all, core, 1, keepdims=False).astype(f32)
        router_w = found[2].reshape(width, experts)
        gate_vec = found[3].reshape(width)
        ids_all = found[4].reshape(devices, top_count, length).astype(jnp.int32)
        prefix_all = found[5].reshape(devices).astype(jnp.int32)
        prefix_pair = jnp.stack([prefix_all[me], prefix_all[me ^ 1]])


        match = jnp.any(ids_all[seq_of] == me, axis=1)
        triangle = jnp.asarray(np.triu(np.ones((length, length), np.float32)), bf16)
        rank = jnp.where(match, mm(match.astype(bf16), triangle) - 1.0, no_slot)
        rank = rank.reshape(chips, 2, length)
        row_aux = jnp.concatenate([rank, jnp.zeros((chips, 6, length), f32)], axis=1)
        ids_ring = ids_all[seq_of].reshape(chips, 2 * top_count, length).astype(f32)
        blank = jnp.zeros((chips, -(2 + 2 * top_count) % 8, length), f32)
        col_aux = jnp.concatenate([rank, ids_ring, blank], axis=1).transpose(0, 2, 1)
        router_all = jnp.concatenate(
            [
                router_w,
                gate_vec[:, None],
                jnp.zeros((width, -(experts + 1) % 128), bf16),
            ],
            axis=1,
        )

        units = shared_out.shape[0]
        unit_chip = units // chips
        sh_send = jnp.concatenate(
            [
                shared_in.transpose(1, 2, 0).reshape(2, chips, unit_chip, rows_dev),
                shared_out.reshape(1, chips, unit_chip, rows_dev),
            ],
            axis=0,
        ).transpose(1, 0, 2, 3)
        sh_send = sh_send.reshape(chips, 3 * unit_chip, rows_dev)

        up_cross = {0: swap_tensor(up_zero)}
        attn_w[-4:-2], sh_send, up_cross[0] = hold(attn_w[-4:-2], sh_send, up_cross[0])
        up_next = ring.step(after(up_zero, *attn_w[-2:]))
        same_core = [[2 * i + c for i in range(chips)] for c in range(2)]
        inputs = tokens_in.astype(f32)
        first_b = rms_norm(inputs, gains_f[0]).astype(bf16)
        first_o = ring.swap_core(first_b)
        cosine, sine = rotary_tables(length, head_size)
        pair_cols = jax.ShapeDtypeStruct((2 * length, half_cols), bf16)
        chip_arg = chip_of.astype(jnp.int32)

        query, key, value, mixed = pl.pallas_call(
            functools.partial(attend_kernel, chips + 1, heads, score_scale),
            out_shape=[pair_cols] * 4,
            in_specs=[in_smem] * 2 + [in_vmem] * 5 + [in_any] * (chips + 1),
            out_specs=[in_vmem] * 4,
            scratch_shapes=[
                pltpu.VMEM((3, width, half_cols), bf16),
                pltpu.SemaphoreType.DMA((3 * chips,)),
            ],
            compiler_params=params(),
            cost_estimate=cost(2 * 2 * length * width * 3 * half_cols, 12 * 1024 * 1024),
            name="attend",
        )(chip_arg, prefix_pair, first_b, first_o, bias.reshape(1, -1), cosine, sine, *attn_w)
        sh_mine = lax.all_to_all(
            after(sh_send, *attn_w[-2:]),
            "expert",
            split_axis=0,
            concat_axis=0,
            tiled=True,
            axis_index_groups=same_core,
        )
        attn_own, attn_give = pl.pallas_call(
            functools.partial(project_kernel, chips + 1),
            out_shape=[
                jax.ShapeDtypeStruct((length, width), f32),
                jax.ShapeDtypeStruct((length, width), bf16),
            ],
            in_specs=[in_smem, in_vmem] + [in_any] * (chips + 1),
            out_specs=[in_vmem] * 2,
            scratch_shapes=[
                pltpu.VMEM((1, width, half_cols), bf16),
                pltpu.SemaphoreType.DMA((chips,)),
            ],
            compiler_params=params(),
            cost_estimate=cost(2 * 2 * length * width * half_cols, 6 * 1024 * 1024),
            name="project",
        )(chip_arg, mixed, *attn_w)
        attn_own = (attn_own + ring.swap_core(attn_give).astype(f32)).astype(bf16)
        attn_got = swap_tensor(attn_own)
        attn_got, sh_mine, up_next = hold(attn_got, sh_mine, up_next)
        attn_out = attn_own.astype(f32) + attn_got.astype(f32)
        residual = inputs + attn_out
        second_b = rms_norm(residual, gains_f[1]).astype(bf16)

        second_b, up_next, sh_mine, row_aux, col_aux, router_all = hold(
            second_b, up_next, sh_mine, row_aux, col_aux, router_all
        )
        pair = {
            0: [
                jnp.concatenate([second_b, up_next[0]], axis=0),
                jnp.concatenate([up_next[1], second_b], axis=0),
            ]
        }
        pair_o = {0: [swap_core(pair[0][0]), swap_core(up_next[1])]}
        up_zero_o = swap_core(up_zero)
        cross_o = {}

        logits = mm(second_b, router_w)
        expert_range = jnp.arange(experts, dtype=jnp.int32)
        route_match = expert_ids[:, :, None] == expert_range[None, None, :]
        chosen = jnp.sum(jnp.where(route_match, logits[:, None, :], 0.0), axis=-1)
        gate_weights = jax.nn.softmax(chosen, axis=-1)
        shared_sigma = jax.nn.sigmoid(
            jnp.sum(second_b.astype(f32) * gate_vec.astype(f32)[None], axis=-1)
        )
        gate_dense = jnp.sum(jnp.where(route_match, gate_weights[:, :, None], 0.0), axis=1)
        ex_in = expert_in[0].transpose(1, 2, 0)
        ex_out = expert_out[0]
        part_units = ex_out.shape[0]
        sizes = (length, width, capacity, part_units, unit_chip, experts, top_count)
        half_arg = jnp.stack([half, me]).astype(jnp.int32)
        core_arg = core.astype(jnp.int32).reshape(1)

        sh_w = pl.pallas_call(
            spread_kernel,
            out_shape=jax.ShapeDtypeStruct((3, unit_chip, width), bf16),
            in_specs=[in_smem, in_vmem, in_vmem],
            out_specs=in_vmem,
            compiler_params=params(),
            cost_estimate=cost(0, 16 * 1024 * 1024),
            name="spread",
        )(core_arg, sh_mine, swap_core(sh_mine))

        def row_pieces(found, own_zero, g):
            full, part = length, length // 2
            if g == 0:
                return [[(own_zero, (0, full, 0, 0))]]
            if g == steps:
                ahead, back = found[g]
                return [[(ahead, (0, part, 0, 0)), (back, (0, part, part, part))]]
            return [[(found[g][0], (0, full, 0, 0))], [(found[g][1], (half_length, full, 0, 0))]]

        def up_pieces(found, own_zero, crossed, g):
            whole, part = half_length, half_length // 2
            if g == 0:
                straight = [[(own_zero, (0, whole, 0, whole))]]
            elif g == steps:
                ahead, back = found[g - 1]
                straight = [
                    [
                        (ahead, (length, part, 0, whole)),
                        (back, (part, part, part, whole + part)),
                    ]
                ]
            else:
                ahead, back = found[g - 1]
                straight = [
                    [(ahead, (length, whole, 0, whole))],
                    [(back, (0, whole, 0, whole))],
                ]
            for j, chip in enumerate(straight):
                chip.append((crossed, (j * whole, whole, whole, 0)))
            return straight

        kept = None
        own_terms, give_terms, dot_rows = {}, {}, []
        terms, crossed = {}, {}

        def receive(g):
            index, count = (0, 1) if g == 0 else (2 * g - 1, 1 if g == steps else 2)
            crossing = []
            for j in range(count):
                own, got, at = own_terms[g][j], give_got[g], 2 * j * length
                parts = []
                for i in range(4):
                    lo, hi = i * half_length, (i + 1) * half_length
                    parts.append([own[lo:hi], got[at + lo : at + hi]])
                terms[ring.offsets[index + j]] = [parts[0], parts[2]]
                crossing.append(ring.add_up(parts[1]).astype(bf16))
                out_gives.setdefault(g, []).append(parts[3])
            return crossing[0] if count == 1 else jnp.concatenate(crossing, axis=0)

        def receive_outs(g):
            parts = [ring.add_up(part).astype(bf16) for part in out_gives[g]]
            return parts[0] if len(parts) == 1 else jnp.concatenate(parts, axis=0)

        def place_crossed(which, g, got):
            index, count = (0, 1) if g == 0 else (2 * g - 1, 1 if g == steps else 2)
            for j in range(count):
                crossed[which, ring.offsets[index + j]] = got[
                    j * half_length : (j + 1) * half_length
                ]

        out_gives, give_got = {}, {}
        for k in range(1, steps + 2):
            g = k - 1
            now = []
            if k <= steps:
                ahead, back = pair[g]
                cut = half_length // 2
                if k == steps:
                    ahead, back = ahead[: length // 2], back[half_length + length // 2 :]
                pair[k] = ring.send_pair(ahead, back)
                first, second = pair[g][0][length:], pair[g][1][:half_length]
                if k == steps:
                    first, second = first[:cut], second[cut:]
                up_cross[k] = swap_tensor(jnp.concatenate([first, second], axis=0))
                now = [pair[k], up_cross[k]]
            if g > 0:
                pair_o[g] = [swap_core(x) for x in pair[g]]
            if g > 0:
                cross_o[g] = swap_core(after(up_cross[g], *pair_o[g]))
            else:
                cross_o[g] = swap_core(up_cross[g])
            if g >= 1:
                give_got[g - 1] = swap_core(after(give_terms[g - 1], cross_o[g]))
                now.append(give_got[g - 1])
            if g >= 3:
                grads = receive(g - 2)
                grads, pair_o[g] = hold(grads, pair_o[g])
                now.append(swap_tensor(grads))
            pieces = (
                row_pieces(pair, second_b, g)
                + row_pieces(pair_o, pair_o[0][0], g)
                + up_pieces(pair, up_zero, up_cross[g], g)
                + up_pieces(pair_o, up_zero_o, cross_o[g], g)
            )
            span = 1 if g in (0, steps) else 2
            kept, own_terms[g], give_terms[g], rows = moe_call(
                0 if g == 0 else 2 * g - 1,
                span,
                sizes,
                chips,
                pieces,
                half_arg,
                row_aux,
                col_aux,
                router_all,
                (ex_in, ex_out, sh_w),
                kept,
            )
            dot_rows.append(rows)
            *now, dot_rows[-1], give_terms[g] = hold(*now, rows, give_terms[g])
            if k <= steps:
                pair[k], up_cross[k], *now = now
            if g >= 1:
                give_got[g - 1] = now[0]
            if g >= 3:
                place_crossed(0, g - 2, now[1])

        rows_all, slots_all, hidden_all, gu_all, tok_all, y_all, s_hidden_all, s_gu_all = kept
        give_got[steps] = swap_core(give_terms[steps])
        near_far = receive(steps - 1)
        grads = receive(steps)
        s_hidden_all, grads = hold(s_hidden_all, grads)
        far = ring.offsets[-1]
        grads = swap_tensor(grads)
        sh_grad = pl.pallas_call(
            shared_grad_kernel,
            grid=(chips,),
            out_shape=jax.ShapeDtypeStruct((2, chips, 3 * unit_chip, rows_dev), bf16),
            in_specs=[
                pl.BlockSpec((chips * length, depth), lambda n: (0, n)),
                pl.BlockSpec((chips * length, depth), lambda n: (0, n)),
                pl.BlockSpec((chips * length, unit_chip), lambda n: (0, 0)),
                pl.BlockSpec((2, chips * length, unit_chip), lambda n: (0, 0, 0)),
            ],
            out_specs=pl.BlockSpec((2, 1, 3 * unit_chip, rows_dev), lambda n: (0, n, 0, 0)),
            compiler_params=params(),
            cost_estimate=cost(2 * chips * length * width * 3 * unit_chip, 26 * 1024 * 1024),
            name="shared_grad",
        )(tok_all, y_all, s_hidden_all, s_gu_all)
        near_got = swap_tensor(near_far)
        grads, sh_grad = hold(grads, sh_grad)
        place_crossed(0, steps, grads)

        def ring_terms(which, o):
            return [*terms[o][which], crossed[which, o]]

        zero_got = swap_tensor(after(receive(0), grads))
        sending = ring.reduce_first(ring_terms(0, far))
        own, other = halves(sh_grad, 0)
        sh_got = swap_core(other)
        gu_all = after(gu_all, grads)
        sh_sum = (own.astype(f32) + sh_got.astype(f32)).astype(bf16)[0]
        expert_in_grad = mm(gu_all, rows_all, 1, 0).transpose(2, 0, 1)[None]
        near_got, zero_got, sending, sh_sum, expert_in_grad = hold(
            near_got, zero_got, sending, sh_sum, expert_in_grad
        )
        place_crossed(0, 0, zero_got)
        place_crossed(0, steps - 1, near_got)
        out_sent = {}
        for k in range(steps - 1, 0, -1):
            send = ring.reduce_terms(
                ring_terms(0, k), ring_terms(0, -k), sending, k == steps - 1
            )
            now = []
            if k == steps - 1:
                send, far_outs = hold(send, receive_outs(steps))
                out_sent[steps] = swap_tensor(far_outs)
                dots = jnp.concatenate(after_all(dot_rows, send[0]), axis=0)
                sdots = jnp.concatenate([dots[:, 2:3], jnp.zeros_like(dots[:, 2:3])], axis=1)
                dot_send = jnp.stack([dots[:, :2], sdots], axis=2)
                dot_send = dot_send.reshape(devices, 2, length)[seq_inv]
                dot_got = lax.all_to_all(
                    dot_send, "expert", split_axis=0, concat_axis=0, tiled=True
                )
                dot_got = jnp.concatenate(
                    [dot_got[:, 0], jnp.sum(dot_got[:, 1], axis=0)[None]], axis=0
                )
                now = [out_sent[steps], dot_got]
            sending = ring.send_pair(*send)
            sending, *now = hold(sending, *now)
            if k == steps - 1:
                out_sent[steps], dot_got = now
        place_crossed(1, steps, out_sent[steps])
        dot_got = dot_got + swap_tensor(dot_got)
        second_half = ring.add_up([*ring_terms(0, 0), *sending]).astype(bf16)
        sh_back = lax.all_to_all(
            after(sh_sum, second_half),
            "expert",
            split_axis=0,
            concat_axis=0,
            tiled=True,
            axis_index_groups=same_core,
        )
        second_got = swap_tensor(second_half)
        out_sending = ring.reduce_first(ring_terms(1, far))
        second_got, out_sending = hold(second_got, out_sending)

        def both_halves(own, other):
            return jnp.where(
                half == 0,
                jnp.concatenate([own, other], axis=0),
                jnp.concatenate([other, own], axis=0),
            )

        second_part = both_halves(second_half, second_got)

        gate_grad_dense, sigma_grad = dot_got[:experts].T, dot_got[experts]
        row_term = jnp.sum(gate_dense * gate_grad_dense, axis=-1, keepdims=True)
        logit_grad = (gate_dense * (gate_grad_dense - row_term)).astype(bf16)
        gate_logit_grad = sigma_grad * shared_sigma * (1.0 - shared_sigma)

        second_grad = second_part.astype(f32)
        second_grad = second_grad + mm(logit_grad, router_w, 1, 1)
        second_grad = second_grad + gate_logit_grad[:, None] * gate_vec.astype(f32)[None]
        upstream = cotangent.astype(f32)
        residual_norm_grad, gain_two_grad = jax.vjp(rms_norm, residual, gains_f[1])[1](second_grad)
        residual_grad = upstream + residual_norm_grad
        attn_grad = residual_grad.astype(bf16)
        attn_grad_o = ring.swap_core(attn_grad)

        def by_chip(left, right, wanted=tuple(ring.offsets)):
            return {
                offset: [
                    mm(lax.dynamic_slice_in_dim(left, chip_of[i] * depth, depth, 1), right, 0, 0)
                ]
                for i, offset in enumerate(ring.offsets)
                if offset in wanted
            }

        proj_grad, bias_grad = pl.pallas_call(
            functools.partial(attend_back_kernel, chips + 1, heads, score_scale),
            out_shape=[
                jax.ShapeDtypeStruct((2 * length, 3 * half_cols), bf16),
                jax.ShapeDtypeStruct((1, 3 * half_cols), f32),
            ],
            in_specs=[in_smem] * 2 + [in_vmem] * 7 + [in_any] * (chips + 1),
            out_specs=[in_vmem] * 2,
            scratch_shapes=[
                pltpu.VMEM((1, width, half_cols), bf16),
                pltpu.SemaphoreType.DMA((chips,)),
            ],
            compiler_params=params(),
            cost_estimate=cost(2 * 2 * length * width * half_cols * 2, 8 * 1024 * 1024),
            name="attend_back",
        )(
            chip_arg,
            prefix_pair,
            attn_grad,
            attn_grad_o,
            query,
            key,
            value,
            cosine,
            sine,
            *attn_w,
        )
        crossing = swap_tensor(receive_outs(steps - 1))
        first_pair = jnp.concatenate([first_b, first_o], axis=0)
        attn_grad_pair = jnp.concatenate([attn_grad, attn_grad_o], axis=0)
        out_parts = by_chip(attn_grad_pair, mixed)
        far_out = out_parts[steps][0].astype(bf16)
        far_out, proj_grad, sh_back = hold(far_out, proj_grad, sh_back)
        far_part = by_chip(first_pair, proj_grad, [steps])[steps][0].astype(bf16)
        far_part = jnp.concatenate([far_part, far_out], axis=1)
        cut = depth // 2
        proj_grad, ahead, back = hold(proj_grad, far_part[:cut], far_part[cut:])
        going = ring.send_pair(ahead, back)
        qkv_parts = by_chip(first_pair, proj_grad, ring.offsets[:-1])
        attn_parts = {
            o: [
                jnp.concatenate(
                    [qkv_parts[o][0].astype(bf16), out_parts[o][0].astype(bf16)], axis=1
                )
            ]
            for o in qkv_parts
        }
        bias_grad = bias_grad[0]
        def send_outs(k, going):
            return ring.send_pair(
                *ring.reduce_terms(ring_terms(1, k), ring_terms(1, -k), going, k == steps - 1)
            )

        second_f = second_b.astype(f32)
        router_part = mm(second_b, logit_grad, 0, 0)
        shared_gate_part = jnp.sum(gate_logit_grad[:, None] * second_f, axis=0)
        early = jnp.concatenate(
            [router_part, shared_gate_part[:, None], gain_two_grad[:, None]], axis=1
        ).reshape(devices, rows_dev * (experts + 2))

        def send_next(k, going):
            return ring.send_pair(
                *ring.reduce_terms(attn_parts[k], attn_parts[-k], going, k == steps - 1)
            )

        pieces = [attn_parts[o][0] for o in ring.offsets[:-1]]
        going, crossing, proj_grad, pieces = hold(going, crossing, proj_grad, pieces)
        for o, piece in zip(ring.offsets[:-1], pieces, strict=True):
            attn_parts[o] = [piece]
        place_crossed(1, steps - 1, crossing)
        send = ring.reduce_terms(
            attn_parts[steps - 1], attn_parts[1 - steps], going, steps > 1
        )
        proj_grad, hidden_all, *send = hold(proj_grad, hidden_all, *send)
        expert_out_grad = mm(hidden_all, slots_all, 0, 0)[None]
        first_own, first_give = pl.pallas_call(
            functools.partial(project_back_kernel, chips + 1),
            out_shape=[
                jax.ShapeDtypeStruct((length, width), f32),
                jax.ShapeDtypeStruct((length, width), bf16),
            ],
            in_specs=[in_smem, in_vmem] + [in_any] * (chips + 1),
            out_specs=[in_vmem] * 2,
            scratch_shapes=[
                pltpu.VMEM((3, width, half_cols), bf16),
                pltpu.SemaphoreType.DMA((3 * chips,)),
            ],
            compiler_params=params(),
            cost_estimate=cost(2 * 2 * length * width * 3 * half_cols, 12 * 1024 * 1024),
            name="project_back",
        )(chip_arg, proj_grad, *attn_w)
        first_own = (first_own + swap_core(first_give).astype(f32)).astype(bf16)
        for k in range(steps - 1, -1, -1):
            if k > 0:
                going = ring.send_pair(*send) if k == steps - 1 else send_next(k, going)
                out_sending = send_outs(k, out_sending)
            now = []
            if k > 0:
                now.append(swap_tensor(receive_outs(k - 1)))
            if k == steps - 2:
                now.append(swap_tensor(first_own))
            if k == 0:
                res_half = lax.dynamic_slice_in_dim(residual, half * half_length, half_length, 0)
                out_half = ring.add_up([res_half, *ring_terms(1, 0), *out_sending]).astype(bf16)
                output = both_halves(out_half, swap_tensor(out_half))
                break
            if k == 2:
                now.append(sh_back)
            if k == steps - 1:
                now.append(expert_out_grad)
            going, out_sending, *now = hold(going, out_sending, *now)
            place_crossed(1, k - 1, now[0])
            if k == steps - 1:
                expert_out_grad = now[-1]
            if k == 2:
                sh_back = now[-1]
            if k == steps - 2:
                first_got = now[1]
        attn_grads = ring.add_up([*attn_parts[0], *going])
        first_grad = first_own.astype(f32) + first_got.astype(f32)
        input_norm_grad, gain_one_grad = jax.vjp(rms_norm, inputs, gains_f[0])[1](first_grad)
        input_grad = (residual_grad + input_norm_grad).astype(bf16)

        own, other = halves(attn_grads.astype(bf16), 0)
        both = by_core(
            own.reshape(rows_dev, 4, half_cols),
            swap_core(other).reshape(rows_dev, 4, half_cols),
            2,
        ).astype(f32)
        qkv_weight_grad = both[:, :3]
        out_weight_grad = both[:, 3].T

        sh_back = sh_back.reshape(chips, 3, unit_chip, rows_dev).astype(f32)
        shared_in_grad = sh_back[:, :2].transpose(3, 1, 0, 2).reshape(rows_dev, 2, units)
        shared_out_grad = sh_back[:, 2].reshape(units, rows_dev)

        bias_send = bias_grad.reshape(3 * heads, devices, hd_dev).transpose(1, 0, 2)
        late = jnp.concatenate(
            [gain_one_grad.reshape(devices, rows_dev), bias_send.reshape(devices, -1), early],
            axis=1,
        )
        late = lax.all_to_all(late, "expert", split_axis=0, concat_axis=0, tiled=True)
        gain_one = jnp.sum(late[:, :rows_dev], axis=0)
        count = 3 * heads * hd_dev
        early = late[:, rows_dev + count :]
        early = jnp.sum(early, axis=0).reshape(rows_dev, experts + 2)
        router_grad, shared_gate_grad = early[:, :experts], early[:, experts]
        bias_got = late[:, rows_dev : rows_dev + count].reshape(chips, 2, 3, heads, hd_dev)
        bias_got = jnp.sum(bias_got, axis=0)
        qkv_bias_grad = bias_got.transpose(1, 0, 2, 3).reshape(3, heads_t, hd_dev)
        gains_grad = jnp.stack([gain_one, early[:, experts + 1]], axis=0)

        return (
            output,
            input_grad,
            gains_grad,
            qkv_weight_grad,
            qkv_bias_grad,
            out_weight_grad,
            router_grad,
            shared_gate_grad,
            shared_in_grad,
            shared_out_grad,
            expert_in_grad,
            expert_out_grad,
        )

    return local


def solution(mesh):
    ring = Ring(mesh.shape["expert"])
    return jax.shard_map(
        make_local(ring),
        mesh=mesh,
        in_specs=(
            P("expert", None),
            P("expert", None),
            P(None, "expert"),
            P("expert", None, "tensor"),
            P(None, "tensor", "expert"),
            P("tensor", "expert"),
            P("expert", None),
            P("expert"),
            P("expert", None, "tensor"),
            P("tensor", "expert"),
            P("expert", None, None, "tensor"),
            P("expert", "tensor", None),
            P("expert", None),
            P("expert"),
        ),
        out_specs=(
            P("expert", None),
            P("expert", None),
            P(None, "expert"),
            P("expert", None, "tensor"),
            P(None, "tensor", "expert"),
            P("tensor", "expert"),
            P("expert", None),
            P("expert"),
            P("expert", None, "tensor"),
            P("tensor", "expert"),
            P("expert", None, None, "tensor"),
            P("expert", "tensor", None),
        ),
        check_vma=False,
    )
```
